32 devices in a mesh: sky: 2 (over x), tm: 16 (over z, y, core).
Axes of the slice: x: 2, y: 2, z: 4, core: 2. Of those that a mesh axis runs over, the one named last changes fastest.
Arguments:
- series: bfloat16 [4, 4, 1024, 2048], P('sky', None, 'tm'), parts along dimension 0, may hold values from -6 to 6
- antenna: float32 [4, 3], P('sky'), parts along dimension 0, as said below
- offsets: int32 [16, 2], P('sky'), parts along dimension 0, may hold values from -8 to 8, as said below
Outputs:
- detection: float32 [16, 1024, 2048], P('sky', 'tm'), parts along dimension 0
The draws below stay inside these ranges and needn't reach their ends.
There are 2 independent parts, one for each index of `sky`. The reference program is written for one: setup_inputs(seed, part) draws one part's arguments, and reference() takes and returns one part's arrays. A program takes and returns all parts, laid end to end along the dimension named above; each array names one. Nothing has to cross between parts.
Inputs may be any that keep to these rules, and one draw needn't show every extreme that they name: `offsets`: both -8 and 8 occur in every draw. `antenna`: A and B are positive and C C is at most 0.49 A B in every row.
All inputs are finite; a program needn't handle non-finite values.
Results may differ from the reference program's by a relative error of at most 0.0032.
Values may be sent and summed in bfloat16 or wider, within the bound.
No kernel may reach another device: no remote copies, remote signals or barrier semaphores. Data moves between devices by JAX's collectives and lax.ppermute only.
A program may use at most 128 MiB of HBM per device.

```python
import math
import jax
import jax.numpy as jnp
from jax import lax

NA = 2048
NB = 1024
LEN = 2097152
SEG = 2
TEMPL = 8
DMAX = 8


def draw_antenna(key, part):
    key_a, key_b, key_c = jax.random.split(key, 3)
    coef_a = jnp.exp(jax.random.uniform(key_a, (SEG,), jnp.float32, math.log(0.5), math.log(2.0)))
    coef_b = jnp.exp(jax.random.uniform(key_b, (SEG,), jnp.float32, math.log(0.5), math.log(2.0)))
    mixing = jax.random.uniform(key_c, (SEG,), jnp.float32, -1.0, 1.0)
    coef_c = 0.7 * mixing * jnp.sqrt(coef_a * coef_b)
    return jnp.stack([coef_a, coef_b, coef_c], axis=1).astype(jnp.float32)


def draw_offsets(key, part):
    drawn = jax.random.randint(key, (TEMPL, SEG), -DMAX, DMAX + 1, dtype=jnp.int32)
    drawn = drawn.at[0, 0].set(DMAX)
    drawn = drawn.at[1, 0].set(-DMAX)
    return drawn.astype(jnp.int32)


def block_scale(stream_key, shape, cuts, smallest, top_value):
    gain = 1.0
    for axis_at, blocks in cuts:
        draws = jax.random.uniform(jax.random.fold_in(jax.random.fold_in(stream_key, 6), axis_at), (blocks,), jnp.float32, smallest / len(cuts), top_value / len(cuts))
        gain = gain * jnp.repeat(jnp.exp(draws), shape[axis_at] // blocks).reshape((-1,) + (1,) * (len(shape) - 1 - axis_at))
    return gain


def bell_draw(key, shape, width, most, cuts=(), kind=jnp.bfloat16):
    gain = block_scale(key, shape, cuts, -0.22, 0.18) if cuts else 1.0
    values = jax.random.normal(key, shape, jnp.float32) * width * gain
    return jnp.minimum(jnp.maximum(values, -most), most).astype(kind)


def setup_inputs(seed: int = 0, part: int = 0) -> dict:
    seeds = jax.random.split(jax.random.key(seed), 4)
    part_splits = jax.random.split(jax.random.fold_in(seeds[3], part), 4)
    return {
        "series": bell_draw(part_splits[0], (SEG, 4, NB, NA), 1.0, 6.0, ((2, 16),)),
        "antenna": draw_antenna(jax.random.fold_in(jax.random.fold_in(seeds[3], part), 71), part),
        "offsets": draw_offsets(jax.random.fold_in(jax.random.fold_in(seeds[3], part), 71), part),
    }


def dft_table(length):
    indices = jnp.arange(length, dtype=jnp.int32)
    products = (indices[:, None] * indices[None, :]) % length
    phase_angle = products.astype(jnp.float32) * (2.0 * math.pi / length)
    return jnp.cos(phase_angle).astype(jnp.bfloat16), (-jnp.sin(phase_angle)).astype(jnp.bfloat16)


def complex_dft(x_real, x_imag, w_real, w_imag, formula):
    x_real = x_real.astype(jnp.float32)
    x_imag = x_imag.astype(jnp.float32)
    w_real = w_real.astype(jnp.float32)
    w_imag = w_imag.astype(jnp.float32)
    real_part = jnp.einsum(formula, x_real, w_real) - jnp.einsum(formula, x_imag, w_imag)
    imag_part = jnp.einsum(formula, x_real, w_imag) + jnp.einsum(formula, x_imag, w_real)
    return real_part, imag_part


def projection(spectra, antenna):
    coef_a = antenna[:, 0][:, None, None]
    coef_b = antenna[:, 1][:, None, None]
    coef_c = antenna[:, 2][:, None, None]
    a_real, a_imag, b_real, b_imag = spectra[:, 0], spectra[:, 1], spectra[:, 2], spectra[:, 3]
    numer = coef_b * (a_real * a_real + a_imag * a_imag) + coef_a * (b_real * b_real + b_imag * b_imag) - 2.0 * coef_c * (a_real * b_real + a_imag * b_imag)
    return numer / ((coef_a * coef_b - coef_c * coef_c) * LEN)


def reference(series, antenna, offsets):
    short_real, short_imag = dft_table(NB)
    long_real, long_imag = dft_table(NA)
    columns = jnp.arange(NA, dtype=jnp.int32)
    bins = jnp.arange(NB, dtype=jnp.int32)
    twist = ((columns[:, None] * bins[None, :]) % LEN).astype(jnp.float32) * (2.0 * math.pi / LEN)
    twid_real = jnp.cos(twist)
    twid_imag = -jnp.sin(twist)
    comps = []
    for lead in (0, 2):
        real_part, imag_part = complex_dft(series[:, lead], series[:, lead + 1], short_real, short_imag, "snj,nk->sjk")
        turned_real = (real_part * twid_real - imag_part * twid_imag).astype(jnp.bfloat16)
        turned_imag = (real_part * twid_imag + imag_part * twid_real).astype(jnp.bfloat16)
        out_real, out_imag = complex_dft(turned_real, turned_imag, long_real, long_imag, "sjk,jm->skm")
        comps += [out_real, out_imag]
    spectra = jnp.stack(comps, axis=1)
    fstat = projection(spectra, antenna)
    spectrum_line = jnp.transpose(fstat, (0, 2, 1)).reshape(SEG, LEN)

    def one_template(shift_row):
        total_sum = jnp.zeros((LEN,), jnp.float32)
        for segment in range(SEG):
            total_sum = total_sum + jnp.roll(spectrum_line[segment], -shift_row[segment])
        return (total_sum / SEG).reshape(NA, NB).T

    return lax.map(one_template, offsets)
```

```python
import functools
import math

import jax
import jax.numpy as jnp
import numpy as np
from jax import lax
from jax.experimental import pallas as pl
from jax.experimental.pallas import tpu as pltpu
from jax.sharding import PartitionSpec as P

DMAX = 8
LANES = 128
VMEM_LIMIT = 48 * 1024 * 1024
BF16 = jnp.bfloat16
F32 = jnp.float32


def params():
    return pltpu.CompilerParams(vmem_limit_bytes=VMEM_LIMIT)


def dft_table(length):
    indices = np.arange(length, dtype=np.int32)
    products = indices[:, None] * indices[None, :] % length
    angle = products.astype(np.float32) * np.float32(2.0 * math.pi / length)
    return np.cos(angle).astype(BF16), (-np.sin(angle)).astype(BF16)


def dot(x, y):
    return jnp.dot(x, y, preferred_element_type=F32)


def pack_kernel(x_ref, out_ref):
    cols = out_ref.shape[-1]
    for piece in range(out_ref.shape[0]):
        out_ref[piece] = x_ref[0, :, :, piece * cols : (piece + 1) * cols]


def pack(series, lead, groups):
    segs, _, rows, width = series.shape
    cols = width // groups
    return pl.pallas_call(
        pack_kernel,
        grid=(segs,),
        in_specs=[pl.BlockSpec((1, 2, rows, width), lambda s: (s, lead // 2, 0, 0))],
        out_specs=pl.BlockSpec((groups, 2, rows, cols), lambda s: (s, 0, 0, 0)),
        out_shape=jax.ShapeDtypeStruct((segs * groups, 2, rows, cols), BF16),
        compiler_params=params(),
        cost_estimate=pl.CostEstimate(flops=0, bytes_accessed=2 * 2 * 2 * segs * rows * width, transcendentals=0),
        name="pack",
    )(series)


def first_kernel(x_ref, wr_ref, wi_ref, tr_ref, ti_ref, out_ref):
    length = wr_ref.shape[1]
    cols = x_ref.shape[-1]
    x_real = x_ref[:, 0].reshape(length, cols)
    x_imag = x_ref[:, 1].reshape(length, cols)
    w_real, w_imag = wr_ref[...], wi_ref[...]
    real_part = dot(w_real, x_real) - dot(w_imag, x_imag)
    imag_part = dot(w_imag, x_real) + dot(w_real, x_imag)
    t_real, t_imag = tr_ref[...], ti_ref[...]
    shape = (out_ref.shape[0],) + out_ref.shape[3:]
    out_ref[:, 0, 0] = (real_part * t_real - imag_part * t_imag).astype(BF16).reshape(shape)
    out_ref[:, 1, 0] = (real_part * t_imag + imag_part * t_real).astype(BF16).reshape(shape)


def first_pass(pieces, tables, twiddles, groups):
    count, _, rows, cols = pieces.shape
    length = count * rows
    segs = count // groups
    per_seg = length // segs
    tile = min(256, per_seg)
    owners = tile // rows
    steps = per_seg // tile
    return pl.pallas_call(
        first_kernel,
        grid=(segs, steps),
        in_specs=[
            pl.BlockSpec((count, 2, rows, cols), lambda h, t: (0, 0, 0, 0)),
            pl.BlockSpec((tile, length), lambda h, t: (h * steps + t, 0)),
            pl.BlockSpec((tile, length), lambda h, t: (h * steps + t, 0)),
            pl.BlockSpec((tile, cols), lambda h, t: (h * steps + t, 0)),
            pl.BlockSpec((tile, cols), lambda h, t: (h * steps + t, 0)),
        ],
        out_specs=pl.BlockSpec((owners, 2, 1, rows, cols), lambda h, t: (t, 0, h, 0, 0)),
        out_shape=jax.ShapeDtypeStruct((groups, 2, segs, rows, cols), BF16),
        compiler_params=params(),
        cost_estimate=pl.CostEstimate(
            flops=8 * length * length * cols, bytes_accessed=4 * length * (length + 4 * cols), transcendentals=0
        ),
        name="first_pass",
    )(pieces, *tables, *twiddles)


def gather_rows(z_ref, lhs_ref):
    groups, _, _, _, cols = z_ref.shape
    for piece in range(groups):
        lhs_ref[:, piece * cols : (piece + 1) * cols] = z_ref[piece].reshape(lhs_ref.shape[0], cols)


def transform(lhs_ref, wr_ref, wi_ref):
    half = lhs_ref.shape[0] // 2
    by_real = dot(lhs_ref[...], wr_ref[...])
    by_imag = dot(lhs_ref[...], wi_ref[...])
    return by_real[:half] - by_imag[half:], by_imag[:half] + by_real[half:]


def second_kernel(z_ref, wr_ref, wi_ref, re_ref, im_ref, lhs_ref):
    @pl.when(pl.program_id(0) == 0)
    def _():
        gather_rows(z_ref, lhs_ref)

    re_ref[...], im_ref[...] = transform(lhs_ref, wr_ref, wi_ref)


def fstat_kernel(length, coef_ref, place_ref, z_ref, wr_ref, wi_ref, ar_ref, ai_ref, own_ref, other_ref, head_ref, tail_ref, lhs_ref):
    @pl.when(pl.program_id(0) == 0)
    def _():
        gather_rows(z_ref, lhs_ref)

    b_real, b_imag = transform(lhs_ref, wr_ref, wi_ref)
    a_real, a_imag = ar_ref[...], ai_ref[...]
    coef_a, coef_b, coef_c = coef_ref[0], coef_ref[1], coef_ref[2]
    numer = (
        coef_b * (a_real * a_real + a_imag * a_imag)
        + coef_a * (b_real * b_real + b_imag * b_imag)
        - 2.0 * coef_c * (a_real * b_real + a_imag * b_imag)
    )
    fstat = numer / ((coef_a * coef_b - coef_c * coef_c) * length)
    rows = own_ref.shape[0]
    first, last = fstat[:rows], fstat[rows:]
    is_first = place_ref[0] == 0
    own_ref[...] = jnp.where(is_first, first, last)
    other_ref[...] = jnp.where(is_first, last, first).astype(BF16)
    head_ref[...] = jnp.concatenate([first[:DMAX], last[:DMAX]], axis=0).astype(BF16)
    tail_ref[...] = jnp.concatenate([first[rows - DMAX :], last[rows - DMAX :]], axis=0).astype(BF16)


def second_specs(z, width, tile):
    return [
        pl.BlockSpec(z.shape, lambda t: (0, 0, 0, 0, 0)),
        pl.BlockSpec((width, tile), lambda t: (0, t)),
        pl.BlockSpec((width, tile), lambda t: (0, t)),
    ]


def second_pass(z, tables):
    groups, _, segs, rows, cols = z.shape
    width = groups * cols
    tile = 512
    height = segs * rows
    return pl.pallas_call(
        second_kernel,
        grid=(width // tile,),
        in_specs=second_specs(z, width, tile),
        out_specs=[pl.BlockSpec((height, tile), lambda t: (0, t))] * 2,
        out_shape=[jax.ShapeDtypeStruct((height, width), F32)] * 2,
        scratch_shapes=[pltpu.VMEM((2 * height, width), BF16)],
        compiler_params=params(),
        cost_estimate=pl.CostEstimate(
            flops=8 * height * width * width, bytes_accessed=4 * width * width, transcendentals=0
        ),
        name="second_pass",
    )(z, *tables)


def fstat_pass(z, tables, spectrum, coefs, place, length):
    groups, _, segs, rows, cols = z.shape
    width = groups * cols
    tile = 512
    height = segs * rows
    smem = pl.BlockSpec(memory_space=pltpu.SMEM)
    strip = lambda count: pl.BlockSpec((count, tile), lambda t: (0, t))
    return pl.pallas_call(
        functools.partial(fstat_kernel, length),
        grid=(width // tile,),
        in_specs=[smem, smem] + second_specs(z, width, tile) + [strip(height)] * 2,
        out_specs=[strip(rows), strip(rows), strip(segs * DMAX), strip(segs * DMAX)],
        out_shape=[
            jax.ShapeDtypeStruct((rows, width), F32),
            jax.ShapeDtypeStruct((rows, width), BF16),
            jax.ShapeDtypeStruct((segs * DMAX, width), BF16),
            jax.ShapeDtypeStruct((segs * DMAX, width), BF16),
        ],
        scratch_shapes=[pltpu.VMEM((2 * height, width), BF16)],
        compiler_params=params(),
        cost_estimate=pl.CostEstimate(
            flops=8 * height * width * width, bytes_accessed=4 * width * width, transcendentals=0
        ),
        name="fstat_pass",
    )(coefs, place, z, *tables, *spectrum)


def detect_kernel(offsets_ref, place_ref, own_ref, other_ref, own_rim_ref, other_rim_ref, out_ref, *wide_refs):
    rows = own_ref.shape[0]

    @pl.when(pl.program_id(0) == 0)
    def _():
        is_first, is_last, seg = place_ref[1] == 1, place_ref[2] == 1, place_ref[0]
        width = own_ref.shape[1]

        def widen(wide_ref, middle, rims):
            rims = rims.astype(F32)
            lower, upper = rims[:DMAX], rims[DMAX:]
            lower = jnp.where(is_first, pltpu.roll(lower, 1, 1), lower)
            upper = jnp.where(is_last, pltpu.roll(upper, width - 1, 1), upper)
            for strip in range(width // LANES):
                at = slice(strip * LANES, (strip + 1) * LANES)
                wide_ref[strip, :DMAX] = lower[:, at]
                wide_ref[strip, DMAX : DMAX + rows] = middle[:, at]
                wide_ref[strip, DMAX + rows :] = upper[:, at]

        def place(own_wide, other_wide):
            widen(own_wide, own_ref[...], own_rim_ref[...])
            widen(other_wide, other_ref[...].astype(F32), other_rim_ref[...])

        @pl.when(seg == 0)
        def _():
            place(wide_refs[0], wide_refs[1])

        @pl.when(seg != 0)
        def _():
            place(wide_refs[1], wide_refs[0])

    template = pl.program_id(0)
    begins = [DMAX + offsets_ref[template, s] for s in range(len(wide_refs))]
    for strip in range(own_ref.shape[1] // LANES):
        total = wide_refs[0][strip, pl.ds(begins[0], rows), :]
        for begin, wide_ref in zip(begins[1:], wide_refs[1:]):
            total = total + wide_ref[strip, pl.ds(begin, rows), :]
        out_ref[0, :, strip * LANES : (strip + 1) * LANES] = total / len(wide_refs)


def detect(offsets, place, own, other, own_rims, other_rims):
    templates = offsets.shape[0]
    rows, width = own.shape
    smem = pl.BlockSpec(memory_space=pltpu.SMEM)
    whole = lambda x: pl.BlockSpec(x.shape, lambda t: (0, 0))
    return pl.pallas_call(
        detect_kernel,
        grid=(templates,),
        in_specs=[smem, smem] + [whole(x) for x in (own, other, own_rims, other_rims)],
        out_specs=pl.BlockSpec((1, rows, width), lambda t: (t, 0, 0)),
        out_shape=jax.ShapeDtypeStruct((templates, rows, width), F32),
        scratch_shapes=[pltpu.VMEM((width // LANES, rows + 2 * DMAX, LANES), F32)] * 2,
        compiler_params=params(),
        cost_estimate=pl.CostEstimate(
            flops=3 * templates * rows * width, bytes_accessed=4 * templates * rows * width, transcendentals=0
        ),
        name="detect",
    )(offsets, place, own, other, own_rims, other_rims)


def local(series, antenna, offsets):
    devices = lax.axis_size("tm")
    index = lax.axis_index("tm")
    segs, _, rows, width = series.shape
    groups = devices // segs
    slow = devices * rows
    length = slow * width
    seg = index // groups
    member = index % groups
    cols = width // groups
    short = dft_table(slow)
    long = dft_table(width)

    halves = [[g * groups + i for i in range(groups)] for g in range(segs)]
    pieces = [pack(series, lead, groups) for lead in (0, 2)]
    pieces = [lax.all_to_all(x, "tm", split_axis=0, concat_axis=0, tiled=True) for x in pieces]

    columns = member * cols + jnp.arange(cols, dtype=jnp.int32)
    bins = jnp.arange(slow, dtype=jnp.int32)
    twist = (bins[:, None] * columns[None, :] % length).astype(F32) * (2.0 * math.pi / length)
    twiddles = (jnp.cos(twist), -jnp.sin(twist))

    turned = [first_pass(x, short, twiddles, groups) for x in pieces]
    turned = [
        lax.all_to_all(x, "tm", split_axis=0, concat_axis=0, axis_index_groups=halves, tiled=True) for x in turned
    ]
    spectrum = second_pass(turned[0], long)
    place = jnp.stack([seg, index == 0, index == devices - 1]).astype(jnp.int32)
    coefs = lax.dynamic_index_in_dim(antenna, seg, 0, keepdims=False)
    own, other, heads, tails = fstat_pass(turned[1], long, spectrum, coefs, place, length)

    swap = [(i, (i + groups) % devices) for i in range(devices)]
    other = lax.ppermute(other, "tm", swap)

    up = [(g * groups + i, g * groups + (i + 1) % groups) for g in range(segs) for i in range(groups)]
    down = [(target, source) for source, target in up]
    lower = lax.ppermute(tails, "tm", up).reshape(segs, DMAX, width)
    upper = lax.ppermute(heads, "tm", down).reshape(segs, DMAX, width)
    lower = jnp.where(member == 0, jnp.roll(lower, 1, axis=0), lower)
    upper = jnp.where(member == groups - 1, jnp.roll(upper, -1, axis=0), upper)
    rims = jnp.concatenate([lower, upper], axis=1)
    own_rims = lax.dynamic_index_in_dim(rims, seg, 0, keepdims=False)
    other_rims = lax.ppermute(lax.dynamic_index_in_dim(rims, 1 - seg, 0, keepdims=False), "tm", swap)
    return detect(offsets, place, own, other, own_rims, other_rims)


def solution(mesh):
    return jax.shard_map(
        local,
        mesh=mesh,
        in_specs=(P("sky", None, "tm", None), P("sky", None), P("sky", None)),
        out_specs=P("sky", "tm", None),
        check_vma=False,
    )
```

```python
import functools
import math

import jax
import jax.numpy as jnp
import numpy as np
from jax import lax
from jax.experimental import pallas as pl
from jax.experimental.pallas import tpu as pltpu
from jax.sharding import PartitionSpec as P

DMAX = 8
LANES = 128
DEVICE, CHIP, MEMBER, SEG, FIRST, LAST = range(6)
BF16 = jnp.bfloat16
F32 = jnp.float32


SMEM = pl.BlockSpec(memory_space=pltpu.SMEM)
VMEM = pl.BlockSpec(memory_space=pltpu.VMEM)


def params(mebibytes):
    return pltpu.CompilerParams(vmem_limit_bytes=mebibytes * 1024 * 1024)


def dft_table(length):
    indices = np.arange(length, dtype=np.int32)
    products = indices[:, None] * indices[None, :] % length
    angle = products.astype(np.float32) * np.float32(2.0 * math.pi / length)
    return np.cos(angle).astype(BF16), (-np.sin(angle)).astype(BF16)


def dot(x, y):
    return jnp.dot(x, y, preferred_element_type=F32)


def pack_kernel(lead, place_ref, x_ref, *refs):
    out_refs, sem = refs[:-1], refs[-1]
    cols = out_refs[0].shape[-1]
    groups = x_ref.shape[-1] // cols
    copies = []
    for turn, out_ref in enumerate(out_refs):
        chip = place_ref[CHIP] ^ turn
        begin = pl.multiple_of(chip % groups * cols, cols)
        source = x_ref.at[chip // groups, pl.ds(lead, 2), :, pl.ds(begin, cols)]
        copies.append(pltpu.make_async_copy(source, out_ref, sem.at[turn]))
        copies[-1].start()
    for copy in copies:
        copy.wait()


def pack(series, place, lead, chips):
    segs, _, rows, width = series.shape
    cols = width * segs // chips
    return pl.pallas_call(
        functools.partial(pack_kernel, lead),
        in_specs=[SMEM, pl.BlockSpec(memory_space=pl.ANY)],
        out_specs=[VMEM] * chips,
        out_shape=[jax.ShapeDtypeStruct((2, rows, cols), BF16)] * chips,
        scratch_shapes=[pltpu.SemaphoreType.DMA((chips,))],
        compiler_params=params(16),
        cost_estimate=pl.CostEstimate(flops=0, bytes_accessed=8 * segs * rows * width, transcendentals=0),
        name="pack",
    )(place, series)


def first_kernel(chips, groups, place_ref, *refs):
    piece_refs, refs = refs[: 2 * chips], refs[2 * chips :]
    wr_ref, wi_ref, tr_ref, ti_ref = refs[:4]
    out_refs, x_ref = refs[4:-1], refs[-1]
    rows = piece_refs[0].shape[1]
    for turn in range(2 * chips):
        source = place_ref[DEVICE] ^ turn
        x_ref[:, pl.ds(pl.multiple_of(source * rows, rows), rows), :] = piece_refs[turn][...]
    height = out_refs[0].shape[1]
    cols = x_ref.shape[-1]
    tile = min(256, cols)
    for begin in range(0, cols, tile):
        at = slice(begin, begin + tile)
        x_real, x_imag = x_ref[0, :, at], x_ref[1, :, at]
        w_real, w_imag = wr_ref[...], wi_ref[...]
        real_part = dot(w_real, x_real) - dot(w_imag, x_imag)
        imag_part = dot(w_imag, x_real) + dot(w_real, x_imag)
        t_real, t_imag = tr_ref[:, at], ti_ref[:, at]
        turned_real = (real_part * t_real - imag_part * t_imag).astype(BF16)
        turned_imag = (real_part * t_imag + imag_part * t_real).astype(BF16)
        for turn, out_ref in enumerate(out_refs):
            part = slice(turn * height, (turn + 1) * height)
            out_ref[0, :, at] = turned_real[part]
            out_ref[1, :, at] = turned_imag[part]


def first_pass(pieces, place, tables, twiddles, groups):
    chips = len(pieces) // 2
    _, rows, cols = pieces[0].shape
    length = 2 * chips * rows
    height = length // 2 // groups
    return pl.pallas_call(
        functools.partial(first_kernel, chips, groups),
        in_specs=[SMEM] + [VMEM] * (len(pieces) + 4),
        out_specs=[VMEM] * groups,
        out_shape=[jax.ShapeDtypeStruct((2, height, cols), BF16)] * groups,
        scratch_shapes=[pltpu.VMEM((2, length, cols), BF16)],
        compiler_params=params(16),
        cost_estimate=pl.CostEstimate(
            flops=4 * length * length * cols, bytes_accessed=2 * length * length, transcendentals=0
        ),
        name="first_pass",
    )(place, *pieces, *tables, *twiddles)


def gather_rows(place_ref, piece_refs, lhs_ref):
    @pl.when(pl.program_id(0) == 0)
    def _():
        cols = piece_refs[0].shape[-1]
        for turn, piece_ref in enumerate(piece_refs):
            begin = pl.multiple_of((place_ref[MEMBER] ^ turn) * cols, cols)
            lhs_ref[:, pl.ds(begin, cols)] = piece_ref[...].reshape(lhs_ref.shape[0], cols)


def transform(lhs_ref, wr_ref, wi_ref):
    half = lhs_ref.shape[0] // 2
    by_real = dot(lhs_ref[...], wr_ref[...])
    by_imag = dot(lhs_ref[...], wi_ref[...])
    return by_real[:half] - by_imag[half:], by_imag[:half] + by_real[half:]


def second_kernel(groups, place_ref, *refs):
    wr_ref, wi_ref, re_ref, im_ref, lhs_ref = refs[groups:]
    gather_rows(place_ref, refs[:groups], lhs_ref)
    re_ref[...], im_ref[...] = transform(lhs_ref, wr_ref, wi_ref)


def fstat_kernel(groups, length, place_ref, coef_ref, *refs):
    wr_ref, wi_ref, ar_ref, ai_ref, own_ref, other_ref, head_ref, tail_ref, lhs_ref = refs[groups:]
    gather_rows(place_ref, refs[:groups], lhs_ref)
    b_real, b_imag = transform(lhs_ref, wr_ref, wi_ref)
    a_real, a_imag = ar_ref[...], ai_ref[...]
    coef_a, coef_b, coef_c = coef_ref[0], coef_ref[1], coef_ref[2]
    numer = (
        coef_b * (a_real * a_real + a_imag * a_imag)
        + coef_a * (b_real * b_real + b_imag * b_imag)
        - 2.0 * coef_c * (a_real * b_real + a_imag * b_imag)
    )
    fstat = numer / ((coef_a * coef_b - coef_c * coef_c) * length)
    rows = own_ref.shape[0]
    first, last = fstat[:rows], fstat[rows:]
    is_first = place_ref[SEG] == 0
    own_ref[...] = jnp.where(is_first, first, last)
    other_ref[...] = jnp.where(is_first, last, first).astype(BF16)
    head_ref[...] = jnp.concatenate([first[:DMAX], last[:DMAX]], axis=0).astype(BF16)
    tail_ref[...] = jnp.concatenate([first[rows - DMAX :], last[rows - DMAX :]], axis=0).astype(BF16)


def second_specs(pieces, width, tile):
    return [pl.BlockSpec(x.shape, lambda t: (0, 0, 0)) for x in pieces] + [
        pl.BlockSpec((width, tile), lambda t: (0, t)),
        pl.BlockSpec((width, tile), lambda t: (0, t)),
    ]


def second_pass(pieces, place, tables):
    groups = len(pieces)
    _, height, cols = pieces[0].shape
    width = groups * cols
    tile = 512
    return pl.pallas_call(
        functools.partial(second_kernel, groups),
        grid=(width // tile,),
        in_specs=[SMEM] + second_specs(pieces, width, tile),
        out_specs=[pl.BlockSpec((height, tile), lambda t: (0, t))] * 2,
        out_shape=[jax.ShapeDtypeStruct((height, width), F32)] * 2,
        scratch_shapes=[pltpu.VMEM((2 * height, width), BF16)],
        compiler_params=params(24),
        cost_estimate=pl.CostEstimate(
            flops=8 * height * width * width, bytes_accessed=4 * width * width, transcendentals=0
        ),
        name="second_pass",
    )(place, *pieces, *tables)


def fstat_pass(pieces, place, tables, spectrum, coefs, rows, length):
    groups = len(pieces)
    _, height, cols = pieces[0].shape
    width = groups * cols
    tile = 512
    rims = height // rows * DMAX
    strip = lambda count: pl.BlockSpec((count, tile), lambda t: (0, t))
    return pl.pallas_call(
        functools.partial(fstat_kernel, groups, length),
        grid=(width // tile,),
        in_specs=[SMEM, SMEM] + second_specs(pieces, width, tile) + [strip(height)] * 2,
        out_specs=[strip(rows), strip(rows), strip(rims), strip(rims)],
        out_shape=[
            jax.ShapeDtypeStruct((rows, width), F32),
            jax.ShapeDtypeStruct((rows, width), BF16),
            jax.ShapeDtypeStruct((rims, width), BF16),
            jax.ShapeDtypeStruct((rims, width), BF16),
        ],
        scratch_shapes=[pltpu.VMEM((2 * height, width), BF16)],
        compiler_params=params(24),
        cost_estimate=pl.CostEstimate(
            flops=8 * height * width * width, bytes_accessed=4 * width * width, transcendentals=0
        ),
        name="fstat_pass",
    )(place, coefs, *pieces, *tables, *spectrum)


def detect_kernel(offsets_ref, place_ref, own_ref, other_ref, own_rim_ref, other_rim_ref, out_ref, *wide_refs):
    rows = own_ref.shape[0]

    @pl.when(pl.program_id(0) == 0)
    def _():
        is_first, is_last, seg = place_ref[FIRST] == 1, place_ref[LAST] == 1, place_ref[SEG]
        width = own_ref.shape[1]

        def widen(wide_ref, middle, rims):
            rims = rims.astype(F32)
            lower, upper = rims[:DMAX], rims[DMAX:]
            lower = jnp.where(is_first, pltpu.roll(lower, 1, 1), lower)
            upper = jnp.where(is_last, pltpu.roll(upper, width - 1, 1), upper)
            for strip in range(width // LANES):
                at = slice(strip * LANES, (strip + 1) * LANES)
                wide_ref[strip, :DMAX] = lower[:, at]
                wide_ref[strip, DMAX : DMAX + rows] = middle[:, at]
                wide_ref[strip, DMAX + rows :] = upper[:, at]

        def place(own_wide, other_wide):
            widen(own_wide, own_ref[...], own_rim_ref[...])
            widen(other_wide, other_ref[...].astype(F32), other_rim_ref[...])

        @pl.when(seg == 0)
        def _():
            place(wide_refs[0], wide_refs[1])

        @pl.when(seg != 0)
        def _():
            place(wide_refs[1], wide_refs[0])

    template = pl.program_id(0)
    begins = [DMAX + offsets_ref[template, s] for s in range(len(wide_refs))]
    for strip in range(own_ref.shape[1] // LANES):
        total = wide_refs[0][strip, pl.ds(begins[0], rows), :]
        for begin, wide_ref in zip(begins[1:], wide_refs[1:]):
            total = total + wide_ref[strip, pl.ds(begin, rows), :]
        out_ref[0, :, strip * LANES : (strip + 1) * LANES] = total / len(wide_refs)


def detect(offsets, place, own, other, own_rims, other_rims):
    templates = offsets.shape[0]
    rows, width = own.shape
    whole = lambda x: pl.BlockSpec(x.shape, lambda t: (0, 0))
    return pl.pallas_call(
        detect_kernel,
        grid=(templates,),
        in_specs=[SMEM, SMEM] + [whole(x) for x in (own, other, own_rims, other_rims)],
        out_specs=pl.BlockSpec((1, rows, width), lambda t: (t, 0, 0)),
        out_shape=jax.ShapeDtypeStruct((templates, rows, width), F32),
        scratch_shapes=[pltpu.VMEM((width // LANES, rows + 2 * DMAX, LANES), F32)] * 2,
        compiler_params=params(16),
        cost_estimate=pl.CostEstimate(
            flops=3 * templates * rows * width, bytes_accessed=4 * templates * rows * width, transcendentals=0
        ),
        name="detect",
    )(offsets, place, own, other, own_rims, other_rims)


def trade(pieces, step, devices):
    return [pieces[0]] + [
        lax.ppermute(x, "tm", [(i, i ^ (turn * step)) for i in range(devices)])
        for turn, x in enumerate(pieces)
        if turn
    ]


def share(pieces, devices):
    pairs = [(i, i ^ 1) for i in range(devices)]
    return [y for x in pieces for y in (x, lax.ppermute(x, "tm", pairs))]


def local(series, antenna, offsets):
    devices = lax.axis_size("tm")
    index = lax.axis_index("tm")
    segs, _, rows, width = series.shape
    slow = devices * rows
    length = slow * width
    chips = devices // 2
    groups = chips // segs
    cols = width // groups
    core, chip = index % 2, index // 2
    seg, member = chip // groups, chip % groups
    short = dft_table(slow)
    long = dft_table(width)
    place = jnp.stack([index, chip, member, seg, index == 0, index == devices - 1]).astype(jnp.int32)

    received = [trade(pack(series, place, lead, chips), 2, devices) for lead in (0, 2)]
    received = [share(pieces, devices) for pieces in received]

    def owned(table):
        table = table.reshape((segs, groups, 2, rows) + table.shape[1:])
        table = lax.dynamic_index_in_dim(table, core, 2, keepdims=False)
        parts = [lax.dynamic_index_in_dim(table, member ^ turn, 1, keepdims=False) for turn in range(groups)]
        return jnp.stack(parts).reshape((slow // 2,) + table.shape[3:])

    columns = member * cols + jnp.arange(cols, dtype=jnp.int32)
    bins = owned(jnp.arange(slow, dtype=jnp.int32))
    twist = (bins[:, None] * columns[None, :] % length).astype(F32) * (2.0 * math.pi / length)
    twiddles = (jnp.cos(twist), -jnp.sin(twist))
    short = [owned(jnp.asarray(x)) for x in short]

    turned = [trade(first_pass(x, place, short, twiddles, groups), 2, devices) for x in received]
    spectrum = second_pass(turned[0], place, long)
    coefs = lax.dynamic_index_in_dim(antenna, seg, 0, keepdims=False)
    own, other, heads, tails = fstat_pass(turned[1], place, long, spectrum, coefs, rows, length)

    members = 2 * groups
    swap = [(i, (i + members) % devices) for i in range(devices)]
    other = lax.ppermute(other, "tm", swap)

    up = [(g * members + i, g * members + (i + 1) % members) for g in range(segs) for i in range(members)]
    down = [(target, source) for source, target in up]
    lower = lax.ppermute(tails, "tm", up).reshape(segs, DMAX, width)
    upper = lax.ppermute(heads, "tm", down).reshape(segs, DMAX, width)
    lower = jnp.where(index % members == 0, jnp.roll(lower, 1, axis=0), lower)
    upper = jnp.where(index % members == members - 1, jnp.roll(upper, -1, axis=0), upper)
    rims = jnp.concatenate([lower, upper], axis=1)
    own_rims = lax.dynamic_index_in_dim(rims, seg, 0, keepdims=False)
    other_rims = lax.ppermute(lax.dynamic_index_in_dim(rims, 1 - seg, 0, keepdims=False), "tm", swap)
    return detect(offsets, place, own, other, own_rims, other_rims)


def solution(mesh):
    return jax.shard_map(
        local,
        mesh=mesh,
        in_specs=(P("sky", None, "tm", None), P("sky", None), P("sky", None)),
        out_specs=P("sky", "tm", None),
        check_vma=False,
    )
```

```python
import functools
import math

import jax
import jax.numpy as jnp
import numpy as np
from jax import lax
from jax.experimental import pallas as pl
from jax.experimental.pallas import tpu as pltpu
from jax.sharding import PartitionSpec as P

DMAX = 8
LANES = 128
BF16 = jnp.bfloat16
F32 = jnp.float32
DEVICE, CHIP, MEMBER, CORE, SEG, FIRST, LAST = range(7)
SMEM = pl.BlockSpec(memory_space=pltpu.SMEM)
VMEM = pl.BlockSpec(memory_space=pltpu.VMEM)
ANY = pl.BlockSpec(memory_space=pl.ANY)


def params(mebibytes):
    return pltpu.CompilerParams(vmem_limit_bytes=mebibytes * 1024 * 1024)


def cost(flops, moved):
    return pl.CostEstimate(flops=flops, bytes_accessed=moved, transcendentals=0)


def dft_table(rows, cols, length):
    products = rows[:, None].astype(np.int64) * cols[None, :] % length
    angle = products.astype(np.float32) * np.float32(2.0 * math.pi / length)
    return np.cos(angle), -np.sin(angle)


def dot(x, y):
    return jnp.dot(x, y, preferred_element_type=F32)


def run_copies(copies):
    for copy in copies:
        copy.start()
    for copy in copies:
        copy.wait()


def piece_of(x_ref, place_ref, turn, comps, groups):
    cols = x_ref.shape[-1] // groups
    chip = place_ref[CHIP] ^ turn
    begin = pl.multiple_of(chip % groups * cols, cols)
    return x_ref.at[chip // groups, pl.ds(comps[0], comps[1]), :, pl.ds(begin, cols)]


def pack_kernel(cuts, groups, place_ref, x_ref, *refs):
    out_refs, sem = refs[:-1], refs[-1]
    run_copies(
        [
            pltpu.make_async_copy(piece_of(x_ref, place_ref, turn, comps, groups), out_ref, sem.at[at])
            for at, ((turn, comps), out_ref) in enumerate(zip(cuts, out_refs))
        ]
    )


def pack(series, place, cuts, groups):
    _, _, rows, width = series.shape
    shapes = [(comps[1], rows, width // groups) for _, comps in cuts]
    return pl.pallas_call(
        functools.partial(pack_kernel, cuts, groups),
        in_specs=[SMEM, ANY],
        out_specs=[ANY] * len(cuts),
        out_shape=[jax.ShapeDtypeStruct(shape, BF16) for shape in shapes],
        scratch_shapes=[pltpu.SemaphoreType.DMA((len(cuts),))],
        compiler_params=params(2),
        cost_estimate=cost(0, 4 * sum(math.prod(shape) for shape in shapes)),
        name="pack",
    )(place, series)


def join_kernel(turns, chips, groups, place_ref, x_ref, *refs):
    piece_refs, out_ref, sem = refs[: len(turns)], refs[-2], refs[-1]
    far = chips - groups
    moves = []
    for turn, piece_ref in zip(turns, piece_refs):
        if turn >= groups:
            moves.append((piece_ref, turn - groups))
        else:
            moves += [(piece_ref.at[pl.ds(2 * k, 2)], far + k * groups + turn) for k in range(2)]
    if out_ref.shape[0] > far:
        moves += [(piece_of(x_ref, place_ref, 0, (2 * k, 2), groups), far + k * groups) for k in range(2)]
    run_copies(
        [
            pltpu.make_async_copy(source, out_ref.at[slot], sem.at[at])
            for at, (source, slot) in enumerate(moves)
        ]
    )


def join(series, place, pieces, turns, slots, chips, groups, after):
    shape = (slots, 2) + pieces[0].shape[1:]
    return pl.pallas_call(
        functools.partial(join_kernel, turns, chips, groups),
        in_specs=[SMEM] + [ANY] * (1 + len(pieces) + len(after)),
        out_specs=ANY,
        out_shape=jax.ShapeDtypeStruct(shape, BF16),
        scratch_shapes=[pltpu.SemaphoreType.DMA((slots,))],
        compiler_params=params(2),
        cost_estimate=cost(0, 4 * math.prod(shape)),
        name="join",
    )(place, series, *pieces, *after)


def first_kernel(near_slot, groups, place_ref, *refs):
    near_refs, far_refs, refs = refs[:2], refs[2:4], refs[4:]
    w_refs, t_refs, turn_refs = refs[:2], refs[2:4], refs[4:6]
    out_refs, x_ref = refs[6:-1], refs[-1]
    rows = near_refs[0].shape[2]
    device = place_ref[DEVICE]
    for core in range(2):
        for turn in range(x_ref.shape[1] // rows // 2):
            begin = pl.multiple_of((device ^ (2 * turn + core)) * rows, rows)
            source = far_refs[core].at[turn - groups] if turn >= groups else near_refs[core].at[near_slot + turn]
            x_ref[:, pl.ds(begin, rows), :] = source[...]

    height = out_refs[0].shape[1]
    cols = x_ref.shape[-1]
    tile = min(256, cols)
    owners = [place_ref[CORE] * groups + (place_ref[MEMBER] ^ turn) for turn in range(groups)]
    spots = [pl.ds(pl.multiple_of(owner * height, height), height) for owner in owners]
    stack = lambda ref: jnp.concatenate([ref[spot, :] for spot in spots], axis=0)
    for begin in range(0, cols, tile):
        at = slice(begin, begin + tile)
        x_real, x_imag = x_ref[0, :, at], x_ref[1, :, at]
        w_real, w_imag = stack(w_refs[0]), stack(w_refs[1])
        real_part = dot(w_real, x_real) - dot(w_imag, x_imag)
        imag_part = dot(w_imag, x_real) + dot(w_real, x_imag)
        for turn, (out_ref, spot) in enumerate(zip(out_refs, spots)):
            part = slice(turn * height, (turn + 1) * height)
            by_real, by_imag = turn_refs[0][spot, :], turn_refs[1][spot, :]
            base_real, base_imag = t_refs[0][spot, at], t_refs[1][spot, at]
            t_real = base_real * by_real - base_imag * by_imag
            t_imag = base_real * by_imag + base_imag * by_real
            out_ref[0, :, at] = (real_part[part] * t_real - imag_part[part] * t_imag).astype(BF16)
            out_ref[1, :, at] = (real_part[part] * t_imag + imag_part[part] * t_real).astype(BF16)


def first_pass(near_slot, near, far, place, tables, twiddles, turns, groups):
    _, _, rows, cols = near[0].shape
    length = tables[0].shape[0]
    height = length // 2 // groups
    return pl.pallas_call(
        functools.partial(first_kernel, near_slot, groups),
        in_specs=[SMEM] + [VMEM] * 10,
        out_specs=[VMEM] * groups,
        out_shape=[jax.ShapeDtypeStruct((2, height, cols), BF16)] * groups,
        scratch_shapes=[pltpu.VMEM((2, length, cols), BF16)],
        compiler_params=params(16),
        cost_estimate=cost(4 * length * length * cols, 4 * length * length),
        name="first_pass",
    )(place, *near, *far, *tables, *twiddles, *turns)


def gather_rows(place_ref, piece_refs, lhs_ref):
    cols = piece_refs[0].shape[-1]
    height = lhs_ref.shape[0] // 2
    odd = lax.broadcasted_iota(jnp.int32, (height, cols), 1) % 2 == 1
    for turn, piece_ref in enumerate(piece_refs):
        at = pl.ds(pl.multiple_of((place_ref[MEMBER] ^ turn) * cols, cols), cols)
        piece = piece_ref[...].reshape(height, cols)
        lhs_ref[:height, at] = piece
        lhs_ref[height:, at] = jnp.where(odd, -piece, piece)


def transform(lhs_ref, w_refs, at, store):
    by_real = dot(lhs_ref[...], w_refs[0][:, at])
    by_imag = dot(lhs_ref[...], w_refs[1][:, at])
    rows = lhs_ref.shape[0] // 4
    for half in range(2):
        upper = slice(2 * half * rows, (2 * half + 1) * rows)
        lower = slice((2 * half + 1) * rows, (2 * half + 2) * rows)
        store(half, by_real[upper] - by_imag[lower], by_imag[upper] + by_real[lower])


def second_kernel(groups, place_ref, *refs):
    w_refs, (re_ref, im_ref, lhs_ref) = refs[groups : groups + 2], refs[groups + 2 :]
    gather_rows(place_ref, refs[:groups], lhs_ref)
    span = w_refs[0].shape[1]
    tile = min(256, span)

    def store(begin, half, real_part, imag_part):
        at = pl.ds(pl.multiple_of(half * span + begin, tile), tile)
        re_ref[:, at] = real_part
        im_ref[:, at] = imag_part

    @pl.loop(0, span // tile)
    def _(step):
        begin = pl.multiple_of(step * tile, tile)
        transform(lhs_ref, w_refs, pl.ds(begin, tile), functools.partial(store, begin))


def fstat_kernel(groups, place_ref, coef_ref, *refs):
    w_refs, refs, piece_refs = refs[groups : groups + 2], refs[groups + 2 :], refs[:groups]
    ar_ref, ai_ref, other_ref, own_ref, tail_refs, head_refs, lhs_ref = *refs[:4], refs[4:6], refs[6:8], refs[8]
    gather_rows(place_ref, piece_refs, lhs_ref)
    span = w_refs[0].shape[1]
    tile = min(256, span)
    rows = own_ref.shape[0]
    is_first = place_ref[SEG] == 0
    last_member = 2 * groups - 1
    member = 2 * place_ref[MEMBER] + place_ref[CORE]
    tail_first = jnp.where(member == last_member, 1 - place_ref[SEG], place_ref[SEG]) == 0
    head_first = jnp.where(member == 0, 1 - place_ref[SEG], place_ref[SEG]) == 0

    def store(begin, half, b_real, b_imag):
        at = pl.ds(pl.multiple_of(half * span + begin, tile), tile)
        a_real, a_imag = ar_ref[:, at], ai_ref[:, at]
        fstat = (
            coef_ref[1] * (a_real * a_real + a_imag * a_imag)
            + coef_ref[0] * (b_real * b_real + b_imag * b_imag)
            - coef_ref[2] * (a_real * b_real + a_imag * b_imag)
        )
        first, last = fstat[:rows], fstat[rows:]
        own_ref[:, at] = jnp.where(is_first, first, last)
        other_ref[:, at] = jnp.where(is_first, last, first).astype(BF16)
        rims = pl.ds(half * DMAX, DMAX), pl.ds(begin, tile)
        tails, heads = (first[rows - DMAX :], last[rows - DMAX :]), (first[:DMAX], last[:DMAX])
        for refs, pair, takes_first in ((tail_refs, tails, tail_first), (head_refs, heads, head_first)):
            refs[0][rims] = jnp.where(takes_first, pair[0], pair[1])
            refs[1][rims] = jnp.where(takes_first, pair[1], pair[0])

    @pl.loop(0, span // tile)
    def _(step):
        begin = pl.multiple_of(step * tile, tile)
        transform(lhs_ref, w_refs, pl.ds(begin, tile), functools.partial(store, begin))


def second_pass(pieces, place, tables):
    groups = len(pieces)
    _, height, cols = pieces[0].shape
    width = groups * cols
    return pl.pallas_call(
        functools.partial(second_kernel, groups),
        in_specs=[SMEM] + [VMEM] * (groups + 2),
        out_specs=[VMEM] * 2,
        out_shape=[jax.ShapeDtypeStruct((height, width), F32)] * 2,
        scratch_shapes=[pltpu.VMEM((4 * height, width), BF16)],
        compiler_params=params(16),
        cost_estimate=cost(8 * height * width * width, 2 * width * width),
        name="second_pass",
    )(place, *pieces, *tables)


def fstat_pass(pieces, place, tables, spectrum, coefs, rows):
    groups = len(pieces)
    _, height, cols = pieces[0].shape
    width = groups * cols
    rim = jax.ShapeDtypeStruct((2 * DMAX, width // 2), F32)
    return pl.pallas_call(
        functools.partial(fstat_kernel, groups),
        in_specs=[SMEM, SMEM] + [VMEM] * (groups + 4),
        out_specs=[VMEM] * 6,
        out_shape=[
            jax.ShapeDtypeStruct((rows, width), BF16),
            jax.ShapeDtypeStruct((rows, width), F32),
        ]
        + [rim] * 4,
        scratch_shapes=[pltpu.VMEM((4 * height, width), BF16)],
        compiler_params=params(16),
        cost_estimate=cost(8 * height * width * width, 2 * width * width),
        name="fstat_pass",
    )(place, coefs, *pieces, *tables, *spectrum)


def detect_kernel(offsets_ref, place_ref, other_ref, own_ref, *refs):
    rim_refs, out_ref, wide_refs = refs[:4], refs[4], refs[5:]
    rows = own_ref.shape[0]

    @pl.when(pl.program_id(0) == 0)
    def _():
        is_first, is_last, seg = place_ref[FIRST] == 1, place_ref[LAST] == 1, place_ref[SEG]
        width = own_ref.shape[1]

        def widen(wide_ref, middle, lower_ref, upper_ref):
            lower = jnp.concatenate([lower_ref[:DMAX], lower_ref[DMAX:]], axis=1)
            upper = jnp.concatenate([upper_ref[:DMAX], upper_ref[DMAX:]], axis=1)
            lower = jnp.where(is_first, pltpu.roll(lower, 1, 1), lower)
            upper = jnp.where(is_last, pltpu.roll(upper, width - 1, 1), upper)
            for strip in range(width // LANES):
                at = slice(strip * LANES, (strip + 1) * LANES)
                wide_ref[strip, :DMAX] = lower[:, at]
                wide_ref[strip, DMAX : DMAX + rows] = middle[:, at]
                wide_ref[strip, DMAX + rows :] = upper[:, at]

        def place(own_wide, other_wide):
            widen(own_wide, own_ref[...], *rim_refs[:2])
            widen(other_wide, other_ref[...].astype(F32), *rim_refs[2:])

        @pl.when(seg == 0)
        def _():
            place(wide_refs[0], wide_refs[1])

        @pl.when(seg != 0)
        def _():
            place(wide_refs[1], wide_refs[0])

    template = pl.program_id(0)
    begins = [DMAX + offsets_ref[template, s] for s in range(len(wide_refs))]
    for strip in range(own_ref.shape[1] // LANES):
        total = wide_refs[0][strip, pl.ds(begins[0], rows), :]
        for begin, wide_ref in zip(begins[1:], wide_refs[1:]):
            total = total + wide_ref[strip, pl.ds(begin, rows), :]
        out_ref[0, :, strip * LANES : (strip + 1) * LANES] = total * (1.0 / len(wide_refs))


def detect(offsets, place, other, own, rims):
    templates = offsets.shape[0]
    rows, width = own.shape
    return pl.pallas_call(
        detect_kernel,
        grid=(templates,),
        in_specs=[SMEM, SMEM] + [VMEM] * 6,
        out_specs=pl.BlockSpec((1, rows, width), lambda t: (t, 0, 0)),
        out_shape=jax.ShapeDtypeStruct((templates, rows, width), F32),
        scratch_shapes=[pltpu.VMEM((width // LANES, rows + 2 * DMAX, LANES), F32)] * 2,
        compiler_params=params(8),
        cost_estimate=cost(3 * templates * rows * width, 4 * templates * rows * width),
        name="detect",
    )(offsets, place, other, own, *rims)


def local(series, antenna, offsets):
    devices = lax.axis_size("tm")
    index = lax.axis_index("tm")
    segs, _, rows, width = series.shape
    slow = devices * rows
    length = slow * width
    chips = devices // 2
    groups = chips // segs
    cols = width // groups
    core, chip = index % 2, index // 2
    seg, member = chip // groups, chip % groups
    place = jnp.stack([index, chip, member, core, seg, index == 0, index == devices - 1]).astype(jnp.int32)

    bins = np.arange(slow).reshape(segs, groups, 2, rows).transpose(2, 1, 0, 3).reshape(-1)
    short = [x.astype(BF16) for x in dft_table(bins, np.arange(slow), slow)]
    long = [x.astype(BF16) for x in dft_table(np.arange(width), np.arange(width // 2), width)]
    twiddles = dft_table(bins, np.arange(cols), length)
    angle = (jnp.asarray(bins, jnp.int32) * (member * cols) % length).astype(F32) * (2.0 * math.pi / length)
    turns = (jnp.cos(angle)[:, None], -jnp.sin(angle)[:, None])

    def send(piece, turn):
        return lax.ppermute(piece, "tm", [(i, i ^ turn) for i in range(devices)])

    def pass_on(pieces):
        return [pieces[0]] + [send(x, 2 * turn) for turn, x in enumerate(pieces) if turn]

    far_turns = list(range(groups, chips))[::-1]
    near_turns = list(range(1, groups))[::-1]
    half = len(far_turns) // 2
    both, series_a, series_b = (0, 4), (0, 2), (2, 2)
    cuts_a = [(turn, series_a) for turn in far_turns]
    cuts_a = cuts_a[:half] + [(turn, both) for turn in near_turns] + cuts_a[half:]
    cuts_b = [(turn, series_b) for turn in far_turns]
    packed = pack(series, place, cuts_a + cuts_b, groups)
    turns_a, turns_b = [turn for turn, _ in cuts_a], [turn for turn, _ in cuts_b]
    sent = [send(x, 2 * turn) for x, turn in zip(packed, turns_a + turns_b)]
    sent_a, sent_b = sent[: len(cuts_a)], sent[len(cuts_a) :]

    def pass_one(series_at, near, joined):
        slot = chips - groups + series_at * groups
        return pass_on(first_pass(slot, near, joined, place, short, twiddles, turns, groups))

    joined = join(series, place, sent_a, turns_a, chips + groups, chips, groups, sent_b[:1])
    near = (joined, send(joined, 1))
    turned = [pass_one(0, near, near)]
    joined = join(series, place, sent_b, turns_b, chips - groups, chips, groups, turned[0][1:2])
    turned.append(pass_one(1, near, (joined, send(joined, 1))))
    spectrum = second_pass(turned[0], place, long)
    coef = lax.dynamic_index_in_dim(antenna, seg, 0, keepdims=False)
    scale = (coef[0] * coef[1] - coef[2] * coef[2]) * length
    coefs = coef * jnp.array([1.0, 1.0, 2.0], F32) / scale
    other, own, tail, far_tail, head, far_head = fstat_pass(turned[1], place, long, spectrum, coefs, rows)

    members = 2 * groups
    def moved(x, across, by):
        half_of = lambda i: (i // members + across) % segs * members
        return lax.ppermute(x, "tm", [(i, half_of(i) + (i + by) % members) for i in range(devices)])

    other = moved(other, 1, 0)
    rims = [moved(tail, 0, 1), moved(head, 0, -1), moved(far_tail, 1, 1), moved(far_head, 1, -1)]
    return detect(offsets, place, other, own, rims)


def solution(mesh):
    return jax.shard_map(
        local,
        mesh=mesh,
        in_specs=(P("sky", None, "tm", None), P("sky", None), P("sky", None)),
        out_specs=P("sky", "tm", None),
        check_vma=False,
    )
```

```python
import functools
import math

import jax
import jax.numpy as jnp
import numpy as np
from jax import lax
from jax.experimental import pallas as pl
from jax.experimental.pallas import tpu as pltpu
from jax.sharding import PartitionSpec as P

DMAX = 8
LANES = 128
BF16 = jnp.bfloat16
F32 = jnp.float32
SEG, LOWEST, TOP, FIRST, LAST = range(5)
SMEM = pl.BlockSpec(memory_space=pltpu.SMEM)
VMEM = pl.BlockSpec(memory_space=pltpu.VMEM)
ANY = pl.BlockSpec(memory_space=pl.ANY)


def params(mebibytes):
    return pltpu.CompilerParams(vmem_limit_bytes=mebibytes * 1024 * 1024)


def cost(flops, moved):
    return pl.CostEstimate(flops=flops, bytes_accessed=moved, transcendentals=0)


def dft_table(rows, cols, length):
    products = rows[:, None].astype(np.int64) * cols[None, :] % length
    angle = products.astype(np.float32) * np.float32(2.0 * math.pi / length)
    return np.cos(angle), -np.sin(angle)


def dot(x, y):
    return jnp.dot(x, y, preferred_element_type=F32)


def pack_kernel(x_ref, out_ref, sem):
    count, _, _, cols = out_ref.shape
    groups = x_ref.shape[-1] // cols
    copies = [
        pltpu.make_async_copy(
            x_ref.at[piece // groups, :, :, pl.ds(piece % groups * cols, cols)], out_ref.at[piece], sem.at[piece]
        )
        for piece in range(count)
    ]
    for copy in copies:
        copy.start()
    for copy in copies:
        copy.wait()


def pack(series, groups):
    segs, comps, rows, width = series.shape
    shape = (segs * groups, comps, rows, width // groups)
    return pl.pallas_call(
        pack_kernel,
        in_specs=[ANY],
        out_specs=ANY,
        out_shape=jax.ShapeDtypeStruct(shape, BF16),
        scratch_shapes=[pltpu.SemaphoreType.DMA((shape[0],))],
        compiler_params=params(56),
        cost_estimate=cost(0, 4 * math.prod(shape)),
        name="pack",
    )(series)


def first_kernel(half_ref, x_ref, wr_ref, wi_ref, br_ref, bi_ref, vr_ref, vi_ref, out_ref):
    length = wr_ref.shape[1]
    cols = x_ref.shape[-1]
    shape = (out_ref.shape[0],) + out_ref.shape[2:]
    by_real, by_imag = vr_ref[...], vi_ref[...]
    t_real = br_ref[...] * by_real - bi_ref[...] * by_imag
    t_imag = br_ref[...] * by_imag + bi_ref[...] * by_real
    for lead in range(0, x_ref.shape[1], 2):
        x_real = x_ref[:, lead].reshape(length, cols)
        x_imag = x_ref[:, lead + 1].reshape(length, cols)
        real_part = dot(wr_ref[...], x_real) - dot(wi_ref[...], x_imag)
        imag_part = dot(wi_ref[...], x_real) + dot(wr_ref[...], x_imag)
        out_ref[:, lead] = (real_part * t_real - imag_part * t_imag).astype(BF16).reshape(shape)
        out_ref[:, lead + 1] = (real_part * t_imag + imag_part * t_real).astype(BF16).reshape(shape)


def first_pass(pieces, half, tables, bases, turns, groups):
    count, comps, rows, cols = pieces.shape
    length = count * rows
    per_half = groups * rows
    tile = min(256, per_half)
    steps = per_half // tile
    strip = lambda width: pl.BlockSpec((tile, width), lambda t, half: (half[0] * steps + t, 0))
    return pl.pallas_call(
        first_kernel,
        grid_spec=pltpu.PrefetchScalarGridSpec(
            num_scalar_prefetch=1,
            grid=(steps,),
            in_specs=[pl.BlockSpec(pieces.shape, lambda t, half: (0, 0, 0, 0))]
            + [strip(length)] * 2
            + [strip(cols)] * 2
            + [strip(1)] * 2,
            out_specs=pl.BlockSpec((tile // rows, comps, rows, cols), lambda t, half: (t, 0, 0, 0)),
        ),
        out_shape=jax.ShapeDtypeStruct((groups, comps, rows, cols), BF16),
        compiler_params=params(20),
        cost_estimate=cost(4 * comps * per_half * length * cols, 4 * per_half * length),
        name="first_pass",
    )(half, pieces, *tables, *bases, *turns)


def gather_rows(z_ref, lhs_ref):
    groups, _, _, cols = z_ref.shape
    height = lhs_ref.shape[0] // 2
    odd = lax.broadcasted_iota(jnp.int32, (height, cols), 1) % 2 == 1
    for source in range(groups):
        at = slice(source * cols, (source + 1) * cols)
        piece = z_ref[source].reshape(height, cols)
        lhs_ref[:height, at] = piece
        lhs_ref[height:, at] = jnp.where(odd, -piece, piece)


def fstat_kernel(coef_ref, z_ref, wr_ref, wi_ref, fstat_ref, tail_ref, head_ref, lhs_ref):
    step = pl.program_id(0)

    @pl.when(step == 0)
    def _():
        gather_rows(z_ref, lhs_ref)

    rows, width = fstat_ref.shape
    tile = wr_ref.shape[1]
    by_real = dot(lhs_ref[...], wr_ref[...])
    by_imag = dot(lhs_ref[...], wi_ref[...])
    for half in range(2):
        part = lambda x, comp: x[(4 * half + comp) * rows : (4 * half + comp + 1) * rows]
        a_real = part(by_real, 0) - part(by_imag, 1)
        a_imag = part(by_imag, 0) + part(by_real, 1)
        b_real = part(by_real, 2) - part(by_imag, 3)
        b_imag = part(by_imag, 2) + part(by_real, 3)
        fstat = (
            coef_ref[1] * (a_real * a_real + a_imag * a_imag)
            + coef_ref[0] * (b_real * b_real + b_imag * b_imag)
            - coef_ref[2] * (a_real * b_real + a_imag * b_imag)
        )
        begin = pl.multiple_of(step * tile, tile)
        rims = pl.ds(half * DMAX, DMAX), pl.ds(begin, tile)
        tail_ref[rims] = fstat[rows - DMAX :]
        head_ref[rims] = fstat[:DMAX]
        at = pl.ds(pl.multiple_of(half * (width // 2) + begin, tile), tile)
        fstat_ref[:, at] = fstat.astype(fstat_ref.dtype)


def fstat_pass(z, tables, coefs, kind):
    groups, comps, rows, cols = z.shape
    width = groups * cols
    span = width // 2
    tile = min(256, span)
    rim = (2 * DMAX, span)
    still = lambda shape: pl.BlockSpec(shape, lambda t: (0,) * len(shape))
    return pl.pallas_call(
        fstat_kernel,
        grid=(span // tile,),
        in_specs=[SMEM, still(z.shape)] + [pl.BlockSpec((width, tile), lambda t: (0, t))] * 2,
        out_specs=[still((rows, width)), still(rim), still(rim)],
        out_shape=[jax.ShapeDtypeStruct((rows, width), kind)] + [jax.ShapeDtypeStruct(rim, F32)] * 2,
        scratch_shapes=[pltpu.VMEM((2 * comps * rows, width), BF16)],
        compiler_params=params(24),
        cost_estimate=cost(4 * comps * rows * width * width, 2 * width * width),
        name="fstat_pass",
    )(coefs, z, *tables)


def detect_kernel(offsets_ref, place_ref, other_ref, own_ref, *refs):
    early_refs, late_refs, out_ref, wide_refs = refs[:2], refs[2:4], refs[4], refs[5:]
    rows = own_ref.shape[0]

    @pl.when(pl.program_id(0) == 0)
    def _():
        is_first, is_last, seg = place_ref[FIRST] == 1, place_ref[LAST] == 1, place_ref[SEG]
        lowest, top = place_ref[LOWEST] == 1, place_ref[TOP] == 1
        width = own_ref.shape[1]
        unfold = lambda ref: jnp.concatenate([ref[:DMAX], ref[DMAX:]], axis=1)
        early, late = [unfold(ref) for ref in early_refs], [unfold(ref) for ref in late_refs]

        def widen(wide_ref, middle, lower, upper):
            lower = jnp.where(is_first, pltpu.roll(lower, 1, 1), lower)
            upper = jnp.where(is_last, pltpu.roll(upper, width - 1, 1), upper)
            for strip in range(width // LANES):
                at = slice(strip * LANES, (strip + 1) * LANES)
                wide_ref[strip, :DMAX] = lower[:, at]
                wide_ref[strip, DMAX : DMAX + rows] = middle[:, at]
                wide_ref[strip, DMAX + rows :] = upper[:, at]

        def place(own_wide, other_wide):
            lower = jnp.where(lowest, early[0], late[0]), jnp.where(lowest, late[0], early[0])
            upper = jnp.where(top, early[1], late[1]), jnp.where(top, late[1], early[1])
            widen(own_wide, own_ref[...], lower[0], upper[0])
            widen(other_wide, other_ref[...].astype(F32), lower[1], upper[1])

        @pl.when(seg == 0)
        def _():
            place(wide_refs[0], wide_refs[1])

        @pl.when(seg != 0)
        def _():
            place(wide_refs[1], wide_refs[0])

    template = pl.program_id(0)
    begins = [DMAX + offsets_ref[template, s] for s in range(len(wide_refs))]
    for strip in range(own_ref.shape[1] // LANES):
        total = wide_refs[0][strip, pl.ds(begins[0], rows), :]
        for begin, wide_ref in zip(begins[1:], wide_refs[1:]):
            total = total + wide_ref[strip, pl.ds(begin, rows), :]
        out_ref[0, :, strip * LANES : (strip + 1) * LANES] = total * (1.0 / len(wide_refs))


def detect(offsets, place, other, own, early, late):
    templates = offsets.shape[0]
    rows, width = own.shape
    return pl.pallas_call(
        detect_kernel,
        grid=(templates,),
        in_specs=[SMEM, SMEM] + [VMEM] * 6,
        out_specs=pl.BlockSpec((1, rows, width), lambda t: (t, 0, 0)),
        out_shape=jax.ShapeDtypeStruct((templates, rows, width), F32),
        scratch_shapes=[pltpu.VMEM((width // LANES, rows + 2 * DMAX, LANES), F32)] * 2,
        compiler_params=params(8),
        cost_estimate=cost(3 * templates * rows * width, 4 * templates * rows * width),
        name="detect",
    )(offsets, place, other, own, *early, *late)


def local(series, antenna, offsets):
    devices = lax.axis_size("tm")
    index = lax.axis_index("tm")
    segs, _, rows, width = series.shape
    slow = devices * rows
    length = slow * width
    groups = devices // segs
    cols = width // groups
    seg, member = index // groups, index % groups
    place = jnp.stack([seg, member == 0, member == groups - 1, index == 0, index == devices - 1]).astype(jnp.int32)

    bins = np.arange(slow)
    short = [x.astype(BF16) for x in dft_table(bins, bins, slow)]
    long = [x.astype(BF16) for x in dft_table(np.arange(width), np.arange(width // 2), width)]
    bases = dft_table(bins, np.arange(cols), length)
    angle = (jnp.arange(slow, dtype=jnp.int32) * (member * cols) % length).astype(F32) * (2.0 * math.pi / length)
    turns = (jnp.cos(angle)[:, None], -jnp.sin(angle)[:, None])
    coef = lax.dynamic_index_in_dim(antenna, seg, 0, keepdims=False)
    scale = (coef[0] * coef[1] - coef[2] * coef[2]) * length
    coefs = coef * jnp.array([1.0, 1.0, 2.0], F32) / scale

    halves = [[g * groups + i for i in range(groups)] for g in range(segs)]
    trade = functools.partial(lax.all_to_all, axis_name="tm", split_axis=0, concat_axis=0, tiled=True)
    pieces = trade(pack(series, groups))

    def rows_of(half):
        turned = first_pass(pieces, half[None], short, bases, turns, groups)
        return trade(turned, axis_index_groups=halves)

    def move(x, by):
        return lax.ppermute(x, "tm", [(i, (i + by) % devices) for i in range(devices)])

    far, near = rows_of(1 - seg), rows_of(seg)
    other, tail, head = fstat_pass(far, long, coefs, BF16)
    other = move(other, groups)
    early = [move(tail, groups + 1), move(head, groups - 1)]
    own, tail, head = fstat_pass(near, long, coefs, F32)
    late = [move(tail, 1), move(head, -1)]
    return detect(offsets, place, other, own, early, late)


def solution(mesh):
    return jax.shard_map(
        local,
        mesh=mesh,
        in_specs=(P("sky", None, "tm", None), P("sky", None), P("sky", None)),
        out_specs=P("sky", "tm", None),
        check_vma=False,
    )
```

```python
import functools
import math

import jax
import jax.numpy as jnp
import numpy as np
from jax import lax
from jax.experimental import pallas as pl
from jax.experimental.pallas import tpu as pltpu
from jax.sharding import PartitionSpec as P

DMAX = 8
LANES = 128
BF16 = jnp.bfloat16
F32 = jnp.float32
SEG, LOWEST, TOP, FIRST, LAST = range(5)
SMEM = pl.BlockSpec(memory_space=pltpu.SMEM)
VMEM = pl.BlockSpec(memory_space=pltpu.VMEM)
ANY = pl.BlockSpec(memory_space=pl.ANY)


def params(mebibytes):
    return pltpu.CompilerParams(vmem_limit_bytes=mebibytes * 1024 * 1024)


def cost(flops, moved):
    return pl.CostEstimate(flops=flops, bytes_accessed=moved, transcendentals=0)


def dft_table(rows, cols, length):
    products = rows[:, None].astype(np.int64) * cols[None, :] % length
    angle = products.astype(np.float32) * np.float32(2.0 * math.pi / length)
    return np.cos(angle), -np.sin(angle)


def in_hbm(x):
    return pltpu.with_memory_space_constraint(x, pltpu.HBM)


def dot(x, y):
    return jnp.dot(x, y, preferred_element_type=F32)


def pack_kernel(x_ref, out_ref):
    cols = out_ref.shape[-1]
    for piece in range(out_ref.shape[0]):
        out_ref[piece] = x_ref[0, :, :, piece * cols : (piece + 1) * cols]


def pack(series, groups):
    segs, comps, rows, width = series.shape
    shape = (segs * groups, comps, rows, width // groups)
    return pl.pallas_call(
        pack_kernel,
        grid=(segs,),
        in_specs=[pl.BlockSpec((1, comps, rows, width), lambda s: (s, 0, 0, 0))],
        out_specs=pl.BlockSpec((groups,) + shape[1:], lambda s: (s, 0, 0, 0)),
        out_shape=pltpu.HBM(shape, BF16),
        compiler_params=params(16),
        cost_estimate=cost(0, 4 * math.prod(shape)),
        name="pack",
    )(in_hbm(series))


def first_kernel(half_ref, x_ref, wr_ref, wi_ref, br_ref, bi_ref, vr_ref, vi_ref, out_ref):
    length = wr_ref.shape[1]
    cols = x_ref.shape[-1]
    shape = (out_ref.shape[0],) + out_ref.shape[2:]
    by_real, by_imag = vr_ref[...], vi_ref[...]
    t_real = br_ref[...] * by_real - bi_ref[...] * by_imag
    t_imag = br_ref[...] * by_imag + bi_ref[...] * by_real
    for lead in range(0, x_ref.shape[1], 2):
        x_real = x_ref[:, lead].reshape(length, cols)
        x_imag = x_ref[:, lead + 1].reshape(length, cols)
        real_part = dot(wr_ref[...], x_real) - dot(wi_ref[...], x_imag)
        imag_part = dot(wi_ref[...], x_real) + dot(wr_ref[...], x_imag)
        out_ref[:, lead] = (real_part * t_real - imag_part * t_imag).astype(BF16).reshape(shape)
        out_ref[:, lead + 1] = (real_part * t_imag + imag_part * t_real).astype(BF16).reshape(shape)


def first_pass(pieces, half, tables, bases, turns, groups):
    count, comps, rows, cols = pieces.shape
    length = count * rows
    per_half = groups * rows
    tile = min(256, per_half)
    steps = per_half // tile
    strip = lambda width: pl.BlockSpec((tile, width), lambda t, half: (half[0] * steps + t, 0))
    return pl.pallas_call(
        first_kernel,
        grid_spec=pltpu.PrefetchScalarGridSpec(
            num_scalar_prefetch=1,
            grid=(steps,),
            in_specs=[pl.BlockSpec(pieces.shape, lambda t, half: (0, 0, 0, 0))]
            + [strip(length)] * 2
            + [strip(cols)] * 2
            + [strip(1)] * 2,
            out_specs=pl.BlockSpec((tile // rows, comps, rows, cols), lambda t, half: (t, 0, 0, 0)),
        ),
        out_shape=pltpu.HBM((groups, comps, rows, cols), BF16),
        compiler_params=params(20),
        cost_estimate=cost(4 * comps * per_half * length * cols, 4 * per_half * length),
        name="first_pass",
    )(half, pieces, *map(in_hbm, tables), *map(in_hbm, bases), *turns)


def gather_rows(z_ref, lhs_ref):
    groups, _, _, cols = z_ref.shape
    height = lhs_ref.shape[0] // 2
    odd = lax.broadcasted_iota(jnp.int32, (height, cols), 1) % 2 == 1
    for source in range(groups):
        at = slice(source * cols, (source + 1) * cols)
        piece = z_ref[source].reshape(height, cols)
        lhs_ref[:height, at] = piece
        lhs_ref[height:, at] = jnp.where(odd, -piece, piece)


def fstat_kernel(coef_ref, z_ref, wr_ref, wi_ref, *refs):
    fstat_ref, tail_ref, head_ref, lhs_ref = refs[-4:]
    step = pl.program_id(0)

    @pl.when(step == 0)
    def _():
        gather_rows(z_ref, lhs_ref)

    rows, width = fstat_ref.shape
    tile = wr_ref.shape[1]
    by_real = dot(lhs_ref[...], wr_ref[...])
    by_imag = dot(lhs_ref[...], wi_ref[...])
    for half in range(2):
        part = lambda x, comp: x[(4 * half + comp) * rows : (4 * half + comp + 1) * rows]
        a_real = part(by_real, 0) - part(by_imag, 1)
        a_imag = part(by_imag, 0) + part(by_real, 1)
        b_real = part(by_real, 2) - part(by_imag, 3)
        b_imag = part(by_imag, 2) + part(by_real, 3)
        fstat = (
            coef_ref[1] * (a_real * a_real + a_imag * a_imag)
            + coef_ref[0] * (b_real * b_real + b_imag * b_imag)
            - coef_ref[2] * (a_real * b_real + a_imag * b_imag)
        )
        begin = pl.multiple_of(step * tile, tile)
        rims = pl.ds(half * DMAX, DMAX), pl.ds(begin, tile)
        tail_ref[rims] = fstat[rows - DMAX :]
        head_ref[rims] = fstat[:DMAX]
        at = pl.ds(pl.multiple_of(half * (width // 2) + begin, tile), tile)
        fstat_ref[:, at] = fstat.astype(fstat_ref.dtype)


def fstat_pass(z, tables, coefs, kind, after=()):
    groups, comps, rows, cols = z.shape
    width = groups * cols
    span = width // 2
    tile = min(256, span)
    rim = (2 * DMAX, span)
    still = lambda shape: pl.BlockSpec(shape, lambda t: (0,) * len(shape))
    return pl.pallas_call(
        fstat_kernel,
        grid=(span // tile,),
        in_specs=[SMEM, still(z.shape)] + [pl.BlockSpec((width, tile), lambda t: (0, t))] * 2 + [ANY] * len(after),
        out_specs=[still((rows, width)), still(rim), still(rim)],
        out_shape=[jax.ShapeDtypeStruct((rows, width), kind)] + [jax.ShapeDtypeStruct(rim, F32)] * 2,
        scratch_shapes=[pltpu.VMEM((2 * comps * rows, width), BF16)],
        compiler_params=params(24),
        cost_estimate=cost(4 * comps * rows * width * width, 2 * width * width),
        name="fstat_pass",
    )(coefs, z, *map(in_hbm, tables), *after)


def detect_kernel(offsets_ref, place_ref, other_ref, own_ref, *refs):
    early_refs, late_refs, out_ref, wide_refs = refs[:2], refs[2:4], refs[4], refs[5:]
    rows = own_ref.shape[0]

    @pl.when(pl.program_id(0) == 0)
    def _():
        is_first, is_last, seg = place_ref[FIRST] == 1, place_ref[LAST] == 1, place_ref[SEG]
        lowest, top = place_ref[LOWEST] == 1, place_ref[TOP] == 1
        width = own_ref.shape[1]
        unfold = lambda ref: jnp.concatenate([ref[:DMAX], ref[DMAX:]], axis=1)
        early, late = [unfold(ref) for ref in early_refs], [unfold(ref) for ref in late_refs]

        def widen(wide_ref, middle, lower, upper):
            lower = jnp.where(is_first, pltpu.roll(lower, 1, 1), lower)
            upper = jnp.where(is_last, pltpu.roll(upper, width - 1, 1), upper)
            for strip in range(width // LANES):
                at = slice(strip * LANES, (strip + 1) * LANES)
                wide_ref[strip, :DMAX] = lower[:, at]
                wide_ref[strip, DMAX : DMAX + rows] = middle[:, at]
                wide_ref[strip, DMAX + rows :] = upper[:, at]

        def place(own_wide, other_wide):
            lower = jnp.where(lowest, early[0], late[0]), jnp.where(lowest, late[0], early[0])
            upper = jnp.where(top, early[1], late[1]), jnp.where(top, late[1], early[1])
            widen(own_wide, own_ref[...], lower[0], upper[0])
            widen(other_wide, other_ref[...].astype(F32), lower[1], upper[1])

        @pl.when(seg == 0)
        def _():
            place(wide_refs[0], wide_refs[1])

        @pl.when(seg != 0)
        def _():
            place(wide_refs[1], wide_refs[0])

    template = pl.program_id(0)
    begins = [DMAX + offsets_ref[template, s] for s in range(len(wide_refs))]
    for strip in range(own_ref.shape[1] // LANES):
        total = wide_refs[0][strip, pl.ds(begins[0], rows), :]
        for begin, wide_ref in zip(begins[1:], wide_refs[1:]):
            total = total + wide_ref[strip, pl.ds(begin, rows), :]
        out_ref[0, :, strip * LANES : (strip + 1) * LANES] = total * (1.0 / len(wide_refs))


def detect(offsets, place, other, own, early, late):
    templates = offsets.shape[0]
    rows, width = own.shape
    return pl.pallas_call(
        detect_kernel,
        grid=(templates,),
        in_specs=[SMEM, SMEM] + [VMEM] * 6,
        out_specs=pl.BlockSpec((1, rows, width), lambda t: (t, 0, 0)),
        out_shape=jax.ShapeDtypeStruct((templates, rows, width), F32),
        scratch_shapes=[pltpu.VMEM((width // LANES, rows + 2 * DMAX, LANES), F32)] * 2,
        compiler_params=params(8),
        cost_estimate=cost(3 * templates * rows * width, 4 * templates * rows * width),
        name="detect",
    )(offsets, place, other, own, *early, *late)


def local(series, antenna, offsets):
    devices = lax.axis_size("tm")
    index = lax.axis_index("tm")
    segs, _, rows, width = series.shape
    slow = devices * rows
    length = slow * width
    groups = devices // segs
    cols = width // groups
    seg, member = index // groups, index % groups
    place = jnp.stack([seg, member == 0, member == groups - 1, index == 0, index == devices - 1]).astype(jnp.int32)

    bins = np.arange(slow)
    short = [x.astype(BF16) for x in dft_table(bins, bins, slow)]
    long = [x.astype(BF16) for x in dft_table(np.arange(width), np.arange(width // 2), width)]
    bases = dft_table(bins, np.arange(cols), length)
    angle = (jnp.arange(slow, dtype=jnp.int32) * (member * cols) % length).astype(F32) * (2.0 * math.pi / length)
    turns = (jnp.cos(angle)[:, None], -jnp.sin(angle)[:, None])
    coef = lax.dynamic_index_in_dim(antenna, seg, 0, keepdims=False)
    scale = (coef[0] * coef[1] - coef[2] * coef[2]) * length
    coefs = coef * jnp.array([1.0, 1.0, 2.0], F32) / scale

    halves = [[g * groups + i for i in range(groups)] for g in range(segs)]
    trade = functools.partial(lax.all_to_all, axis_name="tm", split_axis=0, concat_axis=0, tiled=True)
    pieces = trade(pack(series, groups))

    def rows_of(half):
        turned = first_pass(pieces, half[None], short, bases, turns, groups)
        return trade(turned, axis_index_groups=halves)

    def move(x, by):
        return lax.ppermute(x, "tm", [(i, (i + by) % devices) for i in range(devices)])

    far, near = rows_of(1 - seg), rows_of(seg)
    other, tail, head = fstat_pass(far, long, coefs, BF16)
    other = move(other, groups)
    early = [move(tail, groups + 1), move(head, groups - 1)]
    own, tail, head = fstat_pass(near, long, coefs, F32, early)
    late = [move(tail, 1), move(head, -1)]
    return detect(offsets, place, other, own, early, late)


def solution(mesh):
    return jax.shard_map(
        local,
        mesh=mesh,
        in_specs=(P("sky", None, "tm", None), P("sky", None), P("sky", None)),
        out_specs=P("sky", "tm", None),
        check_vma=False,
    )
```

```python
import functools
import math

import jax
import jax.numpy as jnp
import numpy as np
from jax import lax
from jax.experimental import pallas as pl
from jax.experimental.pallas import tpu as pltpu
from jax.sharding import PartitionSpec as P

DMAX = 8
LANES = 128
BF16 = jnp.bfloat16
F32 = jnp.float32
SEG, LOWEST, TOP, FIRST, LAST = range(5)
SMEM = pl.BlockSpec(memory_space=pltpu.SMEM)
VMEM = pl.BlockSpec(memory_space=pltpu.VMEM)
ANY = pl.BlockSpec(memory_space=pl.ANY)


def params(mebibytes):
    return pltpu.CompilerParams(vmem_limit_bytes=mebibytes * 1024 * 1024)


def cost(flops, moved):
    return pl.CostEstimate(flops=flops, bytes_accessed=moved, transcendentals=0)


def dft_table(rows, cols, length):
    products = rows[:, None].astype(np.int64) * cols[None, :] % length
    angle = products.astype(np.float32) * np.float32(2.0 * math.pi / length)
    return np.cos(angle), -np.sin(angle)


def in_hbm(x):
    return pltpu.with_memory_space_constraint(x, pltpu.HBM)


def dot(x, y):
    return jnp.dot(x, y, preferred_element_type=F32)


def pack_kernel(x_ref, out_ref):
    cols = out_ref.shape[-1]
    for piece in range(out_ref.shape[0]):
        out_ref[piece] = x_ref[0, :, :, piece * cols : (piece + 1) * cols]


def pack(series, groups):
    segs, comps, rows, width = series.shape
    shape = (segs * groups, comps, rows, width // groups)
    return pl.pallas_call(
        pack_kernel,
        grid=(segs,),
        in_specs=[pl.BlockSpec((1, comps, rows, width), lambda s: (s, 0, 0, 0))],
        out_specs=pl.BlockSpec((groups,) + shape[1:], lambda s: (s, 0, 0, 0)),
        out_shape=pltpu.HBM(shape, BF16),
        compiler_params=params(16),
        cost_estimate=cost(0, 4 * math.prod(shape)),
        name="pack",
    )(in_hbm(series))


def first_kernel(x_ref, sort_ref, wr_ref, wi_ref, br_ref, bi_ref, vr_ref, vi_ref, out_ref, sorted_ref):
    length = wr_ref.shape[1]
    comps, cols = x_ref.shape[1], x_ref.shape[-1]

    @pl.when(pl.program_id(0) == 0)
    def _():
        for comp in range(comps):
            sorted_ref[comp] = dot(x_ref[:, comp].reshape(length, cols), sort_ref[...]).astype(BF16)

    shape = (out_ref.shape[0],) + out_ref.shape[3:]
    by_real, by_imag = vr_ref[...], vi_ref[...]
    t_real = br_ref[...] * by_real - bi_ref[...] * by_imag
    t_imag = br_ref[...] * by_imag + bi_ref[...] * by_real
    for lead in range(0, comps, 2):
        x_real, x_imag = sorted_ref[lead], sorted_ref[lead + 1]
        real_part = dot(wr_ref[...], x_real) - dot(wi_ref[...], x_imag)
        imag_part = dot(wi_ref[...], x_real) + dot(wr_ref[...], x_imag)
        out_ref[:, 0, lead] = (real_part * t_real - imag_part * t_imag).astype(BF16).reshape(shape)
        out_ref[:, 0, lead + 1] = (real_part * t_imag + imag_part * t_real).astype(BF16).reshape(shape)


def first_pass(pieces, order, tables, bases, turns, groups):
    count, comps, rows, cols = pieces.shape
    length = count * rows
    segs = count // groups
    tile = min(256, groups * rows)
    steps = groups * rows // tile
    sort = np.zeros((cols, cols), np.float32)
    sort[order, np.arange(cols)] = 1.0
    strip = lambda width: pl.BlockSpec((tile, width), lambda t: (t, 0))
    return pl.pallas_call(
        first_kernel,
        grid=(segs * steps,),
        in_specs=[
            pl.BlockSpec(pieces.shape, lambda t: (0, 0, 0, 0)),
            pl.BlockSpec((cols, cols), lambda t: (0, 0)),
        ]
        + [strip(length)] * 2
        + [strip(cols)] * 2
        + [strip(1)] * 2,
        out_specs=pl.BlockSpec((tile // rows, 1, comps, rows, cols), lambda t: (t % steps, t // steps, 0, 0, 0)),
        out_shape=pltpu.HBM((groups, segs, comps, rows, cols), BF16),
        scratch_shapes=[pltpu.VMEM((comps, length, cols), BF16)],
        compiler_params=params(24),
        cost_estimate=cost(4 * comps * length * length * cols, 4 * length * length),
        name="first_pass",
    )(pieces, in_hbm(sort.astype(BF16)), *map(in_hbm, tables), *map(in_hbm, bases), *turns)


def fstat_kernel(half_ref, coef_ref, z_ref, er_ref, ei_ref, or_ref, oi_ref, fstat_ref, tail_ref, head_ref, lhs_ref):
    step = pl.program_id(0)

    @pl.when(step == 0)
    def _():
        groups, cols = z_ref.shape[0], z_ref.shape[-1] // 2
        for source in range(groups):
            piece = z_ref[source, 0].reshape(lhs_ref.shape[1], 2 * cols)
            for parity in range(2):
                at = slice(source * cols, (source + 1) * cols)
                lhs_ref[parity, :, at] = piece[:, parity * cols : (parity + 1) * cols]

    rows, width = fstat_ref.shape
    tile = er_ref.shape[1]
    even, odd = lhs_ref[0], lhs_ref[1]
    even_real, even_imag = dot(even, er_ref[...]), dot(even, ei_ref[...])
    odd_real, odd_imag = dot(odd, or_ref[...]), dot(odd, oi_ref[...])
    tails, heads = [], []
    for half in range(2):
        by_real = even_real - odd_real if half else even_real + odd_real
        by_imag = even_imag - odd_imag if half else even_imag + odd_imag
        part = lambda x, comp: x[comp * rows : (comp + 1) * rows]
        a_real = part(by_real, 0) - part(by_imag, 1)
        a_imag = part(by_imag, 0) + part(by_real, 1)
        b_real = part(by_real, 2) - part(by_imag, 3)
        b_imag = part(by_imag, 2) + part(by_real, 3)
        fstat = (
            coef_ref[1] * (a_real * a_real + a_imag * a_imag)
            + coef_ref[0] * (b_real * b_real + b_imag * b_imag)
            - coef_ref[2] * (a_real * b_real + a_imag * b_imag)
        )
        tails.append(fstat[rows - DMAX :])
        heads.append(fstat[:DMAX])
        at = pl.ds(pl.multiple_of(half * (width // 2) + step * tile, tile), tile)
        fstat_ref[:, at] = fstat.astype(fstat_ref.dtype)
    at = pl.ds(pl.multiple_of(step * tile, tile), tile)
    tail_ref[:, at] = jnp.concatenate(tails, axis=0).astype(tail_ref.dtype)
    head_ref[:, at] = jnp.concatenate(heads, axis=0).astype(head_ref.dtype)


def fstat_pass(z, half, tables, coefs, kind):
    groups, _, comps, rows, cols = z.shape
    width = groups * cols
    span = width // 2
    tile = min(256, span)
    rim = (2 * DMAX, span)
    still = lambda shape: pl.BlockSpec(shape, lambda t, half: (0,) * len(shape))
    return pl.pallas_call(
        fstat_kernel,
        grid_spec=pltpu.PrefetchScalarGridSpec(
            num_scalar_prefetch=1,
            grid=(span // tile,),
            in_specs=[SMEM, pl.BlockSpec((groups, 1, comps, rows, cols), lambda t, half: (0, half[0], 0, 0, 0))]
            + [pl.BlockSpec((span, tile), lambda t, half: (0, t))] * 4,
            out_specs=[still((rows, width)), still(rim), still(rim)],
            scratch_shapes=[pltpu.VMEM((2, comps * rows, span), BF16)],
        ),
        out_shape=[jax.ShapeDtypeStruct((rows, width), kind)] + [jax.ShapeDtypeStruct(rim, kind)] * 2,
        compiler_params=params(24),
        cost_estimate=cost(2 * comps * rows * width * width, 2 * width * width),
        name="fstat_pass",
    )(half, coefs, z, *map(in_hbm, tables))


def detect_kernel(offsets_ref, place_ref, other_ref, own_ref, *refs):
    early_refs, late_refs, out_ref, wide_refs = refs[:2], refs[2:4], refs[4], refs[5:]
    rows = own_ref.shape[0]

    @pl.when(pl.program_id(0) == 0)
    def _():
        is_first, is_last, seg = place_ref[FIRST] == 1, place_ref[LAST] == 1, place_ref[SEG]
        lowest, top = place_ref[LOWEST] == 1, place_ref[TOP] == 1
        width = own_ref.shape[1]
        unfold = lambda ref: jnp.concatenate([ref[...].astype(F32)[:DMAX], ref[...].astype(F32)[DMAX:]], axis=1)
        early, late = [unfold(ref) for ref in early_refs], [unfold(ref) for ref in late_refs]

        def widen(wide_ref, middle, lower, upper):
            lower = jnp.where(is_first, pltpu.roll(lower, 1, 1), lower)
            upper = jnp.where(is_last, pltpu.roll(upper, width - 1, 1), upper)
            for strip in range(width // LANES):
                at = slice(strip * LANES, (strip + 1) * LANES)
                wide_ref[strip, :DMAX] = lower[:, at]
                wide_ref[strip, DMAX : DMAX + rows] = middle[:, at]
                wide_ref[strip, DMAX + rows :] = upper[:, at]

        def place(own_wide, other_wide):
            lower = jnp.where(lowest, early[0], late[0]), jnp.where(lowest, late[0], early[0])
            upper = jnp.where(top, early[1], late[1]), jnp.where(top, late[1], early[1])
            widen(own_wide, own_ref[...], lower[0], upper[0])
            widen(other_wide, other_ref[...].astype(F32), lower[1], upper[1])

        @pl.when(seg == 0)
        def _():
            place(wide_refs[0], wide_refs[1])

        @pl.when(seg != 0)
        def _():
            place(wide_refs[1], wide_refs[0])

    for at in range(out_ref.shape[0]):
        template = pl.program_id(0) * out_ref.shape[0] + at
        begins = [DMAX + offsets_ref[template, s] for s in range(len(wide_refs))]
        for strip in range(own_ref.shape[1] // LANES):
            total = wide_refs[0][strip, pl.ds(begins[0], rows), :]
            for begin, wide_ref in zip(begins[1:], wide_refs[1:]):
                total = total + wide_ref[strip, pl.ds(begin, rows), :]
            out_ref[at, :, strip * LANES : (strip + 1) * LANES] = total * (1.0 / len(wide_refs))


def detect(offsets, place, other, own, early, late):
    templates = offsets.shape[0]
    rows, width = own.shape
    batch = 2 - templates % 2
    return pl.pallas_call(
        detect_kernel,
        grid=(templates // batch,),
        in_specs=[SMEM, SMEM] + [VMEM] * 6,
        out_specs=pl.BlockSpec((batch, rows, width), lambda t: (t, 0, 0)),
        out_shape=jax.ShapeDtypeStruct((templates, rows, width), F32),
        scratch_shapes=[pltpu.VMEM((width // LANES, rows + 2 * DMAX, LANES), F32)] * 2,
        compiler_params=params(8),
        cost_estimate=cost(3 * templates * rows * width, 4 * templates * rows * width),
        name="detect",
    )(offsets, place, other, own, *early, *late)


def local(series, antenna, offsets):
    devices = lax.axis_size("tm")
    index = lax.axis_index("tm")
    segs, _, rows, width = series.shape
    slow = devices * rows
    length = slow * width
    groups = devices // segs
    cols = width // groups
    seg, member = index // groups, index % groups
    place = jnp.stack([seg, member == 0, member == groups - 1, index == 0, index == devices - 1]).astype(jnp.int32)

    bins = np.arange(slow)
    short = [x.astype(BF16) for x in dft_table(bins, bins, slow)]
    fast = np.arange(width // 2)
    long = [x.astype(BF16) for parity in range(2) for x in dft_table(2 * fast + parity, fast, width)]
    order = np.concatenate([np.arange(0, cols, 2), np.arange(1, cols, 2)])
    bases = dft_table(bins, order, length)
    angle = (jnp.arange(slow, dtype=jnp.int32) * (member * cols) % length).astype(F32) * (2.0 * math.pi / length)
    turns = (jnp.cos(angle)[:, None], -jnp.sin(angle)[:, None])
    coef = lax.dynamic_index_in_dim(antenna, seg, 0, keepdims=False)
    scale = (coef[0] * coef[1] - coef[2] * coef[2]) * length
    coefs = coef * jnp.array([1.0, 1.0, 2.0], F32) / scale

    halves = [[g * groups + i for i in range(groups)] for g in range(segs)]
    trade = functools.partial(lax.all_to_all, axis_name="tm", split_axis=0, concat_axis=0, tiled=True)
    pieces = trade(pack(series, groups))

    turned = first_pass(pieces, order, short, bases, turns, groups)
    turned = trade(turned, axis_index_groups=halves)

    def move(x, by):
        return lax.ppermute(x, "tm", [(i, (i + by) % devices) for i in range(devices)])

    other, far_tail, far_head = fstat_pass(turned, 1 - seg[None], long, coefs, BF16)
    other = move(other, groups)
    own, tail, head = fstat_pass(turned, seg[None], long, coefs, F32)
    early = [move(far_tail, groups + 1), move(far_head, groups - 1)]
    late = [move(tail, 1), move(head, -1)]
    return detect(offsets, place, other, own, early, late)


def solution(mesh):
    return jax.shard_map(
        local,
        mesh=mesh,
        in_specs=(P("sky", None, "tm", None), P("sky", None), P("sky", None)),
        out_specs=P("sky", "tm", None),
        check_vma=False,
    )
```

```python
import functools
import math

import jax
import jax.numpy as jnp
import numpy as np
from jax import lax
from jax.experimental import pallas as pl
from jax.experimental.pallas import tpu as pltpu
from jax.sharding import PartitionSpec as P

DMAX = 8
LANES = 128
BF16 = jnp.bfloat16
F32 = jnp.float32
SEG, LOWEST, TOP, FIRST, LAST = range(5)
SMEM = pl.BlockSpec(memory_space=pltpu.SMEM)
VMEM = pl.BlockSpec(memory_space=pltpu.VMEM)
ANY = pl.BlockSpec(memory_space=pl.ANY)


def params(mebibytes):
    return pltpu.CompilerParams(vmem_limit_bytes=mebibytes * 1024 * 1024)


def cost(flops, moved):
    return pl.CostEstimate(flops=flops, bytes_accessed=moved, transcendentals=0)


def dft_table(rows, cols, length):
    products = rows[:, None].astype(np.int64) * cols[None, :] % length
    angle = products.astype(np.float32) * np.float32(2.0 * math.pi / length)
    return np.cos(angle), -np.sin(angle)


def in_hbm(x):
    return pltpu.with_memory_space_constraint(x, pltpu.HBM)


def dot(x, y):
    return jnp.dot(x, y, preferred_element_type=F32)


def pack_kernel(x_ref, sort_ref, out_ref):
    _, comps, rows, cols = out_ref.shape
    for piece in range(out_ref.shape[0]):
        x = x_ref[0, :, :, piece * cols : (piece + 1) * cols].reshape(comps * rows, cols)
        out_ref[piece] = dot(x, sort_ref[...]).astype(BF16).reshape(comps, rows, cols)


def pack(series, order, groups):
    segs, comps, rows, width = series.shape
    cols = width // groups
    batch = max(1, groups // 2)
    shape = (segs * groups, comps, rows, cols)
    sort = np.zeros((cols, cols), np.float32)
    sort[order, np.arange(cols)] = 1.0
    return pl.pallas_call(
        pack_kernel,
        grid=(segs, groups // batch),
        in_specs=[
            pl.BlockSpec((1, comps, rows, batch * cols), lambda s, t: (s, 0, 0, t)),
            pl.BlockSpec((cols, cols), lambda s, t: (0, 0)),
        ],
        out_specs=pl.BlockSpec((batch,) + shape[1:], lambda s, t: (s * (groups // batch) + t, 0, 0, 0)),
        out_shape=pltpu.HBM(shape, BF16),
        compiler_params=params(16),
        cost_estimate=cost(2 * math.prod(shape) * cols, 4 * math.prod(shape)),
        name="pack",
    )(in_hbm(series), in_hbm(sort.astype(BF16)))


def first_kernel(half_ref, x_ref, wr_ref, wi_ref, br_ref, bi_ref, vr_ref, vi_ref, out_ref):
    length = wr_ref.shape[1]
    cols = x_ref.shape[-1]
    shape = (out_ref.shape[0],) + out_ref.shape[2:]
    by_real, by_imag = vr_ref[...], vi_ref[...]
    t_real = br_ref[...] * by_real - bi_ref[...] * by_imag
    t_imag = br_ref[...] * by_imag + bi_ref[...] * by_real
    for lead in range(0, x_ref.shape[1], 2):
        x_real = x_ref[:, lead].reshape(length, cols)
        x_imag = x_ref[:, lead + 1].reshape(length, cols)
        real_part = dot(wr_ref[...], x_real) - dot(wi_ref[...], x_imag)
        imag_part = dot(wi_ref[...], x_real) + dot(wr_ref[...], x_imag)
        out_ref[:, lead] = (real_part * t_real - imag_part * t_imag).astype(BF16).reshape(shape)
        out_ref[:, lead + 1] = (real_part * t_imag + imag_part * t_real).astype(BF16).reshape(shape)


def first_pass(pieces, half, tables, bases, turns, groups):
    count, comps, rows, cols = pieces.shape
    length = count * rows
    per_half = groups * rows
    tile = min(256, per_half)
    steps = per_half // tile
    strip = lambda width: pl.BlockSpec((tile, width), lambda t, half: (half[0] * steps + t, 0))
    return pl.pallas_call(
        first_kernel,
        grid_spec=pltpu.PrefetchScalarGridSpec(
            num_scalar_prefetch=1,
            grid=(steps,),
            in_specs=[pl.BlockSpec(pieces.shape, lambda t, half: (0, 0, 0, 0))]
            + [strip(length)] * 2
            + [strip(cols)] * 2
            + [strip(1)] * 2,
            out_specs=pl.BlockSpec((tile // rows, comps, rows, cols), lambda t, half: (t, 0, 0, 0)),
        ),
        out_shape=pltpu.HBM((groups, comps, rows, cols), BF16),
        compiler_params=params(24),
        cost_estimate=cost(4 * comps * per_half * length * cols, 4 * per_half * length),
        name="first_pass",
    )(half, pieces, *map(in_hbm, tables), *map(in_hbm, bases), *turns)


def fstat_kernel(coef_ref, z_ref, er_ref, ei_ref, or_ref, oi_ref, fstat_ref, tail_ref, head_ref, lhs_ref):
    step = pl.program_id(0)

    @pl.when(step == 0)
    def _():
        groups, cols = z_ref.shape[0], z_ref.shape[-1] // 2
        for source in range(groups):
            piece = z_ref[source].reshape(lhs_ref.shape[1], 2 * cols)
            for parity in range(2):
                at = slice(source * cols, (source + 1) * cols)
                lhs_ref[parity, :, at] = piece[:, parity * cols : (parity + 1) * cols]

    rows, width = fstat_ref.shape
    tile = er_ref.shape[1]
    even, odd = lhs_ref[0], lhs_ref[1]
    even_real, even_imag = dot(even, er_ref[...]), dot(even, ei_ref[...])
    odd_real, odd_imag = dot(odd, or_ref[...]), dot(odd, oi_ref[...])
    tails, heads = [], []
    for half in range(2):
        by_real = even_real - odd_real if half else even_real + odd_real
        by_imag = even_imag - odd_imag if half else even_imag + odd_imag
        part = lambda x, comp: x[comp * rows : (comp + 1) * rows]
        a_real = part(by_real, 0) - part(by_imag, 1)
        a_imag = part(by_imag, 0) + part(by_real, 1)
        b_real = part(by_real, 2) - part(by_imag, 3)
        b_imag = part(by_imag, 2) + part(by_real, 3)
        fstat = (
            coef_ref[1] * (a_real * a_real + a_imag * a_imag)
            + coef_ref[0] * (b_real * b_real + b_imag * b_imag)
            - coef_ref[2] * (a_real * b_real + a_imag * b_imag)
        )
        tails.append(fstat[rows - DMAX :])
        heads.append(fstat[:DMAX])
        at = pl.ds(pl.multiple_of(half * (width // 2) + step * tile, tile), tile)
        fstat_ref[:, at] = fstat.astype(fstat_ref.dtype)
    at = pl.ds(pl.multiple_of(step * tile, tile), tile)
    tail_ref[:, at] = jnp.concatenate(tails, axis=0).astype(tail_ref.dtype)
    head_ref[:, at] = jnp.concatenate(heads, axis=0).astype(head_ref.dtype)


def fstat_pass(z, tables, coefs, kind):
    groups, comps, rows, cols = z.shape
    width = groups * cols
    span = width // 2
    tile = min(256, span)
    rim = (2 * DMAX, span)
    still = lambda shape: pl.BlockSpec(shape, lambda t: (0,) * len(shape))
    return pl.pallas_call(
        fstat_kernel,
        grid=(span // tile,),
        in_specs=[SMEM, still(z.shape)] + [pl.BlockSpec((span, tile), lambda t: (0, t))] * 4,
        out_specs=[still((rows, width)), still(rim), still(rim)],
        out_shape=[jax.ShapeDtypeStruct((rows, width), kind)] + [jax.ShapeDtypeStruct(rim, kind)] * 2,
        scratch_shapes=[pltpu.VMEM((2, comps * rows, span), BF16)],
        compiler_params=params(24),
        cost_estimate=cost(2 * comps * rows * width * width, 2 * width * width),
        name="fstat_pass",
    )(coefs, z, *map(in_hbm, tables))


def detect_kernel(offsets_ref, place_ref, other_ref, own_ref, *refs):
    early_refs, late_refs, out_ref, wide_refs = refs[:2], refs[2:4], refs[4], refs[5:]
    rows = own_ref.shape[0]

    @pl.when(pl.program_id(0) == 0)
    def _():
        is_first, is_last, seg = place_ref[FIRST] == 1, place_ref[LAST] == 1, place_ref[SEG]
        lowest, top = place_ref[LOWEST] == 1, place_ref[TOP] == 1
        width = own_ref.shape[1]
        unfold = lambda ref: jnp.concatenate([ref[...].astype(F32)[:DMAX], ref[...].astype(F32)[DMAX:]], axis=1)
        early, late = [unfold(ref) for ref in early_refs], [unfold(ref) for ref in late_refs]

        def widen(wide_ref, middle, lower, upper):
            lower = jnp.where(is_first, pltpu.roll(lower, 1, 1), lower)
            upper = jnp.where(is_last, pltpu.roll(upper, width - 1, 1), upper)
            for strip in range(width // LANES):
                at = slice(strip * LANES, (strip + 1) * LANES)
                wide_ref[strip, :DMAX] = lower[:, at]
                wide_ref[strip, DMAX : DMAX + rows] = middle[:, at]
                wide_ref[strip, DMAX + rows :] = upper[:, at]

        def place(own_wide, other_wide):
            lower = jnp.where(lowest, early[0], late[0]), jnp.where(lowest, late[0], early[0])
            upper = jnp.where(top, early[1], late[1]), jnp.where(top, late[1], early[1])
            widen(own_wide, own_ref[...], lower[0], upper[0])
            widen(other_wide, other_ref[...].astype(F32), lower[1], upper[1])

        @pl.when(seg == 0)
        def _():
            place(wide_refs[0], wide_refs[1])

        @pl.when(seg != 0)
        def _():
            place(wide_refs[1], wide_refs[0])

    for at in range(out_ref.shape[0]):
        template = pl.program_id(0) * out_ref.shape[0] + at
        begins = [DMAX + offsets_ref[template, s] for s in range(len(wide_refs))]
        for strip in range(own_ref.shape[1] // LANES):
            total = wide_refs[0][strip, pl.ds(begins[0], rows), :]
            for begin, wide_ref in zip(begins[1:], wide_refs[1:]):
                total = total + wide_ref[strip, pl.ds(begin, rows), :]
            out_ref[at, :, strip * LANES : (strip + 1) * LANES] = total * (1.0 / len(wide_refs))


def detect(offsets, place, other, own, early, late):
    templates = offsets.shape[0]
    rows, width = own.shape
    batch = 2 - templates % 2
    return pl.pallas_call(
        detect_kernel,
        grid=(templates // batch,),
        in_specs=[SMEM, SMEM] + [VMEM] * 6,
        out_specs=pl.BlockSpec((batch, rows, width), lambda t: (t, 0, 0)),
        out_shape=jax.ShapeDtypeStruct((templates, rows, width), F32),
        scratch_shapes=[pltpu.VMEM((width // LANES, rows + 2 * DMAX, LANES), F32)] * 2,
        compiler_params=params(8),
        cost_estimate=cost(3 * templates * rows * width, 4 * templates * rows * width),
        name="detect",
    )(offsets, place, other, own, *early, *late)


def local(series, antenna, offsets):
    devices = lax.axis_size("tm")
    index = lax.axis_index("tm")
    segs, _, rows, width = series.shape
    slow = devices * rows
    length = slow * width
    groups = devices // segs
    cols = width // groups
    seg, member = index // groups, index % groups
    place = jnp.stack([seg, member == 0, member == groups - 1, index == 0, index == devices - 1]).astype(jnp.int32)

    bins = np.arange(slow)
    short = [x.astype(BF16) for x in dft_table(bins, bins, slow)]
    fast = np.arange(width // 2)
    long = [x.astype(BF16) for parity in range(2) for x in dft_table(2 * fast + parity, fast, width)]
    order = np.concatenate([np.arange(0, cols, 2), np.arange(1, cols, 2)])
    bases = dft_table(bins, order, length)
    angle = (jnp.arange(slow, dtype=jnp.int32) * (member * cols) % length).astype(F32) * (2.0 * math.pi / length)
    turns = (jnp.cos(angle)[:, None], -jnp.sin(angle)[:, None])
    coef = lax.dynamic_index_in_dim(antenna, seg, 0, keepdims=False)
    scale = (coef[0] * coef[1] - coef[2] * coef[2]) * length
    coefs = coef * jnp.array([1.0, 1.0, 2.0], F32) / scale

    halves = [[g * groups + i for i in range(groups)] for g in range(segs)]
    trade = functools.partial(lax.all_to_all, axis_name="tm", split_axis=0, concat_axis=0, tiled=True)
    pieces = trade(pack(series, order, groups))

    def rows_of(half):
        turned = first_pass(pieces, half[None], short, bases, turns, groups)
        return trade(turned, axis_index_groups=halves)

    def move(x, by):
        return lax.ppermute(x, "tm", [(i, (i + by) % devices) for i in range(devices)])

    far, near = rows_of(1 - seg), rows_of(seg)
    other, far_tail, far_head = fstat_pass(far, long, coefs, BF16)
    other = move(other, groups)
    own, tail, head = fstat_pass(near, long, coefs, F32)
    early = [move(far_tail, groups + 1), move(far_head, groups - 1)]
    late = [move(tail, 1), move(head, -1)]
    return detect(offsets, place, other, own, early, late)


def solution(mesh):
    return jax.shard_map(
        local,
        mesh=mesh,
        in_specs=(P("sky", None, "tm", None), P("sky", None), P("sky", None)),
        out_specs=P("sky", "tm", None),
        check_vma=False,
    )
```

```python
import functools
import math

import jax
import jax.numpy as jnp
import numpy as np
from jax import lax
from jax.experimental import pallas as pl
from jax.experimental.pallas import tpu as pltpu
from jax.sharding import PartitionSpec as P

DMAX = 8
LANES = 128
BF16 = jnp.bfloat16
F32 = jnp.float32
SEG, LOWEST, TOP, FIRST, LAST = range(5)
SMEM = pl.BlockSpec(memory_space=pltpu.SMEM)
VMEM = pl.BlockSpec(memory_space=pltpu.VMEM)
ANY = pl.BlockSpec(memory_space=pl.ANY)


def params(mebibytes):
    return pltpu.CompilerParams(vmem_limit_bytes=mebibytes * 1024 * 1024)


def cost(flops, moved):
    return pl.CostEstimate(flops=flops, bytes_accessed=moved, transcendentals=0)


def dft_table(rows, cols, length):
    products = rows[:, None].astype(np.int64) * cols[None, :] % length
    angle = products.astype(np.float32) * np.float32(2.0 * math.pi / length)
    return np.cos(angle), -np.sin(angle)


def in_hbm(x):
    return pltpu.with_memory_space_constraint(x, pltpu.HBM)


def dot(x, y):
    return jnp.dot(x, y, preferred_element_type=F32)


def pack_kernel(x_ref, out_ref):
    cols = out_ref.shape[-1]
    for piece in range(out_ref.shape[0]):
        out_ref[piece] = x_ref[0, :, :, piece * cols : (piece + 1) * cols]


def pack(series, groups):
    segs, comps, rows, width = series.shape
    shape = (segs * groups, comps, rows, width // groups)
    return pl.pallas_call(
        pack_kernel,
        grid=(segs,),
        in_specs=[pl.BlockSpec((1, comps, rows, width), lambda s: (s, 0, 0, 0))],
        out_specs=pl.BlockSpec((groups,) + shape[1:], lambda s: (s, 0, 0, 0)),
        out_shape=pltpu.HBM(shape, BF16),
        compiler_params=params(16),
        cost_estimate=cost(0, 4 * math.prod(shape)),
        name="pack",
    )(in_hbm(series))


def first_kernel(half_ref, x_ref, sort_ref, wr_ref, wi_ref, br_ref, bi_ref, vr_ref, vi_ref, out_ref, sorted_ref):
    length = wr_ref.shape[1]
    comps, cols = x_ref.shape[1], x_ref.shape[-1]

    @pl.when(pl.program_id(0) == 0)
    def _():
        for comp in range(comps):
            sorted_ref[comp] = dot(x_ref[:, comp].reshape(length, cols), sort_ref[...]).astype(BF16)

    shape = (out_ref.shape[0],) + out_ref.shape[2:]
    by_real, by_imag = vr_ref[...], vi_ref[...]
    t_real = br_ref[...] * by_real - bi_ref[...] * by_imag
    t_imag = br_ref[...] * by_imag + bi_ref[...] * by_real
    for lead in range(0, comps, 2):
        x_real, x_imag = sorted_ref[lead], sorted_ref[lead + 1]
        real_part = dot(wr_ref[...], x_real) - dot(wi_ref[...], x_imag)
        imag_part = dot(wi_ref[...], x_real) + dot(wr_ref[...], x_imag)
        out_ref[:, lead] = (real_part * t_real - imag_part * t_imag).astype(BF16).reshape(shape)
        out_ref[:, lead + 1] = (real_part * t_imag + imag_part * t_real).astype(BF16).reshape(shape)


def first_pass(pieces, half, order, tables, bases, turns, groups):
    count, comps, rows, cols = pieces.shape
    length = count * rows
    per_half = groups * rows
    tile = min(256, per_half)
    steps = per_half // tile
    sort = np.zeros((cols, cols), np.float32)
    sort[order, np.arange(cols)] = 1.0
    strip = lambda width: pl.BlockSpec((tile, width), lambda t, half: (half[0] * steps + t, 0))
    return pl.pallas_call(
        first_kernel,
        grid_spec=pltpu.PrefetchScalarGridSpec(
            num_scalar_prefetch=1,
            grid=(steps,),
            in_specs=[VMEM, pl.BlockSpec((cols, cols), lambda t, half: (0, 0))]
            + [strip(length)] * 2
            + [strip(cols)] * 2
            + [strip(1)] * 2,
            out_specs=pl.BlockSpec((tile // rows, comps, rows, cols), lambda t, half: (t, 0, 0, 0)),
            scratch_shapes=[pltpu.VMEM((comps, length, cols), BF16)],
        ),
        out_shape=pltpu.HBM((groups, comps, rows, cols), BF16),
        compiler_params=params(24),
        cost_estimate=cost(4 * comps * per_half * length * cols, 4 * per_half * length),
        name="first_pass",
    )(half, pieces, in_hbm(sort.astype(BF16)), *map(in_hbm, tables), *map(in_hbm, bases), *turns)


def fstat_kernel(length, place_ref, coef_ref, z_ref, er_ref, ei_ref, or_ref, oi_ref, fstat_ref, lhs_ref):
    step = pl.program_id(0)

    @pl.when(step == 0)
    def _():
        groups, cols = z_ref.shape[0], z_ref.shape[-1] // 2
        for source in range(groups):
            piece = z_ref[source].reshape(lhs_ref.shape[1], 2 * cols)
            for parity in range(2):
                at = slice(source * cols, (source + 1) * cols)
                lhs_ref[parity, :, at] = piece[:, parity * cols : (parity + 1) * cols]

    rows, width = fstat_ref.shape
    tile = er_ref.shape[1]
    even, odd = lhs_ref[0], lhs_ref[1]
    even_real, even_imag = dot(even, er_ref[...]), dot(even, ei_ref[...])
    odd_real, odd_imag = dot(odd, or_ref[...]), dot(odd, oi_ref[...])
    coef_a, coef_b, coef_c = [jnp.full((1, tile), coef_ref[place_ref[SEG], at], F32) for at in range(3)]
    scale = 1.0 / ((coef_a * coef_b - coef_c * coef_c) * length)
    coef_a, coef_b, coef_c = coef_a * scale, coef_b * scale, 2.0 * coef_c * scale
    for half in range(2):
        by_real = even_real - odd_real if half else even_real + odd_real
        by_imag = even_imag - odd_imag if half else even_imag + odd_imag
        part = lambda x, comp: x[comp * rows : (comp + 1) * rows]
        a_real = part(by_real, 0) - part(by_imag, 1)
        a_imag = part(by_imag, 0) + part(by_real, 1)
        b_real = part(by_real, 2) - part(by_imag, 3)
        b_imag = part(by_imag, 2) + part(by_real, 3)
        fstat = (
            coef_b * (a_real * a_real + a_imag * a_imag)
            + coef_a * (b_real * b_real + b_imag * b_imag)
            - coef_c * (a_real * b_real + a_imag * b_imag)
        )
        at = pl.ds(pl.multiple_of(half * (width // 2) + step * tile, tile), tile)
        fstat_ref[:, at] = fstat.astype(fstat_ref.dtype)


def fstat_pass(z, place, tables, antenna, length, kind):
    groups, comps, rows, cols = z.shape
    width = groups * cols
    span = width // 2
    tile = min(256, span)
    return pl.pallas_call(
        functools.partial(fstat_kernel, length),
        grid=(span // tile,),
        in_specs=[SMEM, SMEM, VMEM] + [pl.BlockSpec((span, tile), lambda t: (0, t))] * 4,
        out_specs=pl.BlockSpec((rows, width), lambda t: (0, 0)),
        out_shape=jax.ShapeDtypeStruct((rows, width), kind),
        scratch_shapes=[pltpu.VMEM((2, comps * rows, span), BF16)],
        compiler_params=params(24),
        cost_estimate=cost(2 * comps * rows * width * width, 2 * width * width),
        name="fstat_pass",
    )(place, antenna, z, *map(in_hbm, tables))


def detect_kernel(offsets_ref, place_ref, other_ref, own_ref, lower_ref, upper_ref, out_ref, *wide_refs):
    rows = own_ref.shape[0]

    @pl.when(pl.program_id(0) == 0)
    def _():
        is_first, is_last, seg = place_ref[FIRST] == 1, place_ref[LAST] == 1, place_ref[SEG]
        lowest, top = place_ref[LOWEST] == 1, place_ref[TOP] == 1
        width = own_ref.shape[1]
        rims = [ref[...].astype(F32) for ref in (lower_ref, upper_ref)]
        first, second = [x[:DMAX] for x in rims], [x[DMAX:] for x in rims]

        def widen(wide_ref, middle, lower, upper):
            lower = jnp.where(is_first, pltpu.roll(lower, 1, 1), lower)
            upper = jnp.where(is_last, pltpu.roll(upper, width - 1, 1), upper)
            for strip in range(width // LANES):
                at = slice(strip * LANES, (strip + 1) * LANES)
                wide_ref[strip, :DMAX] = lower[:, at]
                wide_ref[strip, DMAX : DMAX + rows] = middle[:, at]
                wide_ref[strip, DMAX + rows :] = upper[:, at]

        def place(own_wide, other_wide):
            lower = jnp.where(lowest, second[0], first[0]), jnp.where(lowest, first[0], second[0])
            upper = jnp.where(top, second[1], first[1]), jnp.where(top, first[1], second[1])
            widen(own_wide, own_ref[...], lower[0], upper[0])
            widen(other_wide, other_ref[...].astype(F32), lower[1], upper[1])

        @pl.when(seg == 0)
        def _():
            place(wide_refs[0], wide_refs[1])

        @pl.when(seg != 0)
        def _():
            place(wide_refs[1], wide_refs[0])

    for at in range(out_ref.shape[0]):
        template = pl.program_id(0) * out_ref.shape[0] + at
        begins = [DMAX + offsets_ref[template, s] for s in range(len(wide_refs))]
        for strip in range(own_ref.shape[1] // LANES):
            total = wide_refs[0][strip, pl.ds(begins[0], rows), :]
            for begin, wide_ref in zip(begins[1:], wide_refs[1:]):
                total = total + wide_ref[strip, pl.ds(begin, rows), :]
            out_ref[at, :, strip * LANES : (strip + 1) * LANES] = total * (1.0 / len(wide_refs))


def detect(offsets, place, other, own, lower, upper):
    templates = offsets.shape[0]
    rows, width = own.shape
    batch = 2 - templates % 2
    return pl.pallas_call(
        detect_kernel,
        grid=(templates // batch,),
        in_specs=[SMEM, SMEM] + [VMEM] * 4,
        out_specs=pl.BlockSpec((batch, rows, width), lambda t: (t, 0, 0)),
        out_shape=jax.ShapeDtypeStruct((templates, rows, width), F32),
        scratch_shapes=[pltpu.VMEM((width // LANES, rows + 2 * DMAX, LANES), F32)] * 2,
        compiler_params=params(8),
        cost_estimate=cost(3 * templates * rows * width, 4 * templates * rows * width),
        name="detect",
    )(offsets, place, other, own, lower, upper)


def local(series, antenna, offsets):
    devices = lax.axis_size("tm")
    index = lax.axis_index("tm")
    segs, _, rows, width = series.shape
    slow = devices * rows
    length = slow * width
    groups = devices // segs
    cols = width // groups
    seg, member = index // groups, index % groups
    place = jnp.stack([seg, member == 0, member == groups - 1, index == 0, index == devices - 1]).astype(jnp.int32)

    bins = np.arange(slow)
    short = [x.astype(BF16) for x in dft_table(bins, bins, slow)]
    fast = np.arange(width // 2)
    long = [x.astype(BF16) for parity in range(2) for x in dft_table(2 * fast + parity, fast, width)]
    order = np.concatenate([np.arange(0, cols, 2), np.arange(1, cols, 2)])
    bases = dft_table(bins, order, length)
    angle = (jnp.arange(slow, dtype=jnp.int32) * (member * cols) % length).astype(F32) * (2.0 * math.pi / length)
    turns = (jnp.cos(angle)[:, None], -jnp.sin(angle)[:, None])

    halves = [[g * groups + i for i in range(groups)] for g in range(segs)]
    trade = functools.partial(lax.all_to_all, axis_name="tm", split_axis=0, concat_axis=0, tiled=True)
    pieces = trade(pack(series, groups))

    def rows_of(half):
        turned = first_pass(pieces, half[None], order, short, bases, turns, groups)
        return trade(turned, axis_index_groups=halves)

    def move(x, by):
        return lax.ppermute(x, "tm", [(i, (i + by) % devices) for i in range(devices)])

    far, near = rows_of(1 - seg), rows_of(seg)
    other = move(fstat_pass(far, place, long, antenna, length, BF16), groups)
    own = fstat_pass(near, place, long, antenna, length, F32)

    def rims(begin):
        at = slice(begin, begin + DMAX)
        return jnp.concatenate([own[at].astype(BF16), other[at]], axis=0)

    return detect(offsets, place, other, own, move(rims(rows - DMAX), 1), move(rims(0), -1))


def solution(mesh):
    return jax.shard_map(
        local,
        mesh=mesh,
        in_specs=(P("sky", None, "tm", None), P("sky", None), P("sky", None)),
        out_specs=P("sky", "tm", None),
        check_vma=False,
    )
```

```python
import functools
import math

import jax
import jax.numpy as jnp
import numpy as np
from jax import lax
from jax.experimental import pallas as pl
from jax.experimental.pallas import tpu as pltpu
from jax.sharding import PartitionSpec as P

DMAX = 8
LANES = 128
BF16 = jnp.bfloat16
F32 = jnp.float32
SEG, LOWEST, TOP, FIRST, LAST = range(5)
SMEM = pl.BlockSpec(memory_space=pltpu.SMEM)
VMEM = pl.BlockSpec(memory_space=pltpu.VMEM)
ANY = pl.BlockSpec(memory_space=pl.ANY)


def params(mebibytes):
    return pltpu.CompilerParams(vmem_limit_bytes=mebibytes * 1024 * 1024)


def cost(flops, moved):
    return pl.CostEstimate(flops=flops, bytes_accessed=moved, transcendentals=0)


def dft_table(rows, cols, length):
    products = rows[:, None].astype(np.int64) * cols[None, :] % length
    angle = products.astype(np.float32) * np.float32(2.0 * math.pi / length)
    return np.cos(angle), -np.sin(angle)


def in_hbm(x):
    return pltpu.with_memory_space_constraint(x, pltpu.HBM)


def dot(x, y):
    return jnp.dot(x, y, preferred_element_type=F32)


def pack_kernel(x_ref, out_ref):
    cols = out_ref.shape[-1]
    for piece in range(out_ref.shape[0]):
        out_ref[piece] = x_ref[0, :, :, piece * cols : (piece + 1) * cols]


def pack(series, groups):
    segs, comps, rows, width = series.shape
    shape = (segs * groups, comps, rows, width // groups)
    return pl.pallas_call(
        pack_kernel,
        grid=(segs,),
        in_specs=[pl.BlockSpec((1, comps, rows, width), lambda s: (s, 0, 0, 0))],
        out_specs=pl.BlockSpec((groups,) + shape[1:], lambda s: (s, 0, 0, 0)),
        out_shape=pltpu.HBM(shape, BF16),
        compiler_params=params(16),
        cost_estimate=cost(0, 4 * math.prod(shape)),
        name="pack",
    )(in_hbm(series))


def first_kernel(half_ref, x_ref, sort_ref, wr_ref, wi_ref, br_ref, bi_ref, vr_ref, vi_ref, *refs):
    out_ref, sorted_ref = refs[-2:]
    length = wr_ref.shape[1]
    comps, cols = x_ref.shape[1], x_ref.shape[-1]
    spots = [slice(comp * cols, (comp + 1) * cols) for comp in range(comps)]

    @pl.when(pl.program_id(0) == 0)
    def _():
        for comp, spot in enumerate(spots):
            sorted_ref[:, spot] = dot(x_ref[:, comp].reshape(length, cols), sort_ref[...]).astype(BF16)

    shape = (out_ref.shape[0],) + out_ref.shape[2:]
    by_real, by_imag = vr_ref[...], vi_ref[...]
    t_real = br_ref[...] * by_real - bi_ref[...] * by_imag
    t_imag = br_ref[...] * by_imag + bi_ref[...] * by_real
    with_real, with_imag = dot(wr_ref[...], sorted_ref[...]), dot(wi_ref[...], sorted_ref[...])
    for lead in range(0, comps, 2):
        real_part = with_real[:, spots[lead]] - with_imag[:, spots[lead + 1]]
        imag_part = with_imag[:, spots[lead]] + with_real[:, spots[lead + 1]]
        out_ref[:, lead] = (real_part * t_real - imag_part * t_imag).astype(BF16).reshape(shape)
        out_ref[:, lead + 1] = (real_part * t_imag + imag_part * t_real).astype(BF16).reshape(shape)


def first_pass(pieces, half, order, tables, bases, turns, groups, after):
    count, comps, rows, cols = pieces.shape
    length = count * rows
    per_half = groups * rows
    tile = min(256, per_half)
    steps = per_half // tile
    sort = np.zeros((cols, cols), np.float32)
    sort[order, np.arange(cols)] = 1.0
    strip = lambda width: pl.BlockSpec((tile, width), lambda t, half: (half[0] * steps + t, 0))
    return pl.pallas_call(
        first_kernel,
        grid_spec=pltpu.PrefetchScalarGridSpec(
            num_scalar_prefetch=1,
            grid=(steps,),
            in_specs=[VMEM, pl.BlockSpec((cols, cols), lambda t, half: (0, 0))]
            + [strip(length)] * 2
            + [strip(cols)] * 2
            + [strip(1)] * 2
            + [ANY] * len(after),
            out_specs=pl.BlockSpec((tile // rows, comps, rows, cols), lambda t, half: (t, 0, 0, 0)),
            scratch_shapes=[pltpu.VMEM((length, comps * cols), BF16)],
        ),
        out_shape=pltpu.HBM((groups, comps, rows, cols), BF16),
        compiler_params=params(24),
        cost_estimate=cost(4 * comps * per_half * length * cols, 4 * per_half * length),
        name="first_pass",
    )(half, pieces, in_hbm(sort.astype(BF16)), *map(in_hbm, tables), *map(in_hbm, bases), *turns, *after)


def fstat_kernel(length, place_ref, coef_ref, z_ref, w_ref, fstat_ref, lhs_ref):
    step = pl.program_id(0)

    @pl.when(step == 0)
    def _():
        groups, cols = z_ref.shape[0], z_ref.shape[-1] // 2
        for source in range(groups):
            piece = z_ref[source].reshape(lhs_ref.shape[1], 2 * cols)
            for parity in range(2):
                at = slice(source * cols, (source + 1) * cols)
                lhs_ref[parity, :, at] = piece[:, parity * cols : (parity + 1) * cols]

    rows, width = fstat_ref.shape
    tile = w_ref.shape[-1]
    even, odd = lhs_ref[0], lhs_ref[1]
    even_real, even_imag = dot(even, w_ref[0, 0]), dot(even, w_ref[0, 1])
    odd_real, odd_imag = dot(odd, w_ref[0, 2]), dot(odd, w_ref[0, 3])
    coef_a, coef_b, coef_c = [jnp.full((1, tile), coef_ref[place_ref[SEG], at], F32) for at in range(3)]
    scale = 1.0 / ((coef_a * coef_b - coef_c * coef_c) * length)
    coef_a, coef_b, coef_c = coef_a * scale, coef_b * scale, 2.0 * coef_c * scale
    for half in range(2):
        by_real = even_real - odd_real if half else even_real + odd_real
        by_imag = even_imag - odd_imag if half else even_imag + odd_imag
        part = lambda x, comp: x[comp * rows : (comp + 1) * rows]
        a_real = part(by_real, 0) - part(by_imag, 1)
        a_imag = part(by_imag, 0) + part(by_real, 1)
        b_real = part(by_real, 2) - part(by_imag, 3)
        b_imag = part(by_imag, 2) + part(by_real, 3)
        fstat = (
            coef_b * (a_real * a_real + a_imag * a_imag)
            + coef_a * (b_real * b_real + b_imag * b_imag)
            - coef_c * (a_real * b_real + a_imag * b_imag)
        )
        at = pl.ds(pl.multiple_of(half * (width // 2) + step * tile, tile), tile)
        fstat_ref[:, at] = fstat.astype(fstat_ref.dtype)


def fstat_pass(z, place, table, antenna, length, kind):
    groups, comps, rows, cols = z.shape
    width = groups * cols
    return pl.pallas_call(
        functools.partial(fstat_kernel, length),
        grid=(table.shape[0],),
        in_specs=[SMEM, SMEM, VMEM, pl.BlockSpec((1,) + table.shape[1:], lambda t: (t, 0, 0, 0))],
        out_specs=pl.BlockSpec((rows, width), lambda t: (0, 0)),
        out_shape=jax.ShapeDtypeStruct((rows, width), kind),
        scratch_shapes=[pltpu.VMEM((2, comps * rows, width // 2), BF16)],
        compiler_params=params(24),
        cost_estimate=cost(2 * comps * rows * width * width, 2 * width * width),
        name="fstat_pass",
    )(place, antenna, z, in_hbm(table))


def detect_kernel(offsets_ref, place_ref, other_ref, own_ref, lower_ref, upper_ref, out_ref, *wide_refs):
    rows = own_ref.shape[0]

    @pl.when(pl.program_id(0) == 0)
    def _():
        is_first, is_last, seg = place_ref[FIRST] == 1, place_ref[LAST] == 1, place_ref[SEG]
        lowest, top = place_ref[LOWEST] == 1, place_ref[TOP] == 1
        width = own_ref.shape[1]
        rims = [ref[...].astype(F32) for ref in (lower_ref, upper_ref)]
        first, second = [x[:DMAX] for x in rims], [x[DMAX:] for x in rims]

        def widen(wide_ref, middle, lower, upper):
            lower = jnp.where(is_first, pltpu.roll(lower, 1, 1), lower)
            upper = jnp.where(is_last, pltpu.roll(upper, width - 1, 1), upper)
            for strip in range(width // LANES):
                at = slice(strip * LANES, (strip + 1) * LANES)
                wide_ref[strip, :DMAX] = lower[:, at]
                wide_ref[strip, DMAX : DMAX + rows] = middle[:, at]
                wide_ref[strip, DMAX + rows :] = upper[:, at]

        def place(own_wide, other_wide):
            lower = jnp.where(lowest, second[0], first[0]), jnp.where(lowest, first[0], second[0])
            upper = jnp.where(top, second[1], first[1]), jnp.where(top, first[1], second[1])
            widen(own_wide, own_ref[...], lower[0], upper[0])
            widen(other_wide, other_ref[...].astype(F32), lower[1], upper[1])

        @pl.when(seg == 0)
        def _():
            place(wide_refs[0], wide_refs[1])

        @pl.when(seg != 0)
        def _():
            place(wide_refs[1], wide_refs[0])

    for at in range(out_ref.shape[0]):
        template = pl.program_id(0) * out_ref.shape[0] + at
        begins = [DMAX + offsets_ref[template, s] for s in range(len(wide_refs))]
        for strip in range(own_ref.shape[1] // LANES):
            total = wide_refs[0][strip, pl.ds(begins[0], rows), :]
            for begin, wide_ref in zip(begins[1:], wide_refs[1:]):
                total = total + wide_ref[strip, pl.ds(begin, rows), :]
            out_ref[at, :, strip * LANES : (strip + 1) * LANES] = total * (1.0 / len(wide_refs))


def detect(offsets, place, other, own, lower, upper):
    templates = offsets.shape[0]
    rows, width = own.shape
    batch = 2 - templates % 2
    return pl.pallas_call(
        detect_kernel,
        grid=(templates // batch,),
        in_specs=[SMEM, SMEM] + [VMEM] * 4,
        out_specs=pl.BlockSpec((batch, rows, width), lambda t: (t, 0, 0)),
        out_shape=jax.ShapeDtypeStruct((templates, rows, width), F32),
        scratch_shapes=[pltpu.VMEM((width // LANES, rows + 2 * DMAX, LANES), F32)] * 2,
        compiler_params=params(8),
        cost_estimate=cost(3 * templates * rows * width, 4 * templates * rows * width),
        name="detect",
    )(offsets, place, other, own, lower, upper)


def local(series, antenna, offsets):
    devices = lax.axis_size("tm")
    index = lax.axis_index("tm")
    segs, _, rows, width = series.shape
    slow = devices * rows
    length = slow * width
    groups = devices // segs
    cols = width // groups
    seg, member = index // groups, index % groups
    place = jnp.stack([seg, member == 0, member == groups - 1, index == 0, index == devices - 1]).astype(jnp.int32)

    bins = np.arange(slow)
    short = [x.astype(BF16) for x in dft_table(bins, bins, slow)]
    fast = np.arange(width // 2)
    tile = min(256, width // 2)
    long = np.stack([x.astype(BF16) for parity in range(2) for x in dft_table(2 * fast + parity, fast, width)])
    long = long.reshape(4, width // 2, -1, tile).transpose(2, 0, 1, 3)
    order = np.concatenate([np.arange(0, cols, 2), np.arange(1, cols, 2)])
    bases = dft_table(bins, order, length)
    angle = (jnp.arange(slow, dtype=jnp.int32) * (member * cols) % length).astype(F32) * (2.0 * math.pi / length)
    turns = (jnp.cos(angle)[:, None], -jnp.sin(angle)[:, None])

    halves = [[g * groups + i for i in range(groups)] for g in range(segs)]
    trade = functools.partial(lax.all_to_all, axis_name="tm", split_axis=0, concat_axis=0, tiled=True)
    pieces = trade(pack(series, groups))

    def turn(half, *after):
        return first_pass(pieces, half[None], order, short, bases, turns, groups, after)

    def move(x, by):
        return lax.ppermute(x, "tm", [(i, (i + by) % devices) for i in range(devices)])

    far = turn(1 - seg)
    near = turn(seg, far)
    far, near = trade(far, axis_index_groups=halves), trade(near, axis_index_groups=halves)
    other = move(fstat_pass(far, place, long, antenna, length, BF16), groups)
    own = fstat_pass(near, place, long, antenna, length, F32)

    def rims(begin):
        at = slice(begin, begin + DMAX)
        return jnp.concatenate([own[at].astype(BF16), other[at]], axis=0)

    return detect(offsets, place, other, own, move(rims(rows - DMAX), 1), move(rims(0), -1))


def solution(mesh):
    return jax.shard_map(
        local,
        mesh=mesh,
        in_specs=(P("sky", None, "tm", None), P("sky", None), P("sky", None)),
        out_specs=P("sky", "tm", None),
        check_vma=False,
    )
```

```python
import functools
import math

import jax
import jax.numpy as jnp
import numpy as np
from jax import lax
from jax.experimental import pallas as pl
from jax.experimental.pallas import tpu as pltpu
from jax.sharding import PartitionSpec as P

DMAX = 8
LANES = 128
BF16 = jnp.bfloat16
F32 = jnp.float32
SEG, LOWEST, TOP, FIRST, LAST = range(5)
SMEM = pl.BlockSpec(memory_space=pltpu.SMEM)
VMEM = pl.BlockSpec(memory_space=pltpu.VMEM)
ANY = pl.BlockSpec(memory_space=pl.ANY)


def params(mebibytes):
    return pltpu.CompilerParams(vmem_limit_bytes=mebibytes * 1024 * 1024)


def cost(flops, moved):
    return pl.CostEstimate(flops=flops, bytes_accessed=moved, transcendentals=0)


def dft_table(rows, cols, length):
    products = rows[:, None].astype(np.int64) * cols[None, :] % length
    angle = products.astype(np.float32) * np.float32(2.0 * math.pi / length)
    return np.cos(angle), -np.sin(angle)


def in_hbm(x):
    return pltpu.with_memory_space_constraint(x, pltpu.HBM)


def dot(x, y):
    return jnp.dot(x, y, preferred_element_type=F32)


def pack_kernel(x_ref, out_ref):
    cols = out_ref.shape[-1]
    for piece in range(out_ref.shape[0]):
        out_ref[piece] = x_ref[0, :, :, piece * cols : (piece + 1) * cols]


def pack(series, groups):
    segs, comps, rows, width = series.shape
    shape = (segs * groups, comps, rows, width // groups)
    return pl.pallas_call(
        pack_kernel,
        grid=(segs,),
        in_specs=[pl.BlockSpec((1, comps, rows, width), lambda s: (s, 0, 0, 0))],
        out_specs=pl.BlockSpec((groups,) + shape[1:], lambda s: (s, 0, 0, 0)),
        out_shape=pltpu.HBM(shape, BF16),
        compiler_params=params(16),
        cost_estimate=cost(0, 4 * math.prod(shape)),
        name="pack",
    )(in_hbm(series))


def first_kernel(half_ref, x_ref, sort_ref, w_ref, br_ref, bi_ref, vr_ref, vi_ref, *refs):
    out_ref, sorted_ref = refs[-2:]
    tile, length = w_ref.shape[1] // 2, w_ref.shape[2]
    comps, cols = x_ref.shape[1], x_ref.shape[-1]
    spots = [slice(comp * cols, (comp + 1) * cols) for comp in range(comps)]

    @pl.when(pl.program_id(0) == 0)
    def _():
        for comp, spot in enumerate(spots):
            sorted_ref[:, spot] = dot(x_ref[:, comp].reshape(length, cols), sort_ref[...]).astype(BF16)

    shape = (out_ref.shape[0],) + out_ref.shape[2:]
    by_real, by_imag = vr_ref[...], vi_ref[...]
    t_real = br_ref[...] * by_real - bi_ref[...] * by_imag
    t_imag = br_ref[...] * by_imag + bi_ref[...] * by_real
    both = dot(w_ref[0], sorted_ref[...])
    with_real, with_imag = both[:tile], both[tile:]
    for lead in range(0, comps, 2):
        real_part = with_real[:, spots[lead]] - with_imag[:, spots[lead + 1]]
        imag_part = with_imag[:, spots[lead]] + with_real[:, spots[lead + 1]]
        out_ref[:, lead] = (real_part * t_real - imag_part * t_imag).astype(BF16).reshape(shape)
        out_ref[:, lead + 1] = (real_part * t_imag + imag_part * t_real).astype(BF16).reshape(shape)


def first_pass(pieces, half, order, table, bases, turns, groups, after):
    count, comps, rows, cols = pieces.shape
    length = count * rows
    per_half = groups * rows
    tile = table.shape[1] // 2
    steps = per_half // tile
    sort = np.zeros((cols, cols), np.float32)
    sort[order, np.arange(cols)] = 1.0
    strip = lambda width: pl.BlockSpec((tile, width), lambda t, half: (half[0] * steps + t, 0))
    return pl.pallas_call(
        first_kernel,
        grid_spec=pltpu.PrefetchScalarGridSpec(
            num_scalar_prefetch=1,
            grid=(steps,),
            in_specs=[VMEM, pl.BlockSpec((cols, cols), lambda t, half: (0, 0))]
            + [pl.BlockSpec((1,) + table.shape[1:], lambda t, half: (half[0] * steps + t, 0, 0))]
            + [strip(cols)] * 2
            + [strip(1)] * 2
            + [ANY] * len(after),
            out_specs=pl.BlockSpec((tile // rows, comps, rows, cols), lambda t, half: (t, 0, 0, 0)),
            scratch_shapes=[pltpu.VMEM((length, comps * cols), BF16)],
        ),
        out_shape=pltpu.HBM((groups, comps, rows, cols), BF16),
        compiler_params=params(24),
        cost_estimate=cost(4 * comps * per_half * length * cols, 4 * per_half * length),
        name="first_pass",
    )(half, pieces, in_hbm(sort.astype(BF16)), in_hbm(table), *map(in_hbm, bases), *turns, *after)


def fstat_kernel(length, place_ref, coef_ref, z_ref, w_ref, *refs):
    fstat_ref, lhs_ref = refs[-2:]
    groups, comps, rows, width = z_ref.shape
    cols = width // 2
    pitch = lhs_ref.shape[1] // comps
    step = pl.program_id(0)

    @pl.when(step == 0)
    def _():
        if pitch > rows:
            lhs_ref[...] = jnp.zeros_like(lhs_ref)
        for slot, comp in enumerate((0, 2, 1, 3)):
            for source in range(groups):
                for parity in range(2):
                    piece = z_ref[source, comp, :, parity * cols : (parity + 1) * cols]
                    lhs_ref[parity, slot * pitch : slot * pitch + rows, source * cols : (source + 1) * cols] = piece

    tile = w_ref.shape[2] // 2
    turned = (((1,), (1,)), ((), ()))
    sums = [
        lax.dot_general(w_ref[0, parity], lhs_ref[parity], turned, preferred_element_type=F32) for parity in range(2)
    ]
    lanes = 2 * pitch
    coef_a, coef_b, coef_c = [jnp.full((1, lanes), coef_ref[place_ref[SEG], at], F32) for at in range(3)]
    scale = 1.0 / ((coef_a * coef_b - coef_c * coef_c) * length)
    is_a = lax.broadcasted_iota(jnp.int32, (1, lanes), 1) < pitch
    of_power, of_cross = jnp.where(is_a, coef_b, coef_a) * scale, 2.0 * coef_c * scale
    across = lambda x: pltpu.roll(x, pitch, 1)
    for half in range(2):
        total = sums[0] - sums[1] if half else sums[0] + sums[1]
        by_real, by_imag = total[:tile], total[tile:]
        real_part = by_real[:, :lanes] - by_imag[:, lanes:]
        imag_part = by_imag[:, :lanes] + by_real[:, lanes:]
        power = of_power * (real_part * real_part + imag_part * imag_part)
        cross = real_part * across(real_part) + imag_part * across(imag_part)
        fstat = power + across(power) - of_cross * cross
        at = pl.ds(pl.multiple_of(half * fstat_ref.shape[1] // 2 + step * tile, tile), tile)
        fstat_ref[:, at] = fstat.T[:rows].astype(fstat_ref.dtype)


def fstat_pass(z, place, table, antenna, length, kind, after=()):
    groups, comps, rows, cols = z.shape
    width = groups * cols
    pitch = max(rows, LANES // 2)
    return pl.pallas_call(
        functools.partial(fstat_kernel, length),
        grid=(table.shape[0],),
        in_specs=[SMEM, SMEM, VMEM, pl.BlockSpec((1,) + table.shape[1:], lambda t: (t, 0, 0, 0))] + [ANY] * len(after),
        out_specs=pl.BlockSpec((rows, width), lambda t: (0, 0)),
        out_shape=jax.ShapeDtypeStruct((rows, width), kind),
        scratch_shapes=[pltpu.VMEM((2, comps * pitch, width // 2), BF16)],
        compiler_params=params(24),
        cost_estimate=cost(2 * comps * rows * width * width, 2 * width * width),
        name="fstat_pass",
    )(place, antenna, z, in_hbm(table), *after)


def gate(x, after):
    return pl.pallas_call(
        lambda *refs: None,
        in_specs=[ANY, ANY],
        out_specs=ANY,
        out_shape=pltpu.HBM(x.shape, x.dtype),
        input_output_aliases={0: 0},
        compiler_params=params(2),
        cost_estimate=cost(0, 0),
        name="gate",
    )(in_hbm(x), after)


def detect_kernel(offsets_ref, place_ref, other_ref, own_ref, lower_ref, upper_ref, out_ref, *wide_refs):
    rows = own_ref.shape[0]

    @pl.when(pl.program_id(0) == 0)
    def _():
        is_first, is_last, seg = place_ref[FIRST] == 1, place_ref[LAST] == 1, place_ref[SEG]
        lowest, top = place_ref[LOWEST] == 1, place_ref[TOP] == 1
        width = own_ref.shape[1]
        rims = [ref[...].astype(F32) for ref in (lower_ref, upper_ref)]
        first, second = [x[:DMAX] for x in rims], [x[DMAX:] for x in rims]

        def widen(wide_ref, middle, lower, upper):
            lower = jnp.where(is_first, pltpu.roll(lower, 1, 1), lower)
            upper = jnp.where(is_last, pltpu.roll(upper, width - 1, 1), upper)
            for strip in range(width // LANES):
                at = slice(strip * LANES, (strip + 1) * LANES)
                wide_ref[strip, :DMAX] = lower[:, at]
                wide_ref[strip, DMAX : DMAX + rows] = middle[:, at]
                wide_ref[strip, DMAX + rows :] = upper[:, at]

        def place(own_wide, other_wide):
            lower = jnp.where(lowest, second[0], first[0]), jnp.where(lowest, first[0], second[0])
            upper = jnp.where(top, second[1], first[1]), jnp.where(top, first[1], second[1])
            widen(own_wide, own_ref[...], lower[0], upper[0])
            widen(other_wide, other_ref[...].astype(F32), lower[1], upper[1])

        @pl.when(seg == 0)
        def _():
            place(wide_refs[0], wide_refs[1])

        @pl.when(seg != 0)
        def _():
            place(wide_refs[1], wide_refs[0])

    for at in range(out_ref.shape[0]):
        template = pl.program_id(0) * out_ref.shape[0] + at
        begins = [DMAX + offsets_ref[template, s] for s in range(len(wide_refs))]
        for strip in range(own_ref.shape[1] // LANES):
            total = wide_refs[0][strip, pl.ds(begins[0], rows), :]
            for begin, wide_ref in zip(begins[1:], wide_refs[1:]):
                total = total + wide_ref[strip, pl.ds(begin, rows), :]
            out_ref[at, :, strip * LANES : (strip + 1) * LANES] = total * (1.0 / len(wide_refs))


def detect(offsets, place, other, own, lower, upper):
    templates = offsets.shape[0]
    rows, width = own.shape
    batch = 2 - templates % 2
    return pl.pallas_call(
        detect_kernel,
        grid=(templates // batch,),
        in_specs=[SMEM, SMEM] + [VMEM] * 4,
        out_specs=pl.BlockSpec((batch, rows, width), lambda t: (t, 0, 0)),
        out_shape=jax.ShapeDtypeStruct((templates, rows, width), F32),
        scratch_shapes=[pltpu.VMEM((width // LANES, rows + 2 * DMAX, LANES), F32)] * 2,
        compiler_params=params(8),
        cost_estimate=cost(3 * templates * rows * width, 4 * templates * rows * width),
        name="detect",
    )(offsets, place, other, own, lower, upper)


def local(series, antenna, offsets):
    devices = lax.axis_size("tm")
    index = lax.axis_index("tm")
    segs, _, rows, width = series.shape
    slow = devices * rows
    length = slow * width
    groups = devices // segs
    cols = width // groups
    seg, member = index // groups, index % groups
    place = jnp.stack([seg, member == 0, member == groups - 1, index == 0, index == devices - 1]).astype(jnp.int32)

    bins = np.arange(slow)
    tile = min(256, groups * rows)
    short = np.stack(dft_table(bins, bins, slow)).astype(BF16).reshape(2, -1, tile, slow)
    short = short.transpose(1, 0, 2, 3).reshape(-1, 2 * tile, slow)
    fast = np.arange(width // 2)
    tile = min(256, width // 2)
    long = np.stack([np.stack(dft_table(fast, 2 * fast + parity, width)) for parity in range(2)]).astype(BF16)
    long = long.reshape(2, 2, -1, tile, width // 2).transpose(2, 0, 1, 3, 4).reshape(-1, 2, 2 * tile, width // 2)
    order = np.concatenate([np.arange(0, cols, 2), np.arange(1, cols, 2)])
    bases = dft_table(bins, order, length)
    angle = (jnp.arange(slow, dtype=jnp.int32) * (member * cols) % length).astype(F32) * (2.0 * math.pi / length)
    turns = (jnp.cos(angle)[:, None], -jnp.sin(angle)[:, None])

    halves = [[g * groups + i for i in range(groups)] for g in range(segs)]
    trade = functools.partial(lax.all_to_all, axis_name="tm", split_axis=0, concat_axis=0, tiled=True)
    pieces = trade(pack(series, groups))

    def turn(half, *after):
        return first_pass(pieces, half[None], order, short, bases, turns, groups, after)

    def move(x, by):
        return lax.ppermute(x, "tm", [(i, (i + by) % devices) for i in range(devices)])

    far = turn(1 - seg)
    near = turn(seg, far)
    far = trade(far, axis_index_groups=halves)
    near = trade(gate(near, far), axis_index_groups=halves)
    far = fstat_pass(far, place, long, antenna, length, BF16)
    other = move(far, groups)
    own = fstat_pass(near, place, long, antenna, length, F32, (far,))

    def rims(begin):
        at = slice(begin, begin + DMAX)
        return jnp.concatenate([own[at].astype(BF16), other[at]], axis=0)

    return detect(offsets, place, other, own, move(rims(rows - DMAX), 1), move(rims(0), -1))


def solution(mesh):
    return jax.shard_map(
        local,
        mesh=mesh,
        in_specs=(P("sky", None, "tm", None), P("sky", None), P("sky", None)),
        out_specs=P("sky", "tm", None),
        check_vma=False,
    )
```

```python
import functools
import math

import jax
import jax.numpy as jnp
import numpy as np
from jax import lax
from jax.experimental import pallas as pl
from jax.experimental.pallas import tpu as pltpu
from jax.sharding import PartitionSpec as P

DMAX = 8
LANES = 128
BF16 = jnp.bfloat16
F32 = jnp.float32
SEG, LOWEST, TOP, FIRST, LAST = range(5)
SMEM = pl.BlockSpec(memory_space=pltpu.SMEM)
VMEM = pl.BlockSpec(memory_space=pltpu.VMEM)
ANY = pl.BlockSpec(memory_space=pl.ANY)


def params(mebibytes):
    return pltpu.CompilerParams(vmem_limit_bytes=mebibytes * 1024 * 1024)


def cost(flops, moved):
    return pl.CostEstimate(flops=flops, bytes_accessed=moved, transcendentals=0)


def dft_table(rows, cols, length):
    products = rows[:, None].astype(np.int64) * cols[None, :] % length
    angle = products.astype(np.float32) * np.float32(2.0 * math.pi / length)
    return np.cos(angle), -np.sin(angle)


def in_hbm(x):
    return pltpu.with_memory_space_constraint(x, pltpu.HBM)


def dot(x, y):
    return jnp.dot(x, y, preferred_element_type=F32)


def pack_kernel(x_ref, out_ref):
    cols = out_ref.shape[-1]
    for piece in range(out_ref.shape[0]):
        out_ref[piece] = x_ref[0, :, :, piece * cols : (piece + 1) * cols]


def pack(series, groups):
    segs, comps, rows, width = series.shape
    shape = (segs * groups, comps, rows, width // groups)
    return pl.pallas_call(
        pack_kernel,
        grid=(segs,),
        in_specs=[pl.BlockSpec((1, comps, rows, width), lambda s: (s, 0, 0, 0))],
        out_specs=pl.BlockSpec((groups,) + shape[1:], lambda s: (s, 0, 0, 0)),
        out_shape=pltpu.HBM(shape, BF16),
        compiler_params=params(16),
        cost_estimate=cost(0, 4 * math.prod(shape)),
        name="pack",
    )(in_hbm(series))


def first_kernel(half_ref, x_ref, sort_ref, w_ref, br_ref, bi_ref, vr_ref, vi_ref, *refs):
    out_ref, sorted_ref = refs[-2:]
    tile, length = w_ref.shape[1] // 2, w_ref.shape[2]
    comps, cols = x_ref.shape[1], x_ref.shape[-1]
    spots = [slice(comp * cols, (comp + 1) * cols) for comp in range(comps)]

    @pl.when(pl.program_id(0) == 0)
    def _():
        for comp, spot in enumerate(spots):
            sorted_ref[:, spot] = dot(x_ref[:, comp].reshape(length, cols), sort_ref[...]).astype(BF16)

    shape = (out_ref.shape[0],) + out_ref.shape[2:]
    by_real, by_imag = vr_ref[...], vi_ref[...]
    t_real = br_ref[...] * by_real - bi_ref[...] * by_imag
    t_imag = br_ref[...] * by_imag + bi_ref[...] * by_real
    both = dot(w_ref[0], sorted_ref[...])
    with_real, with_imag = both[:tile], both[tile:]
    for lead in range(0, comps, 2):
        real_part = with_real[:, spots[lead]] - with_imag[:, spots[lead + 1]]
        imag_part = with_imag[:, spots[lead]] + with_real[:, spots[lead + 1]]
        out_ref[:, lead] = (real_part * t_real - imag_part * t_imag).astype(BF16).reshape(shape)
        out_ref[:, lead + 1] = (real_part * t_imag + imag_part * t_real).astype(BF16).reshape(shape)


def first_pass(pieces, half, order, table, bases, turns, groups, after):
    count, comps, rows, cols = pieces.shape
    length = count * rows
    per_half = groups * rows
    tile = table.shape[1] // 2
    steps = per_half // tile
    sort = np.zeros((cols, cols), np.float32)
    sort[order, np.arange(cols)] = 1.0
    strip = lambda width: pl.BlockSpec((tile, width), lambda t, half: (half[0] * steps + t, 0))
    return pl.pallas_call(
        first_kernel,
        grid_spec=pltpu.PrefetchScalarGridSpec(
            num_scalar_prefetch=1,
            grid=(steps,),
            in_specs=[VMEM, pl.BlockSpec((cols, cols), lambda t, half: (0, 0))]
            + [pl.BlockSpec((1,) + table.shape[1:], lambda t, half: (half[0] * steps + t, 0, 0))]
            + [strip(cols)] * 2
            + [strip(1)] * 2
            + [ANY] * len(after),
            out_specs=pl.BlockSpec((tile // rows, comps, rows, cols), lambda t, half: (t, 0, 0, 0)),
            scratch_shapes=[pltpu.VMEM((length, comps * cols), BF16)],
        ),
        out_shape=pltpu.HBM((groups, comps, rows, cols), BF16),
        compiler_params=params(24),
        cost_estimate=cost(4 * comps * per_half * length * cols, 4 * per_half * length),
        name="first_pass",
    )(half, pieces, in_hbm(sort.astype(BF16)), in_hbm(table), *map(in_hbm, bases), *turns, *after)


def fstat_kernel(length, place_ref, coef_ref, z_ref, w_ref, *refs):
    fstat_ref, tail_ref, head_ref, lhs_ref = refs[-4:]
    step = pl.program_id(0)

    @pl.when(step == 0)
    def _():
        groups, cols = z_ref.shape[0], z_ref.shape[-1] // 2
        for source in range(groups):
            piece = z_ref[source].reshape(lhs_ref.shape[1], 2 * cols)
            for parity in range(2):
                at = slice(source * cols, (source + 1) * cols)
                lhs_ref[parity, :, at] = piece[:, parity * cols : (parity + 1) * cols]

    rows, width = fstat_ref.shape
    tile = w_ref.shape[-1]
    even, odd = lhs_ref[0], lhs_ref[1]
    even_real, even_imag = dot(even, w_ref[0, 0]), dot(even, w_ref[0, 1])
    odd_real, odd_imag = dot(odd, w_ref[0, 2]), dot(odd, w_ref[0, 3])
    coef_a, coef_b, coef_c = [jnp.full((1, tile), coef_ref[place_ref[SEG], at], F32) for at in range(3)]
    scale = 1.0 / ((coef_a * coef_b - coef_c * coef_c) * length)
    coef_a, coef_b, coef_c = coef_a * scale, coef_b * scale, 2.0 * coef_c * scale
    tails, heads = [], []
    for half in range(2):
        by_real = even_real - odd_real if half else even_real + odd_real
        by_imag = even_imag - odd_imag if half else even_imag + odd_imag
        part = lambda x, comp: x[comp * rows : (comp + 1) * rows]
        a_real = part(by_real, 0) - part(by_imag, 1)
        a_imag = part(by_imag, 0) + part(by_real, 1)
        b_real = part(by_real, 2) - part(by_imag, 3)
        b_imag = part(by_imag, 2) + part(by_real, 3)
        fstat = (
            coef_b * (a_real * a_real + a_imag * a_imag)
            + coef_a * (b_real * b_real + b_imag * b_imag)
            - coef_c * (a_real * b_real + a_imag * b_imag)
        )
        tails.append(fstat[rows - DMAX :])
        heads.append(fstat[:DMAX])
        at = pl.ds(pl.multiple_of(half * (width // 2) + step * tile, tile), tile)
        fstat_ref[:, at] = fstat.astype(fstat_ref.dtype)
    at = pl.ds(pl.multiple_of(step * tile, tile), tile)
    tail_ref[:, at] = jnp.concatenate(tails, axis=0).astype(tail_ref.dtype)
    head_ref[:, at] = jnp.concatenate(heads, axis=0).astype(head_ref.dtype)


def fstat_pass(z, place, table, antenna, length, kind, after=()):
    groups, comps, rows, cols = z.shape
    width = groups * cols
    rim = (2 * DMAX, width // 2)
    still = lambda shape: pl.BlockSpec(shape, lambda t: (0, 0))
    return pl.pallas_call(
        functools.partial(fstat_kernel, length),
        grid=(table.shape[0],),
        in_specs=[SMEM, SMEM, VMEM, pl.BlockSpec((1,) + table.shape[1:], lambda t: (t, 0, 0, 0))] + [ANY] * len(after),
        out_specs=[still((rows, width)), still(rim), still(rim)],
        out_shape=[jax.ShapeDtypeStruct((rows, width), kind)] + [jax.ShapeDtypeStruct(rim, kind)] * 2,
        scratch_shapes=[pltpu.VMEM((2, comps * rows, width // 2), BF16)],
        compiler_params=params(24),
        cost_estimate=cost(2 * comps * rows * width * width, 2 * width * width),
        name="fstat_pass",
    )(place, antenna, z, in_hbm(table), *after)


def gate(x, after):
    return pl.pallas_call(
        lambda *refs: None,
        in_specs=[ANY, ANY],
        out_specs=ANY,
        out_shape=pltpu.HBM(x.shape, x.dtype),
        input_output_aliases={0: 0},
        compiler_params=params(2),
        cost_estimate=cost(0, 0),
        name="gate",
    )(in_hbm(x), after)


def detect_kernel(offsets_ref, place_ref, other_ref, own_ref, *refs):
    early_refs, late_refs, out_ref, wide_refs = refs[:2], refs[2:4], refs[4], refs[5:]
    rows = own_ref.shape[0]

    @pl.when(pl.program_id(0) == 0)
    def _():
        is_first, is_last, seg = place_ref[FIRST] == 1, place_ref[LAST] == 1, place_ref[SEG]
        lowest, top = place_ref[LOWEST] == 1, place_ref[TOP] == 1
        width = own_ref.shape[1]
        unfold = lambda ref: jnp.concatenate([ref[...].astype(F32)[:DMAX], ref[...].astype(F32)[DMAX:]], axis=1)
        early, late = [unfold(ref) for ref in early_refs], [unfold(ref) for ref in late_refs]

        def widen(wide_ref, middle, lower, upper):
            lower = jnp.where(is_first, pltpu.roll(lower, 1, 1), lower)
            upper = jnp.where(is_last, pltpu.roll(upper, width - 1, 1), upper)
            for strip in range(width // LANES):
                at = slice(strip * LANES, (strip + 1) * LANES)
                wide_ref[strip, :DMAX] = lower[:, at]
                wide_ref[strip, DMAX : DMAX + rows] = middle[:, at]
                wide_ref[strip, DMAX + rows :] = upper[:, at]

        def place(own_wide, other_wide):
            lower = jnp.where(lowest, early[0], late[0]), jnp.where(lowest, late[0], early[0])
            upper = jnp.where(top, early[1], late[1]), jnp.where(top, late[1], early[1])
            widen(own_wide, own_ref[...], lower[0], upper[0])
            widen(other_wide, other_ref[...].astype(F32), lower[1], upper[1])

        @pl.when(seg == 0)
        def _():
            place(wide_refs[0], wide_refs[1])

        @pl.when(seg != 0)
        def _():
            place(wide_refs[1], wide_refs[0])

    for at in range(out_ref.shape[0]):
        template = pl.program_id(0) * out_ref.shape[0] + at
        begins = [DMAX + offsets_ref[template, s] for s in range(len(wide_refs))]
        for strip in range(own_ref.shape[1] // LANES):
            total = wide_refs[0][strip, pl.ds(begins[0], rows), :]
            for begin, wide_ref in zip(begins[1:], wide_refs[1:]):
                total = total + wide_ref[strip, pl.ds(begin, rows), :]
            out_ref[at, :, strip * LANES : (strip + 1) * LANES] = total * (1.0 / len(wide_refs))


def detect(offsets, place, other, own, early, late):
    templates = offsets.shape[0]
    rows, width = own.shape
    batch = 2 - templates % 2
    return pl.pallas_call(
        detect_kernel,
        grid=(templates // batch,),
        in_specs=[SMEM, SMEM] + [VMEM] * 6,
        out_specs=pl.BlockSpec((batch, rows, width), lambda t: (t, 0, 0)),
        out_shape=jax.ShapeDtypeStruct((templates, rows, width), F32),
        scratch_shapes=[pltpu.VMEM((width // LANES, rows + 2 * DMAX, LANES), F32)] * 2,
        compiler_params=params(8),
        cost_estimate=cost(3 * templates * rows * width, 4 * templates * rows * width),
        name="detect",
    )(offsets, place, other, own, *early, *late)


def local(series, antenna, offsets):
    devices = lax.axis_size("tm")
    index = lax.axis_index("tm")
    segs, _, rows, width = series.shape
    slow = devices * rows
    length = slow * width
    groups = devices // segs
    cols = width // groups
    seg, member = index // groups, index % groups
    place = jnp.stack([seg, member == 0, member == groups - 1, index == 0, index == devices - 1]).astype(jnp.int32)

    bins = np.arange(slow)
    tile = min(256, groups * rows)
    short = np.stack(dft_table(bins, bins, slow)).astype(BF16).reshape(2, -1, tile, slow)
    short = short.transpose(1, 0, 2, 3).reshape(-1, 2 * tile, slow)
    fast = np.arange(width // 2)
    tile = min(256, width // 2)
    long = np.stack([x.astype(BF16) for parity in range(2) for x in dft_table(2 * fast + parity, fast, width)])
    long = long.reshape(4, width // 2, -1, tile).transpose(2, 0, 1, 3)
    order = np.concatenate([np.arange(0, cols, 2), np.arange(1, cols, 2)])
    bases = dft_table(bins, order, length)
    angle = (jnp.arange(slow, dtype=jnp.int32) * (member * cols) % length).astype(F32) * (2.0 * math.pi / length)
    turns = (jnp.cos(angle)[:, None], -jnp.sin(angle)[:, None])

    halves = [[g * groups + i for i in range(groups)] for g in range(segs)]
    trade = functools.partial(lax.all_to_all, axis_name="tm", split_axis=0, concat_axis=0, tiled=True)
    pieces = trade(pack(series, groups))

    def turn(half, *after):
        return first_pass(pieces, half[None], order, short, bases, turns, groups, after)

    def move(x, by):
        return lax.ppermute(x, "tm", [(i, (i + by) % devices) for i in range(devices)])

    far = turn(1 - seg)
    near = turn(seg, far)
    far = trade(far, axis_index_groups=halves)
    near = trade(gate(near, far), axis_index_groups=halves)
    far, far_tail, far_head = fstat_pass(far, place, long, antenna, length, BF16)
    other = move(far, groups)
    own, tail, head = fstat_pass(near, place, long, antenna, length, F32, (far,))
    early = [move(far_tail, groups + 1), move(far_head, groups - 1)]
    late = [move(tail, 1), move(head, -1)]
    return detect(offsets, place, other, own, early, late)


def solution(mesh):
    return jax.shard_map(
        local,
        mesh=mesh,
        in_specs=(P("sky", None, "tm", None), P("sky", None), P("sky", None)),
        out_specs=P("sky", "tm", None),
        check_vma=False,
    )
```

```python
import functools
import math

import jax
import jax.numpy as jnp
import numpy as np
from jax import lax
from jax.experimental import pallas as pl
from jax.experimental.pallas import tpu as pltpu
from jax.sharding import PartitionSpec as P

DMAX = 8
LANES = 128
BF16 = jnp.bfloat16
F32 = jnp.float32
SEG, LOWEST, TOP, FIRST, LAST = range(5)
SMEM = pl.BlockSpec(memory_space=pltpu.SMEM)
VMEM = pl.BlockSpec(memory_space=pltpu.VMEM)
ANY = pl.BlockSpec(memory_space=pl.ANY)


def params(mebibytes):
    return pltpu.CompilerParams(vmem_limit_bytes=mebibytes * 1024 * 1024)


def cost(flops, moved):
    return pl.CostEstimate(flops=flops, bytes_accessed=moved, transcendentals=0)


def dft_table(rows, cols, length):
    products = rows[:, None].astype(np.int64) * cols[None, :] % length
    angle = products.astype(np.float32) * np.float32(2.0 * math.pi / length)
    return np.cos(angle), -np.sin(angle)


def in_hbm(x):
    return pltpu.with_memory_space_constraint(x, pltpu.HBM)


def dot(x, y):
    return jnp.dot(x, y, preferred_element_type=F32)


def pack_kernel(x_ref, out_ref):
    cols = out_ref.shape[-1]
    for piece in range(out_ref.shape[0]):
        out_ref[piece] = x_ref[0, :, :, piece * cols : (piece + 1) * cols]


def pack(series, groups):
    segs, comps, rows, width = series.shape
    shape = (segs * groups, comps, rows, width // groups)
    return pl.pallas_call(
        pack_kernel,
        grid=(segs,),
        in_specs=[pl.BlockSpec((1, comps, rows, width), lambda s: (s, 0, 0, 0))],
        out_specs=pl.BlockSpec((groups,) + shape[1:], lambda s: (s, 0, 0, 0)),
        out_shape=pltpu.HBM(shape, BF16),
        compiler_params=params(16),
        cost_estimate=cost(0, 4 * math.prod(shape)),
        name="pack",
    )(in_hbm(series))


def first_kernel(half_ref, x_ref, sort_ref, w_ref, br_ref, bi_ref, vr_ref, vi_ref, *refs):
    out_ref, sorted_ref = refs[-2:]
    tile, length = w_ref.shape[1] // 2, w_ref.shape[2]
    comps, cols = x_ref.shape[1], x_ref.shape[-1]
    spots = [slice(comp * cols, (comp + 1) * cols) for comp in range(comps)]

    @pl.when(pl.program_id(0) == 0)
    def _():
        for comp, spot in enumerate(spots):
            sorted_ref[:, spot] = dot(x_ref[:, comp].reshape(length, cols), sort_ref[...]).astype(BF16)

    shape = (out_ref.shape[0],) + out_ref.shape[2:]
    by_real, by_imag = vr_ref[...], vi_ref[...]
    t_real = br_ref[...] * by_real - bi_ref[...] * by_imag
    t_imag = br_ref[...] * by_imag + bi_ref[...] * by_real
    both = dot(w_ref[0], sorted_ref[...])
    with_real, with_imag = both[:tile], both[tile:]
    for lead in range(0, comps, 2):
        real_part = with_real[:, spots[lead]] - with_imag[:, spots[lead + 1]]
        imag_part = with_imag[:, spots[lead]] + with_real[:, spots[lead + 1]]
        out_ref[:, lead] = (real_part * t_real - imag_part * t_imag).astype(BF16).reshape(shape)
        out_ref[:, lead + 1] = (real_part * t_imag + imag_part * t_real).astype(BF16).reshape(shape)


def first_pass(pieces, half, order, table, bases, turns, groups, after):
    count, comps, rows, cols = pieces.shape
    length = count * rows
    per_half = groups * rows
    tile = table.shape[1] // 2
    steps = per_half // tile
    sort = np.zeros((cols, cols), np.float32)
    sort[order, np.arange(cols)] = 1.0
    strip = lambda width: pl.BlockSpec((tile, width), lambda t, half: (half[0] * steps + t, 0))
    return pl.pallas_call(
        first_kernel,
        grid_spec=pltpu.PrefetchScalarGridSpec(
            num_scalar_prefetch=1,
            grid=(steps,),
            in_specs=[VMEM, pl.BlockSpec((cols, cols), lambda t, half: (0, 0))]
            + [pl.BlockSpec((1,) + table.shape[1:], lambda t, half: (half[0] * steps + t, 0, 0))]
            + [strip(cols)] * 2
            + [strip(1)] * 2
            + [ANY] * len(after),
            out_specs=pl.BlockSpec((tile // rows, comps, rows, cols), lambda t, half: (t, 0, 0, 0)),
            scratch_shapes=[pltpu.VMEM((length, comps * cols), BF16)],
        ),
        out_shape=pltpu.HBM((groups, comps, rows, cols), BF16),
        compiler_params=params(24),
        cost_estimate=cost(4 * comps * per_half * length * cols, 4 * per_half * length),
        name="first_pass",
    )(half, pieces, in_hbm(sort.astype(BF16)), in_hbm(table), *map(in_hbm, bases), *turns, *after)


def fstat_kernel(length, place_ref, coef_ref, z_ref, w_ref, *refs):
    fstat_ref, tail_ref, head_ref, lhs_ref = refs[-4:]
    step = pl.program_id(0)

    @pl.when(step == 0)
    def _():
        groups, cols = z_ref.shape[0], z_ref.shape[-1] // 2
        for source in range(groups):
            piece = z_ref[source].reshape(lhs_ref.shape[1], 2 * cols)
            for parity in range(2):
                at = slice(source * cols, (source + 1) * cols)
                lhs_ref[parity, :, at] = piece[:, parity * cols : (parity + 1) * cols]

    rows, width = fstat_ref.shape
    tile = w_ref.shape[-1]
    even, odd = lhs_ref[0], lhs_ref[1]
    even_real, even_imag = dot(even, w_ref[0, 0]), dot(even, w_ref[0, 1])
    odd_real, odd_imag = dot(odd, w_ref[0, 2]), dot(odd, w_ref[0, 3])
    coef_a, coef_b, coef_c = [jnp.full((1, tile), coef_ref[place_ref[SEG], at], F32) for at in range(3)]
    scale = 1.0 / ((coef_a * coef_b - coef_c * coef_c) * length)
    coef_a, coef_b, coef_c = coef_a * scale, coef_b * scale, 2.0 * coef_c * scale
    tails, heads = [], []
    for half in range(2):
        by_real = even_real - odd_real if half else even_real + odd_real
        by_imag = even_imag - odd_imag if half else even_imag + odd_imag
        part = lambda x, comp: x[comp * rows : (comp + 1) * rows]
        a_real = part(by_real, 0) - part(by_imag, 1)
        a_imag = part(by_imag, 0) + part(by_real, 1)
        b_real = part(by_real, 2) - part(by_imag, 3)
        b_imag = part(by_imag, 2) + part(by_real, 3)
        fstat = (
            coef_b * (a_real * a_real + a_imag * a_imag)
            + coef_a * (b_real * b_real + b_imag * b_imag)
            - coef_c * (a_real * b_real + a_imag * b_imag)
        )
        tails.append(fstat[rows - DMAX :])
        heads.append(fstat[:DMAX])
        at = pl.ds(pl.multiple_of(half * (width // 2) + step * tile, tile), tile)
        fstat_ref[:, at] = fstat.astype(fstat_ref.dtype)
    at = pl.ds(pl.multiple_of(step * tile, tile), tile)
    tail_ref[:, at] = jnp.concatenate(tails, axis=0).astype(tail_ref.dtype)
    head_ref[:, at] = jnp.concatenate(heads, axis=0).astype(head_ref.dtype)


def fstat_pass(z, place, table, antenna, length, kind, after=()):
    groups, comps, rows, cols = z.shape
    width = groups * cols
    rim = (2 * DMAX, width // 2)
    still = lambda shape: pl.BlockSpec(shape, lambda t: (0, 0))
    return pl.pallas_call(
        functools.partial(fstat_kernel, length),
        grid=(table.shape[0],),
        in_specs=[SMEM, SMEM, VMEM, pl.BlockSpec((1,) + table.shape[1:], lambda t: (t, 0, 0, 0))] + [ANY] * len(after),
        out_specs=[still((rows, width)), still(rim), still(rim)],
        out_shape=[jax.ShapeDtypeStruct((rows, width), kind)] + [jax.ShapeDtypeStruct(rim, kind)] * 2,
        scratch_shapes=[pltpu.VMEM((2, comps * rows, width // 2), BF16)],
        compiler_params=params(24),
        cost_estimate=cost(2 * comps * rows * width * width, 2 * width * width),
        name="fstat_pass",
    )(place, antenna, z, in_hbm(table), *after)


def gate(x, *after):
    return pl.pallas_call(
        lambda *refs: None,
        in_specs=[ANY] * (1 + len(after)),
        out_specs=ANY,
        out_shape=pltpu.HBM(x.shape, x.dtype),
        input_output_aliases={0: 0},
        compiler_params=params(2),
        cost_estimate=cost(0, 0),
        name="gate",
    )(in_hbm(x), *after)


def detect_kernel(offsets_ref, place_ref, other_ref, own_ref, *refs):
    early_refs, late_refs, out_ref, wide_refs = refs[:2], refs[2:4], refs[4], refs[5:]
    rows = own_ref.shape[0]

    @pl.when(pl.program_id(0) == 0)
    def _():
        is_first, is_last, seg = place_ref[FIRST] == 1, place_ref[LAST] == 1, place_ref[SEG]
        lowest, top = place_ref[LOWEST] == 1, place_ref[TOP] == 1
        width = own_ref.shape[1]
        unfold = lambda ref: jnp.concatenate([ref[...].astype(F32)[:DMAX], ref[...].astype(F32)[DMAX:]], axis=1)
        early, late = [unfold(ref) for ref in early_refs], [unfold(ref) for ref in late_refs]

        def widen(wide_ref, middle, lower, upper):
            lower = jnp.where(is_first, pltpu.roll(lower, 1, 1), lower)
            upper = jnp.where(is_last, pltpu.roll(upper, width - 1, 1), upper)
            for strip in range(width // LANES):
                at = slice(strip * LANES, (strip + 1) * LANES)
                wide_ref[strip, :DMAX] = lower[:, at]
                wide_ref[strip, DMAX : DMAX + rows] = middle[:, at]
                wide_ref[strip, DMAX + rows :] = upper[:, at]

        def place(own_wide, other_wide):
            lower = jnp.where(lowest, early[0], late[0]), jnp.where(lowest, late[0], early[0])
            upper = jnp.where(top, early[1], late[1]), jnp.where(top, late[1], early[1])
            widen(own_wide, own_ref[...], lower[0], upper[0])
            widen(other_wide, other_ref[...].astype(F32), lower[1], upper[1])

        @pl.when(seg == 0)
        def _():
            place(wide_refs[0], wide_refs[1])

        @pl.when(seg != 0)
        def _():
            place(wide_refs[1], wide_refs[0])

    for at in range(out_ref.shape[0]):
        template = pl.program_id(0) * out_ref.shape[0] + at
        begins = [DMAX + offsets_ref[template, s] for s in range(len(wide_refs))]
        for strip in range(own_ref.shape[1] // LANES):
            total = wide_refs[0][strip, pl.ds(begins[0], rows), :]
            for begin, wide_ref in zip(begins[1:], wide_refs[1:]):
                total = total + wide_ref[strip, pl.ds(begin, rows), :]
            out_ref[at, :, strip * LANES : (strip + 1) * LANES] = total * (1.0 / len(wide_refs))


def detect(offsets, place, other, own, early, late):
    templates = offsets.shape[0]
    rows, width = own.shape
    batch = 2 - templates % 2
    return pl.pallas_call(
        detect_kernel,
        grid=(templates // batch,),
        in_specs=[SMEM, SMEM] + [VMEM] * 6,
        out_specs=pl.BlockSpec((batch, rows, width), lambda t: (t, 0, 0)),
        out_shape=jax.ShapeDtypeStruct((templates, rows, width), F32),
        scratch_shapes=[pltpu.VMEM((width // LANES, rows + 2 * DMAX, LANES), F32)] * 2,
        compiler_params=params(8),
        cost_estimate=cost(3 * templates * rows * width, 4 * templates * rows * width),
        name="detect",
    )(offsets, place, other, own, *early, *late)


def local(series, antenna, offsets):
    devices = lax.axis_size("tm")
    index = lax.axis_index("tm")
    segs, _, rows, width = series.shape
    slow = devices * rows
    length = slow * width
    groups = devices // segs
    cols = width // groups
    seg, member = index // groups, index % groups
    place = jnp.stack([seg, member == 0, member == groups - 1, index == 0, index == devices - 1]).astype(jnp.int32)

    bins = np.arange(slow)
    tile = min(256, groups * rows)
    short = np.stack(dft_table(bins, bins, slow)).astype(BF16).reshape(2, -1, tile, slow)
    short = short.transpose(1, 0, 2, 3).reshape(-1, 2 * tile, slow)
    fast = np.arange(width // 2)
    tile = min(256, width // 2)
    long = np.stack([x.astype(BF16) for parity in range(2) for x in dft_table(2 * fast + parity, fast, width)])
    long = long.reshape(4, width // 2, -1, tile).transpose(2, 0, 1, 3)
    order = np.concatenate([np.arange(0, cols, 2), np.arange(1, cols, 2)])
    bases = dft_table(bins, order, length)
    angle = (jnp.arange(slow, dtype=jnp.int32) * (member * cols) % length).astype(F32) * (2.0 * math.pi / length)
    turns = (jnp.cos(angle)[:, None], -jnp.sin(angle)[:, None])

    halves = [[g * groups + i for i in range(groups)] for g in range(segs)]
    trade = functools.partial(lax.all_to_all, axis_name="tm", split_axis=0, concat_axis=0, tiled=True)
    pieces = trade(pack(series, groups))

    def turn(half, *after):
        return first_pass(pieces, half[None], order, short, bases, turns, groups, after)

    def move(x, by):
        return lax.ppermute(x, "tm", [(i, (i + by) % devices) for i in range(devices)])

    far = turn(1 - seg)
    near = turn(seg, far)
    far = trade(far, axis_index_groups=halves)
    near = trade(gate(near, far), axis_index_groups=halves)
    far, far_tail, far_head = fstat_pass(far, place, long, antenna, length, BF16)
    early = [move(far_tail, groups + 1), move(far_head, groups - 1)]
    far = gate(far, *early)
    other = move(far, groups)
    own, tail, head = fstat_pass(near, place, long, antenna, length, F32, (far,))
    late = [move(tail, 1), move(head, -1)]
    return detect(offsets, place, other, own, early, late)


def solution(mesh):
    return jax.shard_map(
        local,
        mesh=mesh,
        in_specs=(P("sky", None, "tm", None), P("sky", None), P("sky", None)),
        out_specs=P("sky", "tm", None),
        check_vma=False,
    )
```

```python
import functools
import math

import jax
import jax.numpy as jnp
import numpy as np
from jax import lax
from jax.experimental import pallas as pl
from jax.experimental.pallas import tpu as pltpu
from jax.sharding import PartitionSpec as P

DMAX = 8
LANES = 128
BF16 = jnp.bfloat16
F32 = jnp.float32
SEG, LOWEST, TOP, FIRST, LAST = range(5)
SMEM = pl.BlockSpec(memory_space=pltpu.SMEM)
VMEM = pl.BlockSpec(memory_space=pltpu.VMEM)
ANY = pl.BlockSpec(memory_space=pl.ANY)


def params(mebibytes):
    return pltpu.CompilerParams(vmem_limit_bytes=mebibytes * 1024 * 1024)


def cost(flops, moved):
    return pl.CostEstimate(flops=flops, bytes_accessed=moved, transcendentals=0)


def dft_table(rows, cols, length):
    products = rows[:, None].astype(np.int64) * cols[None, :] % length
    angle = products.astype(np.float32) * np.float32(2.0 * math.pi / length)
    return np.cos(angle), -np.sin(angle)


def in_hbm(x):
    return pltpu.with_memory_space_constraint(x, pltpu.HBM)


def dot(x, y):
    return jnp.dot(x, y, preferred_element_type=F32)


def pack_kernel(x_ref, out_ref):
    cols = out_ref.shape[-1]
    for piece in range(out_ref.shape[0]):
        out_ref[piece] = x_ref[0, :, :, piece * cols : (piece + 1) * cols]


def pack(series, groups):
    segs, comps, rows, width = series.shape
    shape = (segs * groups, comps, rows, width // groups)
    return pl.pallas_call(
        pack_kernel,
        grid=(segs,),
        in_specs=[pl.BlockSpec((1, comps, rows, width), lambda s: (s, 0, 0, 0))],
        out_specs=pl.BlockSpec((groups,) + shape[1:], lambda s: (s, 0, 0, 0)),
        out_shape=pltpu.HBM(shape, BF16),
        compiler_params=params(16),
        cost_estimate=cost(0, 4 * math.prod(shape)),
        name="pack",
    )(in_hbm(series))


def first_kernel(half_ref, x_ref, sort_ref, w_ref, br_ref, bi_ref, vr_ref, vi_ref, *refs):
    out_ref, sorted_ref = refs[-2:]
    tile, length = w_ref.shape[1] // 2, w_ref.shape[2]
    comps, cols = x_ref.shape[1], x_ref.shape[-1]
    spots = [slice(comp * cols, (comp + 1) * cols) for comp in range(comps)]

    @pl.when(pl.program_id(0) == 0)
    def _():
        for comp, spot in enumerate(spots):
            sorted_ref[:, spot] = dot(x_ref[:, comp].reshape(length, cols), sort_ref[...]).astype(BF16)

    shape = (out_ref.shape[0],) + out_ref.shape[2:]
    by_real, by_imag = vr_ref[...], vi_ref[...]
    t_real = br_ref[...] * by_real - bi_ref[...] * by_imag
    t_imag = br_ref[...] * by_imag + bi_ref[...] * by_real
    both = dot(w_ref[0], sorted_ref[...])
    with_real, with_imag = both[:tile], both[tile:]
    for lead in range(0, comps, 2):
        real_part = with_real[:, spots[lead]] - with_imag[:, spots[lead + 1]]
        imag_part = with_imag[:, spots[lead]] + with_real[:, spots[lead + 1]]
        out_ref[:, lead] = (real_part * t_real - imag_part * t_imag).astype(BF16).reshape(shape)
        out_ref[:, lead + 1] = (real_part * t_imag + imag_part * t_real).astype(BF16).reshape(shape)


def first_pass(pieces, half, order, table, bases, turns, groups, after):
    count, comps, rows, cols = pieces.shape
    length = count * rows
    per_half = groups * rows
    tile = table.shape[1] // 2
    steps = per_half // tile
    sort = np.zeros((cols, cols), np.float32)
    sort[order, np.arange(cols)] = 1.0
    strip = lambda width: pl.BlockSpec((tile, width), lambda t, half: (half[0] * steps + t, 0))
    return pl.pallas_call(
        first_kernel,
        grid_spec=pltpu.PrefetchScalarGridSpec(
            num_scalar_prefetch=1,
            grid=(steps,),
            in_specs=[VMEM, pl.BlockSpec((cols, cols), lambda t, half: (0, 0))]
            + [pl.BlockSpec((1,) + table.shape[1:], lambda t, half: (half[0] * steps + t, 0, 0))]
            + [strip(cols)] * 2
            + [strip(1)] * 2
            + [ANY] * len(after),
            out_specs=pl.BlockSpec((tile // rows, comps, rows, cols), lambda t, half: (t, 0, 0, 0)),
            scratch_shapes=[pltpu.VMEM((length, comps * cols), BF16)],
        ),
        out_shape=pltpu.HBM((groups, comps, rows, cols), BF16),
        compiler_params=params(24),
        cost_estimate=cost(4 * comps * per_half * length * cols, 4 * per_half * length),
        name="first_pass",
    )(half, pieces, in_hbm(sort.astype(BF16)), in_hbm(table), *map(in_hbm, bases), *turns, *after)


def fstat_kernel(length, place_ref, coef_ref, z_ref, w_ref, *refs):
    fstat_ref, tail_ref, head_ref, lhs_ref = refs[-4:]
    step = pl.program_id(0)

    @pl.when(step == 0)
    def _():
        groups, cols = z_ref.shape[0], z_ref.shape[-1] // 4
        for source in range(groups):
            piece = z_ref[source].reshape(lhs_ref.shape[1], 4 * cols)
            for kind in range(4):
                at = slice(source * cols, (source + 1) * cols)
                lhs_ref[kind, :, at] = piece[:, kind * cols : (kind + 1) * cols]

    rows, width = fstat_ref.shape
    tile = w_ref.shape[-1]
    sums = []
    for kind in range(4):
        by_real, by_imag = dot(lhs_ref[kind], w_ref[0, kind, 0]), dot(lhs_ref[kind], w_ref[0, kind, 1])
        part = lambda x, comp: x[comp * rows : (comp + 1) * rows]
        pairs = [(part(by_real, c) - part(by_imag, c + 1), part(by_imag, c) + part(by_real, c + 1)) for c in (0, 2)]
        sums.append(pairs[0] + pairs[1])
    plus = [[x + y for x, y in zip(sums[k], sums[k + 2])] for k in range(2)]
    minus = [[x - y for x, y in zip(sums[k], sums[k + 2])] for k in range(2)]
    turned = [minus[1][1], -minus[1][0], minus[1][3], -minus[1][2]]
    coef_a, coef_b, coef_c = [jnp.full((1, tile), coef_ref[place_ref[SEG], at], F32) for at in range(3)]
    scale = 1.0 / ((coef_a * coef_b - coef_c * coef_c) * length)
    coef_a, coef_b, coef_c = coef_a * scale, coef_b * scale, 2.0 * coef_c * scale
    quarter = width // 4
    for odd, (base, swing) in enumerate(((plus[0], plus[1]), (minus[0], turned))):
        tails, heads = [], []
        for half in range(2):
            a_real, a_imag, b_real, b_imag = [x - y if half else x + y for x, y in zip(base, swing)]
            fstat = (
                coef_b * (a_real * a_real + a_imag * a_imag)
                + coef_a * (b_real * b_real + b_imag * b_imag)
                - coef_c * (a_real * b_real + a_imag * b_imag)
            )
            tails.append(fstat[rows - DMAX :])
            heads.append(fstat[:DMAX])
            at = pl.ds(pl.multiple_of((2 * half + odd) * quarter + step * tile, tile), tile)
            fstat_ref[:, at] = fstat.astype(fstat_ref.dtype)
        at = pl.ds(pl.multiple_of(odd * quarter + step * tile, tile), tile)
        tail_ref[:, at] = jnp.concatenate(tails, axis=0).astype(tail_ref.dtype)
        head_ref[:, at] = jnp.concatenate(heads, axis=0).astype(head_ref.dtype)


def fstat_pass(z, place, table, antenna, length, kind, after=()):
    groups, comps, rows, cols = z.shape
    width = groups * cols
    rim = (2 * DMAX, width // 2)
    still = lambda shape: pl.BlockSpec(shape, lambda t: (0, 0))
    return pl.pallas_call(
        functools.partial(fstat_kernel, length),
        grid=(table.shape[0],),
        in_specs=[SMEM, SMEM, VMEM, pl.BlockSpec((1,) + table.shape[1:], lambda t: (t, 0, 0, 0, 0))] + [ANY] * len(after),
        out_specs=[still((rows, width)), still(rim), still(rim)],
        out_shape=[jax.ShapeDtypeStruct((rows, width), kind)] + [jax.ShapeDtypeStruct(rim, kind)] * 2,
        scratch_shapes=[pltpu.VMEM((4, comps * rows, width // 4), BF16)],
        compiler_params=params(24),
        cost_estimate=cost(comps * rows * width * width, width * width),
        name="fstat_pass",
    )(place, antenna, z, in_hbm(table), *after)


def gate(x, *after):
    return pl.pallas_call(
        lambda *refs: None,
        in_specs=[ANY] * (1 + len(after)),
        out_specs=ANY,
        out_shape=jax.ShapeDtypeStruct(x.shape, x.dtype),
        input_output_aliases={0: 0},
        compiler_params=params(2),
        cost_estimate=cost(0, 0),
        name="gate",
    )(x, *after)


def detect_kernel(offsets_ref, place_ref, other_ref, own_ref, *refs):
    early_refs, late_refs, out_ref, wide_refs = refs[:2], refs[2:4], refs[4], refs[5:]
    rows = own_ref.shape[0]

    @pl.when(pl.program_id(0) == 0)
    def _():
        is_first, is_last, seg = place_ref[FIRST] == 1, place_ref[LAST] == 1, place_ref[SEG]
        lowest, top = place_ref[LOWEST] == 1, place_ref[TOP] == 1
        width = own_ref.shape[1]
        unfold = lambda ref: jnp.concatenate([ref[...].astype(F32)[:DMAX], ref[...].astype(F32)[DMAX:]], axis=1)
        early, late = [unfold(ref) for ref in early_refs], [unfold(ref) for ref in late_refs]

        def widen(wide_ref, middle, lower, upper):
            lower = jnp.where(is_first, pltpu.roll(lower, 1, 1), lower)
            upper = jnp.where(is_last, pltpu.roll(upper, width - 1, 1), upper)
            for strip in range(width // LANES):
                at = slice(strip * LANES, (strip + 1) * LANES)
                wide_ref[strip, :DMAX] = lower[:, at]
                wide_ref[strip, DMAX : DMAX + rows] = middle[:, at]
                wide_ref[strip, DMAX + rows :] = upper[:, at]

        def place(own_wide, other_wide):
            lower = jnp.where(lowest, early[0], late[0]), jnp.where(lowest, late[0], early[0])
            upper = jnp.where(top, early[1], late[1]), jnp.where(top, late[1], early[1])
            widen(own_wide, own_ref[...], lower[0], upper[0])
            widen(other_wide, other_ref[...].astype(F32), lower[1], upper[1])

        @pl.when(seg == 0)
        def _():
            place(wide_refs[0], wide_refs[1])

        @pl.when(seg != 0)
        def _():
            place(wide_refs[1], wide_refs[0])

    for at in range(out_ref.shape[0]):
        template = pl.program_id(0) * out_ref.shape[0] + at
        begins = [DMAX + offsets_ref[template, s] for s in range(len(wide_refs))]
        for strip in range(own_ref.shape[1] // LANES):
            total = wide_refs[0][strip, pl.ds(begins[0], rows), :]
            for begin, wide_ref in zip(begins[1:], wide_refs[1:]):
                total = total + wide_ref[strip, pl.ds(begin, rows), :]
            out_ref[at, :, strip * LANES : (strip + 1) * LANES] = total * (1.0 / len(wide_refs))


def detect(offsets, place, other, own, early, late):
    templates = offsets.shape[0]
    rows, width = own.shape
    batch = 2 - templates % 2
    return pl.pallas_call(
        detect_kernel,
        grid=(templates // batch,),
        in_specs=[SMEM, SMEM] + [VMEM] * 6,
        out_specs=pl.BlockSpec((batch, rows, width), lambda t: (t, 0, 0)),
        out_shape=jax.ShapeDtypeStruct((templates, rows, width), F32),
        scratch_shapes=[pltpu.VMEM((width // LANES, rows + 2 * DMAX, LANES), F32)] * 2,
        compiler_params=params(8),
        cost_estimate=cost(3 * templates * rows * width, 4 * templates * rows * width),
        name="detect",
    )(offsets, place, other, own, *early, *late)


def local(series, antenna, offsets):
    devices = lax.axis_size("tm")
    index = lax.axis_index("tm")
    segs, _, rows, width = series.shape
    slow = devices * rows
    length = slow * width
    groups = devices // segs
    cols = width // groups
    seg, member = index // groups, index % groups
    place = jnp.stack([seg, member == 0, member == groups - 1, index == 0, index == devices - 1]).astype(jnp.int32)

    bins = np.arange(slow)
    tile = min(256, groups * rows)
    short = np.stack(dft_table(bins, bins, slow)).astype(BF16).reshape(2, -1, tile, slow)
    short = short.transpose(1, 0, 2, 3).reshape(-1, 2 * tile, slow)
    fast = np.arange(width // 4)
    tile = min(256, width // 4)
    long = np.stack([np.stack(dft_table(4 * fast + kind, fast, width)) for kind in range(4)]).astype(BF16)
    long = long.reshape(4, 2, width // 4, -1, tile).transpose(3, 0, 1, 2, 4)
    order = np.concatenate([np.arange(kind, cols, 4) for kind in range(4)])
    bases = dft_table(bins, order, length)
    angle = (jnp.arange(slow, dtype=jnp.int32) * (member * cols) % length).astype(F32) * (2.0 * math.pi / length)
    turns = (jnp.cos(angle)[:, None], -jnp.sin(angle)[:, None])

    halves = [[g * groups + i for i in range(groups)] for g in range(segs)]
    trade = functools.partial(lax.all_to_all, axis_name="tm", split_axis=0, concat_axis=0, tiled=True)
    pieces = trade(pack(series, groups))

    def turn(half, *after):
        return first_pass(pieces, half[None], order, short, bases, turns, groups, after)

    def move(x, by):
        return lax.ppermute(x, "tm", [(i, (i + by) % devices) for i in range(devices)])

    far = turn(1 - seg)
    near = turn(seg, far)
    far = trade(far, axis_index_groups=halves)
    near = trade(gate(near, far), axis_index_groups=halves)
    far, far_tail, far_head = fstat_pass(far, place, long, antenna, length, BF16)
    early = [move(far_tail, groups + 1), move(far_head, groups - 1)]
    far = gate(far, *early)
    other = move(far, groups)
    own, tail, head = fstat_pass(near, place, long, antenna, length, F32, (far,))
    late = [move(tail, 1), move(head, -1)]
    return detect(offsets, place, other, own, early, late)


def solution(mesh):
    return jax.shard_map(
        local,
        mesh=mesh,
        in_specs=(P("sky", None, "tm", None), P("sky", None), P("sky", None)),
        out_specs=P("sky", "tm", None),
        check_vma=False,
    )
```

```python
import functools
import math

import jax
import jax.numpy as jnp
import numpy as np
from jax import lax
from jax.experimental import pallas as pl
from jax.experimental.pallas import tpu as pltpu
from jax.sharding import PartitionSpec as P

DMAX = 8
LANES = 128
BF16 = jnp.bfloat16
F32 = jnp.float32
SEG, LOWEST, TOP, FIRST, LAST = range(5)
SMEM = pl.BlockSpec(memory_space=pltpu.SMEM)
VMEM = pl.BlockSpec(memory_space=pltpu.VMEM)
ANY = pl.BlockSpec(memory_space=pl.ANY)


def params(mebibytes):
    return pltpu.CompilerParams(vmem_limit_bytes=mebibytes * 1024 * 1024)


def cost(flops, moved):
    return pl.CostEstimate(flops=flops, bytes_accessed=moved, transcendentals=0)


def dft_table(rows, cols, length):
    products = rows[:, None].astype(np.int64) * cols[None, :] % length
    angle = products.astype(np.float32) * np.float32(2.0 * math.pi / length)
    return np.cos(angle), -np.sin(angle)


def in_hbm(x):
    return pltpu.with_memory_space_constraint(x, pltpu.HBM)


def dot(x, y):
    return jnp.dot(x, y, preferred_element_type=F32)


def pack_kernel(x_ref, out_ref):
    cols = out_ref.shape[-1]
    for piece in range(out_ref.shape[0]):
        out_ref[piece] = x_ref[0, :, :, piece * cols : (piece + 1) * cols]


def pack(series, groups):
    segs, comps, rows, width = series.shape
    shape = (segs * groups, comps, rows, width // groups)
    return pl.pallas_call(
        pack_kernel,
        grid=(segs,),
        in_specs=[pl.BlockSpec((1, comps, rows, width), lambda s: (s, 0, 0, 0))],
        out_specs=pl.BlockSpec((groups,) + shape[1:], lambda s: (s, 0, 0, 0)),
        out_shape=pltpu.HBM(shape, BF16),
        compiler_params=params(16),
        cost_estimate=cost(0, 4 * math.prod(shape)),
        name="pack",
    )(in_hbm(series))


def first_kernel(half_ref, x_ref, sort_ref, w_ref, br_ref, bi_ref, vr_ref, vi_ref, *refs):
    out_ref, sorted_ref = refs[-2:]
    tile, length = w_ref.shape[1] // 2, w_ref.shape[2]
    comps, cols = x_ref.shape[1], x_ref.shape[-1]
    spots = [slice(comp * cols, (comp + 1) * cols) for comp in range(comps)]

    @pl.when(pl.program_id(0) == 0)
    def _():
        for comp, spot in enumerate(spots):
            sorted_ref[:, spot] = dot(x_ref[:, comp].reshape(length, cols), sort_ref[...]).astype(BF16)

    shape = (out_ref.shape[0],) + out_ref.shape[2:]
    by_real, by_imag = vr_ref[...], vi_ref[...]
    t_real = br_ref[...] * by_real - bi_ref[...] * by_imag
    t_imag = br_ref[...] * by_imag + bi_ref[...] * by_real
    both = dot(w_ref[0], sorted_ref[...])
    with_real, with_imag = both[:tile], both[tile:]
    for lead in range(0, comps, 2):
        real_part = with_real[:, spots[lead]] - with_imag[:, spots[lead + 1]]
        imag_part = with_imag[:, spots[lead]] + with_real[:, spots[lead + 1]]
        out_ref[:, lead] = (real_part * t_real - imag_part * t_imag).astype(BF16).reshape(shape)
        out_ref[:, lead + 1] = (real_part * t_imag + imag_part * t_real).astype(BF16).reshape(shape)


def first_pass(pieces, half, order, table, bases, turns, groups, after):
    count, comps, rows, cols = pieces.shape
    length = count * rows
    per_half = groups * rows
    tile = table.shape[1] // 2
    steps = per_half // tile
    sort = np.zeros((cols, cols), np.float32)
    sort[order, np.arange(cols)] = 1.0
    strip = lambda width: pl.BlockSpec((tile, width), lambda t, half: (half[0] * steps + t, 0))
    return pl.pallas_call(
        first_kernel,
        grid_spec=pltpu.PrefetchScalarGridSpec(
            num_scalar_prefetch=1,
            grid=(steps,),
            in_specs=[VMEM, pl.BlockSpec((cols, cols), lambda t, half: (0, 0))]
            + [pl.BlockSpec((1,) + table.shape[1:], lambda t, half: (half[0] * steps + t, 0, 0))]
            + [strip(cols)] * 2
            + [strip(1)] * 2
            + [ANY] * len(after),
            out_specs=pl.BlockSpec((tile // rows, comps, rows, cols), lambda t, half: (t, 0, 0, 0)),
            scratch_shapes=[pltpu.VMEM((length, comps * cols), BF16)],
        ),
        out_shape=pltpu.HBM((groups, comps, rows, cols), BF16),
        compiler_params=params(24),
        cost_estimate=cost(4 * comps * per_half * length * cols, 4 * per_half * length),
        name="first_pass",
    )(half, pieces, in_hbm(sort.astype(BF16)), in_hbm(table), *map(in_hbm, bases), *turns, *after)


def fstat_kernel(length, place_ref, coef_ref, z_ref, w_ref, *refs):
    fstat_ref, tail_ref, head_ref, lhs_ref = refs[-4:]
    step = pl.program_id(0)

    @pl.when(step == 0)
    def _():
        groups, cols = z_ref.shape[0], z_ref.shape[-1] // 4
        for source in range(groups):
            piece = z_ref[source].reshape(lhs_ref.shape[1], 4 * cols)
            for kind in range(4):
                at = slice(source * cols, (source + 1) * cols)
                lhs_ref[kind, :, at] = piece[:, kind * cols : (kind + 1) * cols]

    rows, width = fstat_ref.shape
    tile = w_ref.shape[-1]
    sums = []
    for kind in range(4):
        by_real, by_imag = dot(lhs_ref[kind], w_ref[0, kind, 0]), dot(lhs_ref[kind], w_ref[0, kind, 1])
        part = lambda x, comp: x[comp * rows : (comp + 1) * rows]
        pairs = [(part(by_real, c) - part(by_imag, c + 1), part(by_imag, c) + part(by_real, c + 1)) for c in (0, 2)]
        sums.append(pairs[0] + pairs[1])
    plus = [[x + y for x, y in zip(sums[k], sums[k + 2])] for k in range(2)]
    minus = [[x - y for x, y in zip(sums[k], sums[k + 2])] for k in range(2)]
    turned = [minus[1][1], -minus[1][0], minus[1][3], -minus[1][2]]
    coef_a, coef_b, coef_c = [jnp.full((1, tile), coef_ref[place_ref[SEG], at], F32) for at in range(3)]
    scale = 1.0 / ((coef_a * coef_b - coef_c * coef_c) * length)
    coef_a, coef_b, coef_c = coef_a * scale, coef_b * scale, 2.0 * coef_c * scale
    quarter = width // 4
    for odd, (base, swing) in enumerate(((plus[0], plus[1]), (minus[0], turned))):
        tails, heads = [], []
        for half in range(2):
            a_real, a_imag, b_real, b_imag = [x - y if half else x + y for x, y in zip(base, swing)]
            fstat = (
                coef_b * (a_real * a_real + a_imag * a_imag)
                + coef_a * (b_real * b_real + b_imag * b_imag)
                - coef_c * (a_real * b_real + a_imag * b_imag)
            )
            tails.append(fstat[rows - DMAX :])
            heads.append(fstat[:DMAX])
            at = pl.ds(pl.multiple_of((2 * half + odd) * quarter + step * tile, tile), tile)
            fstat_ref[:, at] = fstat.astype(fstat_ref.dtype)
        at = pl.ds(pl.multiple_of(odd * quarter + step * tile, tile), tile)
        tail_ref[:, at] = jnp.concatenate(tails, axis=0).astype(tail_ref.dtype)
        head_ref[:, at] = jnp.concatenate(heads, axis=0).astype(head_ref.dtype)


def fstat_pass(z, place, table, antenna, length, kind, after=()):
    groups, comps, rows, cols = z.shape
    width = groups * cols
    rim = (2 * DMAX, width // 2)
    still = lambda shape: pl.BlockSpec(shape, lambda t: (0, 0))
    return pl.pallas_call(
        functools.partial(fstat_kernel, length),
        grid=(table.shape[0],),
        in_specs=[SMEM, SMEM, VMEM, pl.BlockSpec((1,) + table.shape[1:], lambda t: (t, 0, 0, 0, 0))] + [ANY] * len(after),
        out_specs=[still((rows, width)), still(rim), still(rim)],
        out_shape=[jax.ShapeDtypeStruct((rows, width), kind)] + [jax.ShapeDtypeStruct(rim, kind)] * 2,
        scratch_shapes=[pltpu.VMEM((4, comps * rows, width // 4), BF16)],
        compiler_params=params(24),
        cost_estimate=cost(comps * rows * width * width, width * width),
        name="fstat_pass",
    )(place, antenna, z, in_hbm(table), *after)


def gate(x, *after, make=jax.ShapeDtypeStruct):
    return pl.pallas_call(
        lambda *refs: None,
        in_specs=[ANY] * (1 + len(after)),
        out_specs=ANY,
        out_shape=make(x.shape, x.dtype),
        input_output_aliases={0: 0},
        compiler_params=params(2),
        cost_estimate=cost(0, 0),
        name="gate",
    )(x, *after)


def detect_kernel(offsets_ref, place_ref, other_ref, own_ref, *refs):
    early_refs, late_refs, out_ref, wide_refs = refs[:2], refs[2:4], refs[4], refs[5:]
    rows = own_ref.shape[0]

    @pl.when(pl.program_id(0) == 0)
    def _():
        is_first, is_last, seg = place_ref[FIRST] == 1, place_ref[LAST] == 1, place_ref[SEG]
        lowest, top = place_ref[LOWEST] == 1, place_ref[TOP] == 1
        width = own_ref.shape[1]
        unfold = lambda ref: jnp.concatenate([ref[...].astype(F32)[:DMAX], ref[...].astype(F32)[DMAX:]], axis=1)
        early, late = [unfold(ref) for ref in early_refs], [unfold(ref) for ref in late_refs]

        def widen(wide_ref, middle, lower, upper):
            lower = jnp.where(is_first, pltpu.roll(lower, 1, 1), lower)
            upper = jnp.where(is_last, pltpu.roll(upper, width - 1, 1), upper)
            for strip in range(width // LANES):
                at = slice(strip * LANES, (strip + 1) * LANES)
                wide_ref[strip, :DMAX] = lower[:, at]
                wide_ref[strip, DMAX : DMAX + rows] = middle[:, at]
                wide_ref[strip, DMAX + rows :] = upper[:, at]

        def place(own_wide, other_wide):
            lower = jnp.where(lowest, early[0], late[0]), jnp.where(lowest, late[0], early[0])
            upper = jnp.where(top, early[1], late[1]), jnp.where(top, late[1], early[1])
            widen(own_wide, own_ref[...], lower[0], upper[0])
            widen(other_wide, other_ref[...].astype(F32), lower[1], upper[1])

        @pl.when(seg == 0)
        def _():
            place(wide_refs[0], wide_refs[1])

        @pl.when(seg != 0)
        def _():
            place(wide_refs[1], wide_refs[0])

    for at in range(out_ref.shape[0]):
        template = pl.program_id(0) * out_ref.shape[0] + at
        begins = [DMAX + offsets_ref[template, s] for s in range(len(wide_refs))]
        for strip in range(own_ref.shape[1] // LANES):
            total = wide_refs[0][strip, pl.ds(begins[0], rows), :]
            for begin, wide_ref in zip(begins[1:], wide_refs[1:]):
                total = total + wide_ref[strip, pl.ds(begin, rows), :]
            out_ref[at, :, strip * LANES : (strip + 1) * LANES] = total * (1.0 / len(wide_refs))


def detect(offsets, place, other, own, early, late):
    templates = offsets.shape[0]
    rows, width = own.shape
    batch = 2 - templates % 2
    return pl.pallas_call(
        detect_kernel,
        grid=(templates // batch,),
        in_specs=[SMEM, SMEM] + [VMEM] * 6,
        out_specs=pl.BlockSpec((batch, rows, width), lambda t: (t, 0, 0)),
        out_shape=jax.ShapeDtypeStruct((templates, rows, width), F32),
        scratch_shapes=[pltpu.VMEM((width // LANES, rows + 2 * DMAX, LANES), F32)] * 2,
        compiler_params=params(8),
        cost_estimate=cost(3 * templates * rows * width, 4 * templates * rows * width),
        name="detect",
    )(offsets, place, other, own, *early, *late)


def local(series, antenna, offsets):
    devices = lax.axis_size("tm")
    index = lax.axis_index("tm")
    segs, _, rows, width = series.shape
    slow = devices * rows
    length = slow * width
    groups = devices // segs
    cols = width // groups
    seg, member = index // groups, index % groups
    place = jnp.stack([seg, member == 0, member == groups - 1, index == 0, index == devices - 1]).astype(jnp.int32)

    bins = np.arange(slow)
    tile = min(256, groups * rows)
    short = np.stack(dft_table(bins, bins, slow)).astype(BF16).reshape(2, -1, tile, slow)
    short = short.transpose(1, 0, 2, 3).reshape(-1, 2 * tile, slow)
    fast = np.arange(width // 4)
    tile = min(256, width // 4)
    long = np.stack([np.stack(dft_table(4 * fast + kind, fast, width)) for kind in range(4)]).astype(BF16)
    long = long.reshape(4, 2, width // 4, -1, tile).transpose(3, 0, 1, 2, 4)
    order = np.concatenate([np.arange(kind, cols, 4) for kind in range(4)])
    bases = dft_table(bins, order, length)
    angle = (jnp.arange(slow, dtype=jnp.int32) * (member * cols) % length).astype(F32) * (2.0 * math.pi / length)
    turns = (jnp.cos(angle)[:, None], -jnp.sin(angle)[:, None])

    halves = [[g * groups + i for i in range(groups)] for g in range(segs)]
    trade = functools.partial(lax.all_to_all, axis_name="tm", split_axis=0, concat_axis=0, tiled=True)
    pieces = trade(pack(series, groups))

    def turn(half, *after):
        return first_pass(pieces, half[None], order, short, bases, turns, groups, after)

    def move(x, by):
        return lax.ppermute(x, "tm", [(i, (i + by) % devices) for i in range(devices)])

    far = turn(1 - seg)
    near = turn(seg, far)
    far = trade(far, axis_index_groups=halves)
    near = trade(gate(in_hbm(near), far, make=pltpu.HBM), axis_index_groups=halves)
    far, far_tail, far_head = fstat_pass(far, place, long, antenna, length, BF16)
    early = [move(far_tail, groups + 1), move(far_head, groups - 1)]
    far = gate(far, *early)
    other = move(far, groups)
    own, tail, head = fstat_pass(near, place, long, antenna, length, F32, (far,))
    late = [move(tail, 1), move(head, -1)]
    return detect(offsets, place, other, own, early, late)


def solution(mesh):
    return jax.shard_map(
        local,
        mesh=mesh,
        in_specs=(P("sky", None, "tm", None), P("sky", None), P("sky", None)),
        out_specs=P("sky", "tm", None),
        check_vma=False,
    )
```

```python
import functools
import math

import jax
import jax.numpy as jnp
import numpy as np
from jax import lax
from jax.experimental import pallas as pl
from jax.experimental.pallas import tpu as pltpu
from jax.sharding import PartitionSpec as P

DMAX = 8
LANES = 128
BF16 = jnp.bfloat16
F32 = jnp.float32
SEG, LOWEST, TOP, FIRST, LAST = range(5)
SMEM = pl.BlockSpec(memory_space=pltpu.SMEM)
VMEM = pl.BlockSpec(memory_space=pltpu.VMEM)
ANY = pl.BlockSpec(memory_space=pl.ANY)


def params(mebibytes):
    return pltpu.CompilerParams(vmem_limit_bytes=mebibytes * 1024 * 1024)


def cost(flops, moved):
    return pl.CostEstimate(flops=flops, bytes_accessed=moved, transcendentals=0)


def dft_table(rows, cols, length):
    products = rows[:, None].astype(np.int64) * cols[None, :] % length
    angle = products.astype(np.float32) * np.float32(2.0 * math.pi / length)
    return np.cos(angle), -np.sin(angle)


def in_hbm(x):
    return pltpu.with_memory_space_constraint(x, pltpu.HBM)


def dot(x, y):
    return jnp.dot(x, y, preferred_element_type=F32)


def pack_kernel(x_ref, out_ref):
    cols = out_ref.shape[-1]
    for piece in range(out_ref.shape[0]):
        out_ref[piece] = x_ref[0, :, :, piece * cols : (piece + 1) * cols]


def pack(series, groups):
    segs, comps, rows, width = series.shape
    shape = (segs * groups, comps, rows, width // groups)
    return pl.pallas_call(
        pack_kernel,
        grid=(segs,),
        in_specs=[pl.BlockSpec((1, comps, rows, width), lambda s: (s, 0, 0, 0))],
        out_specs=pl.BlockSpec((groups,) + shape[1:], lambda s: (s, 0, 0, 0)),
        out_shape=pltpu.HBM(shape, BF16),
        compiler_params=params(16),
        cost_estimate=cost(0, 4 * math.prod(shape)),
        name="pack",
    )(in_hbm(series))


def first_kernel(half_ref, x_ref, sort_ref, w_ref, br_ref, bi_ref, vr_ref, vi_ref, *refs):
    out_ref, sorted_ref = refs[-2:]
    tile, length = w_ref.shape[1] // 2, w_ref.shape[2]
    comps, cols = x_ref.shape[1], x_ref.shape[-1]
    spots = [slice(comp * cols, (comp + 1) * cols) for comp in range(comps)]

    @pl.when(pl.program_id(0) == 0)
    def _():
        for comp, spot in enumerate(spots):
            sorted_ref[:, spot] = dot(x_ref[:, comp].reshape(length, cols), sort_ref[...]).astype(BF16)

    shape = (out_ref.shape[0],) + out_ref.shape[2:]
    by_real, by_imag = vr_ref[...], vi_ref[...]
    t_real = br_ref[...] * by_real - bi_ref[...] * by_imag
    t_imag = br_ref[...] * by_imag + bi_ref[...] * by_real
    both = dot(w_ref[0], sorted_ref[...])
    with_real, with_imag = both[:tile], both[tile:]
    for lead in range(0, comps, 2):
        real_part = with_real[:, spots[lead]] - with_imag[:, spots[lead + 1]]
        imag_part = with_imag[:, spots[lead]] + with_real[:, spots[lead + 1]]
        out_ref[:, lead] = (real_part * t_real - imag_part * t_imag).astype(BF16).reshape(shape)
        out_ref[:, lead + 1] = (real_part * t_imag + imag_part * t_real).astype(BF16).reshape(shape)


def first_pass(pieces, half, order, table, bases, turns, groups, after):
    count, comps, rows, cols = pieces.shape
    length = count * rows
    per_half = groups * rows
    tile = table.shape[1] // 2
    steps = per_half // tile
    sort = np.zeros((cols, cols), np.float32)
    sort[order, np.arange(cols)] = 1.0
    strip = lambda width: pl.BlockSpec((tile, width), lambda t, half: (half[0] * steps + t, 0))
    return pl.pallas_call(
        first_kernel,
        grid_spec=pltpu.PrefetchScalarGridSpec(
            num_scalar_prefetch=1,
            grid=(steps,),
            in_specs=[VMEM, pl.BlockSpec((cols, cols), lambda t, half: (0, 0))]
            + [pl.BlockSpec((1,) + table.shape[1:], lambda t, half: (half[0] * steps + t, 0, 0))]
            + [strip(cols)] * 2
            + [strip(1)] * 2
            + [ANY] * len(after),
            out_specs=pl.BlockSpec((tile // rows, comps, rows, cols), lambda t, half: (t, 0, 0, 0)),
            scratch_shapes=[pltpu.VMEM((length, comps * cols), BF16)],
        ),
        out_shape=pltpu.HBM((groups, comps, rows, cols), BF16),
        compiler_params=params(24),
        cost_estimate=cost(4 * comps * per_half * length * cols, 4 * per_half * length),
        name="first_pass",
    )(half, pieces, in_hbm(sort.astype(BF16)), in_hbm(table), *map(in_hbm, bases), *turns, *after)


def fstat_kernel(length, place_ref, coef_ref, z_ref, w_ref, *refs):
    fstat_ref, tail_ref, head_ref, lhs_ref = refs[-4:]
    step = pl.program_id(0)

    @pl.when(step == 0)
    def _():
        groups, cols = z_ref.shape[0], z_ref.shape[-1] // 4
        for source in range(groups):
            piece = z_ref[source].reshape(lhs_ref.shape[1], 4 * cols)
            for kind in range(4):
                at = slice(source * cols, (source + 1) * cols)
                lhs_ref[kind, :, at] = piece[:, kind * cols : (kind + 1) * cols]

    rows, width = fstat_ref.shape
    tile = w_ref.shape[-1]
    sums = []
    for kind in range(4):
        by_real, by_imag = dot(lhs_ref[kind], w_ref[0, kind, 0]), dot(lhs_ref[kind], w_ref[0, kind, 1])
        part = lambda x, comp: x[comp * rows : (comp + 1) * rows]
        pairs = [(part(by_real, c) - part(by_imag, c + 1), part(by_imag, c) + part(by_real, c + 1)) for c in (0, 2)]
        sums.append(pairs[0] + pairs[1])
    plus = [[x + y for x, y in zip(sums[k], sums[k + 2])] for k in range(2)]
    minus = [[x - y for x, y in zip(sums[k], sums[k + 2])] for k in range(2)]
    turned = [minus[1][1], -minus[1][0], minus[1][3], -minus[1][2]]
    coef_a, coef_b, coef_c = [jnp.full((1, tile), coef_ref[place_ref[SEG], at], F32) for at in range(3)]
    scale = 1.0 / ((coef_a * coef_b - coef_c * coef_c) * length)
    coef_a, coef_b, coef_c = coef_a * scale, coef_b * scale, 2.0 * coef_c * scale
    quarter = width // 4
    for odd, (base, swing) in enumerate(((plus[0], plus[1]), (minus[0], turned))):
        tails, heads = [], []
        for half in range(2):
            a_real, a_imag, b_real, b_imag = [x - y if half else x + y for x, y in zip(base, swing)]
            fstat = (
                coef_b * (a_real * a_real + a_imag * a_imag)
                + coef_a * (b_real * b_real + b_imag * b_imag)
                - coef_c * (a_real * b_real + a_imag * b_imag)
            )
            tails.append(fstat[rows - DMAX :])
            heads.append(fstat[:DMAX])
            at = pl.ds(pl.multiple_of((2 * half + odd) * quarter + step * tile, tile), tile)
            fstat_ref[:, at] = fstat.astype(fstat_ref.dtype)
        at = pl.ds(pl.multiple_of(odd * quarter + step * tile, tile), tile)
        tail_ref[:, at] = jnp.concatenate(tails, axis=0).astype(tail_ref.dtype)
        head_ref[:, at] = jnp.concatenate(heads, axis=0).astype(head_ref.dtype)


def fstat_pass(z, place, table, antenna, length, kind, after=()):
    groups, comps, rows, cols = z.shape
    width = groups * cols
    rim = (2 * DMAX, width // 2)
    still = lambda shape: pl.BlockSpec(shape, lambda t: (0, 0))
    return pl.pallas_call(
        functools.partial(fstat_kernel, length),
        grid=(table.shape[0],),
        in_specs=[SMEM, SMEM, VMEM, pl.BlockSpec((1,) + table.shape[1:], lambda t: (t, 0, 0, 0, 0))] + [ANY] * len(after),
        out_specs=[still((rows, width)), still(rim), still(rim)],
        out_shape=[jax.ShapeDtypeStruct((rows, width), kind)] + [jax.ShapeDtypeStruct(rim, kind)] * 2,
        scratch_shapes=[pltpu.VMEM((4, comps * rows, width // 4), BF16)],
        compiler_params=params(24),
        cost_estimate=cost(comps * rows * width * width, width * width),
        name="fstat_pass",
    )(place, antenna, z, in_hbm(table), *after)


def gate(x, *after, make=jax.ShapeDtypeStruct):
    return pl.pallas_call(
        lambda *refs: None,
        in_specs=[ANY] * (1 + len(after)),
        out_specs=ANY,
        out_shape=make(x.shape, x.dtype),
        input_output_aliases={0: 0},
        compiler_params=params(2),
        cost_estimate=cost(0, 0),
        name="gate",
    )(x, *after)


def detect_kernel(offsets_ref, place_ref, other_ref, own_ref, *refs):
    early_refs, late_refs, out_ref, wide_refs = refs[:2], refs[2:4], refs[4], refs[5:]
    rows = own_ref.shape[0]

    @pl.when(pl.program_id(0) == 0)
    def _():
        is_first, is_last, seg = place_ref[FIRST] == 1, place_ref[LAST] == 1, place_ref[SEG]
        lowest, top = place_ref[LOWEST] == 1, place_ref[TOP] == 1
        width = own_ref.shape[1]
        unfold = lambda ref: jnp.concatenate([ref[...].astype(F32)[:DMAX], ref[...].astype(F32)[DMAX:]], axis=1)
        early, late = [unfold(ref) for ref in early_refs], [unfold(ref) for ref in late_refs]

        def widen(wide_ref, middle, lower, upper):
            lower = jnp.where(is_first, pltpu.roll(lower, 1, 1), lower)
            upper = jnp.where(is_last, pltpu.roll(upper, width - 1, 1), upper)
            for strip in range(width // LANES):
                at = slice(strip * LANES, (strip + 1) * LANES)
                wide_ref[strip, :DMAX] = lower[:, at]
                wide_ref[strip, DMAX : DMAX + rows] = middle[:, at]
                wide_ref[strip, DMAX + rows :] = upper[:, at]

        def place(own_wide, other_wide):
            lower = jnp.where(lowest, early[0], late[0]), jnp.where(lowest, late[0], early[0])
            upper = jnp.where(top, early[1], late[1]), jnp.where(top, late[1], early[1])
            widen(own_wide, own_ref[...], lower[0], upper[0])
            widen(other_wide, other_ref[...].astype(F32), lower[1], upper[1])

        @pl.when(seg == 0)
        def _():
            place(wide_refs[0], wide_refs[1])

        @pl.when(seg != 0)
        def _():
            place(wide_refs[1], wide_refs[0])

    for at in range(out_ref.shape[0]):
        template = pl.program_id(0) * out_ref.shape[0] + at
        begins = [DMAX + offsets_ref[template, s] for s in range(len(wide_refs))]
        for strip in range(own_ref.shape[1] // LANES):
            total = wide_refs[0][strip, pl.ds(begins[0], rows), :]
            for begin, wide_ref in zip(begins[1:], wide_refs[1:]):
                total = total + wide_ref[strip, pl.ds(begin, rows), :]
            out_ref[at, :, strip * LANES : (strip + 1) * LANES] = total * (1.0 / len(wide_refs))


def detect(offsets, place, other, own, early, late):
    templates = offsets.shape[0]
    rows, width = own.shape
    batch = 2 - templates % 2
    return pl.pallas_call(
        detect_kernel,
        grid=(templates // batch,),
        in_specs=[SMEM, SMEM] + [VMEM] * 6,
        out_specs=pl.BlockSpec((batch, rows, width), lambda t: (t, 0, 0)),
        out_shape=jax.ShapeDtypeStruct((templates, rows, width), F32),
        scratch_shapes=[pltpu.VMEM((width // LANES, rows + 2 * DMAX, LANES), F32)] * 2,
        compiler_params=params(8),
        cost_estimate=cost(3 * templates * rows * width, 4 * templates * rows * width),
        name="detect",
    )(offsets, place, other, own, *early, *late)


def local(series, antenna, offsets):
    devices = lax.axis_size("tm")
    index = lax.axis_index("tm")
    segs, _, rows, width = series.shape
    slow = devices * rows
    length = slow * width
    groups = devices // segs
    cols = width // groups
    seg, member = index // groups, index % groups
    place = jnp.stack([seg, member == 0, member == groups - 1, index == 0, index == devices - 1]).astype(jnp.int32)

    bins = np.arange(slow)
    tile = min(128, groups * rows)
    short = np.stack(dft_table(bins, bins, slow)).astype(BF16).reshape(2, -1, tile, slow)
    short = short.transpose(1, 0, 2, 3).reshape(-1, 2 * tile, slow)
    fast = np.arange(width // 4)
    tile = min(256, width // 4)
    long = np.stack([np.stack(dft_table(4 * fast + kind, fast, width)) for kind in range(4)]).astype(BF16)
    long = long.reshape(4, 2, width // 4, -1, tile).transpose(3, 0, 1, 2, 4)
    order = np.concatenate([np.arange(kind, cols, 4) for kind in range(4)])
    bases = dft_table(bins, order, length)
    angle = (jnp.arange(slow, dtype=jnp.int32) * (member * cols) % length).astype(F32) * (2.0 * math.pi / length)
    turns = (jnp.cos(angle)[:, None], -jnp.sin(angle)[:, None])

    halves = [[g * groups + i for i in range(groups)] for g in range(segs)]
    trade = functools.partial(lax.all_to_all, axis_name="tm", split_axis=0, concat_axis=0, tiled=True)
    pieces = trade(pack(series, groups))

    def turn(half, *after):
        return first_pass(pieces, half[None], order, short, bases, turns, groups, after)

    def move(x, by):
        return lax.ppermute(x, "tm", [(i, (i + by) % devices) for i in range(devices)])

    far = turn(1 - seg)
    near = turn(seg, far)
    far = trade(far, axis_index_groups=halves)
    near = trade(gate(in_hbm(near), far, make=pltpu.HBM), axis_index_groups=halves)
    far, far_tail, far_head = fstat_pass(far, place, long, antenna, length, BF16)
    early = [move(far_tail, groups + 1), move(far_head, groups - 1)]
    far = gate(far, *early)
    other = move(far, groups)
    own, tail, head = fstat_pass(near, place, long, antenna, length, F32, (far,))
    late = [move(tail, 1), move(head, -1)]
    return detect(offsets, place, other, own, early, late)


def solution(mesh):
    return jax.shard_map(
        local,
        mesh=mesh,
        in_specs=(P("sky", None, "tm", None), P("sky", None), P("sky", None)),
        out_specs=P("sky", "tm", None),
        check_vma=False,
    )
```
